32 devices in a mesh: dp: 8 (over y, x, core), feat: 4 (over z).
Axes of the slice: x: 2, y: 2, z: 4, core: 2. Of those that a mesh axis runs over, the one named last changes fastest.
Arguments:
- tokens: bfloat16 [8192, 1024], P('dp'), may hold values from -6 to 6
- cotangent: bfloat16 [8192, 1024], P('dp'), may hold values from -6 to 6
- doc_starts: int32 [8, 8], P('dp'), may hold values from 0 to 1023, as said below
- queries_keys: float32 [1024, 512], P(None, 'feat'), may hold values from -0.1875 to 0.1875
- value_weight: float32 [1024, 1024], P(None, 'feat'), may hold values from -0.1875 to 0.1875
- out_weight: float32 [1024, 1024], P('feat'), may hold values from -1 to 1
- gate_up: float32 [2, 1024, 2752], P(None, None, 'feat'), may hold values from -0.1875 to 0.1875
- down_weight: float32 [2752, 1024], P('feat'), may hold values from -0.109375 to 0.109375
- norm_gains: float32 [2, 1024], replicated, may hold values from 0.5 to 1.5
- queries_moment: float32 [1024, 512], P(None, 'feat'), may hold values from -224 to 224
- value_moment: float32 [1024, 1024], P(None, 'feat'), may hold values from -224 to 224
- out_moment: float32 [1024, 1024], P('feat'), may hold values from -224 to 224
- gate_moment: float32 [2, 1024, 2752], P(None, None, 'feat'), may hold values from -224 to 224
- down_moment: float32 [2752, 1024], P('feat'), may hold values from -224 to 224
- gains_moment: float32 [2, 1024], replicated, may hold values from -512 to 512
- queries_average: float32 [1024, 512], P(None, 'feat'), may hold values from -0.1875 to 0.1875
- value_average: float32 [1024, 1024], P(None, 'feat'), may hold values from -0.1875 to 0.1875
- out_average: float32 [1024, 1024], P('feat'), may hold values from -1 to 1
- gate_average: float32 [2, 1024, 2752], P(None, None, 'feat'), may hold values from -0.1875 to 0.1875
- down_average: float32 [2752, 1024], P('feat'), may hold values from -0.109375 to 0.109375
- gains_average: float32 [2, 1024], replicated, may hold values from 0.5 to 1.5
Outputs:
- mixed: bfloat16 [8192, 1024], P('dp')
- input_gradient: float32 [8192, 1024], P('dp')
- queries_momentum: float32 [1024, 512], P(None, 'feat')
- queries_new: float32 [1024, 512], P(None, 'feat')
- queries_mean: float32 [1024, 512], P(None, 'feat')
- value_momentum: float32 [1024, 1024], P(None, 'feat')
- value_new: float32 [1024, 1024], P(None, 'feat')
- value_mean: float32 [1024, 1024], P(None, 'feat')
- out_momentum: float32 [1024, 1024], P('feat')
- out_new: float32 [1024, 1024], P('feat')
- out_mean: float32 [1024, 1024], P('feat')
- gate_momentum: float32 [2, 1024, 2752], P(None, None, 'feat')
- gate_new: float32 [2, 1024, 2752], P(None, None, 'feat')
- gate_mean: float32 [2, 1024, 2752], P(None, None, 'feat')
- down_momentum: float32 [2752, 1024], P('feat')
- down_new: float32 [2752, 1024], P('feat')
- down_mean: float32 [2752, 1024], P('feat')
- gains_momentum: float32 [2, 1024], replicated
- gains_new: float32 [2, 1024], replicated
- gains_mean: float32 [2, 1024], replicated
The draws below stay inside these ranges and needn't reach their ends.
Inputs may be any that keep to these rules, and one draw needn't show every extreme that they name: `doc_starts`: each row's first start is 0, its last is 1023, and its 8 starts strictly increase.
All inputs are finite; a program needn't handle non-finite values.
Results may differ from the reference program's by a relative error of at most 0.015.
Values may be sent and summed in bfloat16 or wider, within the bound.
A program may use at most 256 MiB of HBM per device.

```python
from functools import partial
import jax
import jax.numpy as jnp
from jax import lax

D = 1024
HEADS = 16
QK = 16
HV = 64
FF = 2752
SEQ = 1024
NDOC = 8
STEP = 4
ROWS = 8
TOKENS = 8192
FEATS = 276
N_FEAT = 4


def draw_doc_starts(key, part):
    key = jax.random.fold_in(key, 11)

    def one_row(row_key):
        order = jax.random.permutation(row_key, SEQ - 2).astype(jnp.int32) + 1
        picks = jnp.sort(order[:NDOC - 2])
        first = jnp.zeros((1,), jnp.int32)
        last = jnp.full((1,), SEQ - 1, jnp.int32)
        return jnp.concatenate([first, picks, last])
    return jax.vmap(one_row)(jax.random.split(key, ROWS))


def block_scale(stream_key, extent, shards, least, top_value):
    gain = 1.0
    for axis_at, blocks in shards:
        steps = jax.random.uniform(jax.random.fold_in(jax.random.fold_in(stream_key, 6), axis_at), (blocks,), jnp.float32, least / len(shards), top_value / len(shards))
        gain = gain * jnp.repeat(jnp.exp(steps), extent[axis_at] // blocks).reshape((-1,) + (1,) * (len(extent) - 1 - axis_at))
    return gain


def noise(own_key, shape, scale, reach, cuts=(), kind=jnp.bfloat16):
    array = scale * jax.random.normal(own_key, shape, jnp.float32)
    if cuts:
        array = array * block_scale(own_key, shape, cuts, -0.22, 0.18)
    return jnp.clip(array, -reach, reach).astype(kind)


def setup_inputs(seed: int = 0) -> dict:
    keys = jax.random.split(jax.random.key(seed), 22)
    tokens = noise(keys[0], (TOKENS, D), 1.0, 6.0, ((0, 8),))
    cotangent = noise(keys[1], (TOKENS, D), 1.0, 6.0, ((0, 8),))
    doc_starts = draw_doc_starts(jax.random.fold_in(keys[21], 71), 0)
    queries_keys = noise(keys[3], (D, 2 * HEADS * QK), D ** -0.5, 0.1875, ((1, 4),), jnp.float32)
    value_weight = noise(keys[4], (D, HEADS * HV), D ** -0.5, 0.1875, ((1, 4),), jnp.float32)
    out_weight = noise(keys[5], (HEADS * HV, D), (D // 32) ** -0.5, 1.0, ((0, 4),), jnp.float32)
    gate_up = noise(keys[6], (2, D, FF), D ** -0.5, 0.1875, ((2, 4),), jnp.float32)
    down_weight = noise(keys[7], (FF, D), FF ** -0.5, 0.109375, ((0, 4),), jnp.float32)
    norm_gains = jnp.clip(1.0 + 0.1 * jax.random.normal(keys[8], (2, D), jnp.float32), 0.5, 1.5)
    queries_moment = noise(keys[9], (D, 2 * HEADS * QK), (0.4 * TOKENS ** 0.5), 224.0, ((1, 4),), jnp.float32)
    value_moment = noise(keys[10], (D, HEADS * HV), (0.4 * TOKENS ** 0.5), 224.0, ((1, 4),), jnp.float32)
    out_moment = noise(keys[11], (HEADS * HV, D), (0.4 * TOKENS ** 0.5), 224.0, ((0, 4),), jnp.float32)
    gate_moment = noise(keys[12], (2, D, FF), (0.4 * TOKENS ** 0.5), 224.0, ((2, 4),), jnp.float32)
    down_moment = noise(keys[13], (FF, D), (0.4 * TOKENS ** 0.5), 224.0, ((0, 4),), jnp.float32)
    gains_moment = noise(keys[14], (2, D), (TOKENS ** 0.5), 512.0, (), jnp.float32)
    queries_average = noise(keys[15], (D, 2 * HEADS * QK), D ** -0.5, 0.1875, ((1, 4),), jnp.float32)
    value_average = noise(keys[16], (D, HEADS * HV), D ** -0.5, 0.1875, ((1, 4),), jnp.float32)
    out_average = noise(keys[17], (HEADS * HV, D), (D // 32) ** -0.5, 1.0, ((0, 4),), jnp.float32)
    gate_average = noise(keys[18], (2, D, FF), D ** -0.5, 0.1875, ((2, 4),), jnp.float32)
    down_average = noise(keys[19], (FF, D), FF ** -0.5, 0.109375, ((0, 4),), jnp.float32)
    gains_average = jnp.clip(1.0 + 0.1 * jax.random.normal(keys[20], (2, D), jnp.float32), 0.5, 1.5)
    return dict(tokens=tokens, cotangent=cotangent, doc_starts=doc_starts, queries_keys=queries_keys, value_weight=value_weight, out_weight=out_weight, gate_up=gate_up, down_weight=down_weight, norm_gains=norm_gains, queries_moment=queries_moment, value_moment=value_moment, out_moment=out_moment, gate_moment=gate_moment, down_moment=down_moment, gains_moment=gains_moment, queries_average=queries_average, value_average=value_average, out_average=out_average, gate_average=gate_average, down_average=down_average, gains_average=gains_average)


EPS = 1e-06
MOMENTUM = 0.9
HIGH = lax.Precision.HIGHEST

@jax.custom_vjp
def low(v):
    return lax.optimization_barrier(v.astype(jnp.bfloat16)).astype(jnp.float32)

@jax.custom_vjp
def low_back(v):
    return v

def low_keep(v):
    return (low(v), None)

def low_pass(kept, grad):
    return (grad,)

def back_keep(v):
    return (v, None)

def back_low(kept, grad):
    return (low(grad),)
low.defvjp(low_keep, low_pass)
low_back.defvjp(back_keep, back_low)

def product(left, right):
    return jnp.dot(left, right, precision=HIGH, preferred_element_type=jnp.float32)

def feature_map(pairs, features):
    lead = pairs.shape[:-1]
    outer = (pairs[..., :, None] * pairs[..., None, :]).reshape(lead + (QK * QK,)) * 0.5 ** 0.5
    ones = jnp.ones(lead + (1,), jnp.float32)
    zeros = jnp.zeros(lead + (features - 1 - QK - QK * QK,), jnp.float32)
    return jnp.concatenate([ones.astype(pairs.dtype), pairs, outer, zeros.astype(pairs.dtype)], axis=-1)

def doc_mask(starts_row, count):
    position = jnp.arange(count, dtype=jnp.int32)
    document = lax.optimization_barrier(jnp.sum((starts_row[None, :] <= position[:, None]).astype(jnp.int32), axis=1))
    same = document[:, None] == document[None, :]
    causal = position[None, :] <= position[:, None]
    return jnp.logical_and(same, causal)

def sequence_mix(parts):
    query_feats, key_feats, values, starts_row = parts
    keep = doc_mask(starts_row, query_feats.shape[0]).astype(query_feats.dtype)
    group_size = FEATS // N_FEAT
    numer = jnp.zeros(values.shape, values.dtype)
    denom = jnp.zeros(values.shape[:2], values.dtype)
    for group in range(N_FEAT):
        lower = group * group_size
        scores = jnp.einsum('thf,shf->hts', query_feats[:, :, lower:lower + group_size], key_feats[:, :, lower:lower + group_size], precision=HIGH) * keep[None]
        scores = low_back(scores)
        numer = numer + jnp.einsum('hts,shc->thc', low(scores), values, precision=HIGH)
        denom = denom + lax.optimization_barrier(jnp.sum(scores, axis=2)).T
    numer = low_back(numer)
    denom = low_back(denom)
    return numer / denom[:, :, None]

def block(inputs, queries_keys, value_weight, out_weight, gate_up, down_weight, norm_gains, doc_starts):
    scale_one = lax.rsqrt(lax.optimization_barrier(jnp.mean(inputs * inputs, axis=1, keepdims=True)) + EPS)
    normed_one = low(inputs * scale_one * norm_gains[0])
    pairs = low(low_back(product(normed_one, low(queries_keys))))
    values = low(low_back(product(normed_one, low(value_weight))))
    half = HEADS * QK
    query_feats = low(feature_map(pairs[:, :half].reshape(TOKENS, HEADS, QK) * 0.5, FEATS))
    key_feats = low(feature_map(pairs[:, half:].reshape(TOKENS, HEADS, QK) * 0.5, FEATS))
    shaped = (query_feats.reshape(ROWS, SEQ, HEADS, FEATS), key_feats.reshape(ROWS, SEQ, HEADS, FEATS), values.reshape(ROWS, SEQ, HEADS, HV), doc_starts)
    attn_in = lax.map(jax.checkpoint(sequence_mix), shaped).reshape(TOKENS, HEADS * HV)
    attended = low_back(product(low(attn_in), low(out_weight)))
    hidden_one = inputs + attended
    scale_two = lax.rsqrt(lax.optimization_barrier(jnp.mean(hidden_one * hidden_one, axis=1, keepdims=True)) + EPS)
    normed_two = low(hidden_one * scale_two * norm_gains[1])
    gate = low_back(product(normed_two, low(gate_up[0])))
    upper = low_back(product(normed_two, low(gate_up[1])))
    hidden_units = low(jax.nn.silu(gate) * upper)
    return hidden_one + low_back(product(hidden_units, low(down_weight)))

def update(weight, grad_total, moment, average, rate):
    moment_next = MOMENTUM * moment + grad_total
    weight_next = weight - rate * (grad_total + MOMENTUM * moment_next)
    average_next = average + (weight_next - average) / STEP
    return (moment_next, weight_next, average_next)

def reference(tokens, cotangent, doc_starts, queries_keys, value_weight, out_weight, gate_up, down_weight, norm_gains, queries_moment, value_moment, out_moment, gate_moment, down_moment, gains_moment, queries_average, value_average, out_average, gate_average, down_average, gains_average):
    inputs = tokens.astype(jnp.float32)
    forward = partial(block, doc_starts=doc_starts)
    result, pullback = jax.vjp(forward, inputs, queries_keys, value_weight, out_weight, gate_up, down_weight, norm_gains)
    grads = pullback(cotangent.astype(jnp.float32))
    total = float(TOKENS)
    first = update(queries_keys, grads[1], queries_moment, queries_average, (D * total) ** (-0.5))
    second = update(value_weight, grads[2], value_moment, value_average, (D * total) ** (-0.5))
    third = update(out_weight, grads[3], out_moment, out_average, (HEADS * HV * total) ** (-0.5))
    fourth = update(gate_up, grads[4], gate_moment, gate_average, (D * total) ** (-0.5))
    fifth = update(down_weight, grads[5], down_moment, down_average, (FF * total) ** (-0.5))
    sixth = update(norm_gains, grads[6], gains_moment, gains_average, 0.2 * total ** (-0.5))
    return (result.astype(jnp.bfloat16), grads[0], first[0], first[1], first[2], second[0], second[1], second[2], third[0], third[1], third[2], fourth[0], fourth[1], fourth[2], fifth[0], fifth[1], fifth[2], sixth[0], sixth[1], sixth[2])
```

```python
import functools
import jax
import jax.numpy as jnp
from jax import lax
from jax.experimental import pallas as pl
from jax.experimental.pallas import tpu as pltpu
from jax.sharding import PartitionSpec as P

D = 1024
HEADS = 16
QK = 16
HV = 64
FF = 2752
STEP = 4
BT = 256
F32 = jnp.float32
BF16 = jnp.bfloat16

EPS = 1e-06
MOMENTUM = 0.9


def nt(a, b):
    return lax.dot_general(a, b, (((1,), (1,)), ((), ())), preferred_element_type=F32)


def nn(a, b):
    return lax.dot_general(a, b, (((1,), (0,)), ((), ())), preferred_element_type=F32)


def first_start(starts_ref, t):
    begin = jnp.int32(0)
    for n in range(starts_ref.shape[1]):
        begin = jnp.where(starts_ref[0, n] <= t, jnp.maximum(begin, starts_ref[0, n]), begin)
    return begin


def fill_mask(starts_ref, mask_ref, block, low_block):
    t = block * BT + lax.broadcasted_iota(jnp.int32, (BT, 1), 0)
    begin = jnp.zeros((BT, 1), jnp.int32)
    for n in range(starts_ref.shape[1]):
        begin = jnp.where(starts_ref[0, n] <= t, jnp.maximum(begin, starts_ref[0, n]), begin)

    def one(j, carry):
        s = j * BT + lax.broadcasted_iota(jnp.int32, (BT, BT), 1)
        keep = jnp.logical_and(s <= t, s >= begin)
        mask_ref[j] = keep.astype(F32).astype(BF16)
        return carry
    lax.fori_loop(low_block, block + 1, one, 0)


def attn_fwd_kernel(hb, starts_ref, q_ref, k_ref, v_ref, o_ref, rd_ref, mask_ref):
    block = pl.program_id(0)
    low_block = first_start(starts_ref, block * BT) // BT
    fill_mask(starts_ref, mask_ref, block, low_block)
    lane = lax.broadcasted_iota(jnp.int32, (1, 128), 1)

    def group(g, carry):
        qlanes = pl.ds(pl.multiple_of((g * hb) // 8 * 128, 128), 128)
        q = q_ref[:, qlanes]
        qms = []
        for n in range(hb):
            h8 = lax.rem(g * hb + n, 8)
            qms.append(jnp.where(lane // QK == h8, q, jnp.zeros_like(q)))

        def step(j, accs):
            rows = pl.ds(pl.multiple_of(j * BT, BT), BT)
            k = k_ref[rows, qlanes]
            mask = mask_ref[j]
            out = []
            for n in range(hb):
                vl = pl.ds(pl.multiple_of((g * hb + n) // 2 * 128, 128), 128)
                v = v_ref[rows, vl]
                v = jnp.where(lane // HV == n % 2, v, jnp.ones_like(v))
                t1 = nt(qms[n], k) + 1.0
                p = (t1 * t1 + 1.0).astype(BF16) * mask
                out.append(accs[n] + nn(p, v))
            return tuple(out)
        accs = lax.fori_loop(low_block, block + 1, step, tuple(jnp.zeros((BT, 128), F32) for _ in range(hb)))
        for m in range(hb // 2):
            vl = pl.ds(pl.multiple_of((g * hb + 2 * m) // 2 * 128, 128), 128)
            first, second = accs[2 * m], accs[2 * m + 1]
            numer = jnp.where(lane < HV, first, second)
            denom = pltpu.roll(jnp.where(lane < HV, second, first), HV, 1)
            recip = 1.0 / denom
            o_ref[:, vl] = (numer * recip).astype(BF16)
            rd_ref[:, vl] = recip
        return carry
    lax.fori_loop(0, HEADS // hb, group, 0)


def attn_fwd(starts, q, k, v, hb=4):
    length = q.shape[0]
    return pl.pallas_call(
        functools.partial(attn_fwd_kernel, hb),
        grid=(length // BT,),
        out_shape=(jax.ShapeDtypeStruct((length, HEADS * HV), BF16), jax.ShapeDtypeStruct((length, HEADS * HV), F32)),
        in_specs=[pl.BlockSpec(memory_space=pltpu.SMEM), pl.BlockSpec((BT, HEADS * QK), lambda i: (i, 0)),
                  pl.BlockSpec((length, HEADS * QK), lambda i: (0, 0)), pl.BlockSpec((length, HEADS * HV), lambda i: (0, 0))],
        out_specs=(pl.BlockSpec((BT, HEADS * HV), lambda i: (i, 0)), pl.BlockSpec((BT, HEADS * HV), lambda i: (i, 0))),
        scratch_shapes=[pltpu.VMEM((length // BT, BT, BT), BF16)],
        compiler_params=pltpu.CompilerParams(vmem_limit_bytes=40 * 2**20),
    )(starts, q, k, v)


def attn_bwd_kernel(
    hb, starts_ref, q_ref, k_ref, v_ref, attn_ref, rd_ref, ga_ref, out_w_ref,
    gq_ref, gk_ref, gv_ref, mask_ref, gn_ref, gd_ref, qt_ref, gnt_ref, gkt_ref, gvt_ref,
):
    block = pl.program_id(0)

    @pl.when(block == 0)
    def _():
        gkt_ref[...] = jnp.zeros_like(gkt_ref)
        gvt_ref[...] = jnp.zeros_like(gvt_ref)

    low_block = first_start(starts_ref, block * BT) // BT
    fill_mask(starts_ref, mask_ref, block, low_block)
    lane = lax.broadcasted_iota(jnp.int32, (1, 128), 1)
    qt_ref[...] = q_ref[...].T

    def prepare(m, carry):
        vl = pl.ds(pl.multiple_of(m * 128, 128), 128)
        grad_attn = nt(ga_ref[...], out_w_ref[vl, :])
        grad_numer = grad_attn * (2.0 * rd_ref[:, vl])
        both = grad_numer * attn_ref[:, vl].astype(F32)
        first = jnp.sum(jnp.where(lane < HV, both, 0.0), axis=1, keepdims=True)
        second = jnp.sum(jnp.where(lane < HV, 0.0, both), axis=1, keepdims=True)
        gd_ref[:, vl] = jnp.where(lane < HV, -second, -first).astype(BF16)
        low = grad_numer.astype(BF16)
        gn_ref[:, vl] = low
        gnt_ref[vl, :] = low.T
        return carry

    lax.fori_loop(0, HEADS // 2, prepare, 0)

    def group(g, carry):
        first = g * hb
        qlanes = pl.ds(pl.multiple_of(first // 8 * 128, 128), 128)
        q = q_ref[:, qlanes]
        qms, gns = [], []
        for n in range(hb):
            h8 = lax.rem(first + n, 8)
            qms.append(jnp.where(lane // QK == h8, q, jnp.zeros_like(q)))
            vl = pl.ds(pl.multiple_of((first + n) // 2 * 128, 128), 128)
            gn = gn_ref[:, vl]
            gn = jnp.where(lane // HV == n % 2, gn, jnp.zeros_like(gn))
            gns.append(jnp.where(lane == HV * (1 - n % 2), gd_ref[:, vl], gn))

        def step(j, gq):
            rows = pl.ds(pl.multiple_of(j * BT, BT), BT)
            k = k_ref[rows, qlanes]
            mask = mask_ref[j]
            for n in range(hb):
                h = first + n
                vl = pl.ds(pl.multiple_of(h // 2 * 128, 128), 128)
                v = v_ref[rows, vl]
                v = jnp.where(lane // HV == n % 2, v, jnp.ones_like(v))
                t1 = nt(qms[n], k) + 1.0
                p = (t1 * t1 + 1.0).astype(BF16) * mask
                dp = nt(gns[n], v).astype(BF16) * mask
                gs = (dp.astype(F32) * t1).astype(BF16)
                h8 = lax.rem(h, 8)
                km = jnp.where(lane // QK == h8, k, jnp.zeros_like(k))
                gq = gq + nn(gs, km)
                qrows = pl.ds(pl.multiple_of(h * QK, QK), QK)
                vrows = pl.ds(pl.multiple_of(h * HV, HV), HV)
                gkt_ref[qrows, rows] += nn(qt_ref[qrows, :], gs)
                gvt_ref[vrows, rows] += nn(gnt_ref[vrows, :], p)
            return gq

        gq = lax.fori_loop(low_block, block + 1, step, jnp.zeros((BT, 128), F32))
        gq_ref[:, qlanes] = (gq * 0.25).astype(BF16)
        return carry

    lax.fori_loop(0, HEADS // hb, group, 0)

    @pl.when(block == pl.num_programs(0) - 1)
    def _():
        gk_ref[...] = gkt_ref[...].T.astype(BF16)

        def turn(m, carry):
            vl = pl.ds(pl.multiple_of(m * 128, 128), 128)
            gv_ref[:, vl] = (gvt_ref[vl, :] * 0.5).T.astype(BF16)
            return carry

        lax.fori_loop(0, HEADS // 2, turn, 0)


def attn_bwd(starts, q, k, v, attn, rd, ga, out_w):
    hb = 8
    length = q.shape[0]
    nq, nv = HEADS * QK, HEADS * HV

    def whole(rows, cols):
        return pl.BlockSpec((rows, cols), lambda i: (0, 0))

    def rowblk(cols):
        return pl.BlockSpec((BT, cols), lambda i: (i, 0))

    return pl.pallas_call(
        functools.partial(attn_bwd_kernel, hb),
        grid=(length // BT,),
        out_shape=(
            jax.ShapeDtypeStruct((length, nq), BF16),
            jax.ShapeDtypeStruct((length, nq), BF16),
            jax.ShapeDtypeStruct((length, nv), BF16),
        ),
        in_specs=[
            pl.BlockSpec(memory_space=pltpu.SMEM),
            rowblk(nq), whole(length, nq), whole(length, nv), rowblk(nv), rowblk(nv), rowblk(nv), whole(nv, D),
        ],
        out_specs=(rowblk(nq), whole(length, nq), whole(length, nv)),
        scratch_shapes=[
            pltpu.VMEM((length // BT, BT, BT), BF16),
            pltpu.VMEM((BT, nv), BF16),
            pltpu.VMEM((BT, nv), BF16),
            pltpu.VMEM((nq, BT), BF16),
            pltpu.VMEM((nv, BT), BF16),
            pltpu.VMEM((nq, length), F32),
            pltpu.VMEM((nv, length), F32),
        ],
        compiler_params=pltpu.CompilerParams(vmem_limit_bytes=50 * 2**20),
        name="attn_bwd",
    )(starts, q, k, v, attn, rd, ga, out_w)


def update(weight, grad_total, moment, average, rate):
    moment_next = MOMENTUM * moment + grad_total
    weight_next = weight - rate * (grad_total + MOMENTUM * moment_next)
    average_next = average + (weight_next - average) / STEP
    return (moment_next, weight_next, average_next)


def on_device(
    tokens,
    cotangent,
    doc_starts,
    queries_keys,
    value_weight,
    out_weight,
    gate_up,
    down_weight,
    norm_gains,
    queries_moment,
    value_moment,
    out_moment,
    gate_moment,
    down_moment,
    gains_moment,
    queries_average,
    value_average,
    out_average,
    gate_average,
    down_average,
    gains_average,
):
    groups = lax.axis_size("feat")
    length = tokens.shape[0]
    total_tokens = float(length * lax.axis_size("dp"))
    half = HEADS * QK
    pair_cols = queries_keys.shape[1]
    value_cols = value_weight.shape[1]
    feat = lax.axis_index("feat")
    own_qkv = jnp.concatenate([queries_keys.astype(BF16), value_weight.astype(BF16)], axis=1)
    own_out = out_weight.astype(BF16)
    gate_low = gate_up.astype(BF16)
    down_low = down_weight.astype(BF16)
    all_qkv = lax.all_gather(own_qkv, "feat", axis=0)
    all_out = lax.all_gather(own_out, "feat", axis=0, tiled=True)
    pairs_full = all_qkv[:, :, :pair_cols].transpose(1, 0, 2).reshape(D, 2 * half)
    values_full = all_qkv[:, :, pair_cols:].transpose(1, 0, 2).reshape(D, HEADS * HV)
    inputs = tokens.astype(F32)
    scale_one = lax.rsqrt(jnp.mean(inputs * inputs, axis=1, keepdims=True) + EPS)
    unit_one = inputs * scale_one
    normed_one = (unit_one * norm_gains[0]).astype(BF16)
    pairs = jnp.dot(normed_one, pairs_full, preferred_element_type=F32).astype(BF16)
    values = jnp.dot(normed_one, values_full, preferred_element_type=F32).astype(BF16)
    queries = pairs[:, :half] * jnp.bfloat16(0.25)
    keys = pairs[:, half:]
    attn_low, recip = attn_fwd(doc_starts, queries, keys, values, 8)
    attended = jnp.dot(attn_low, all_out, preferred_element_type=F32)
    hidden_one = inputs + attended
    scale_two = lax.rsqrt(jnp.mean(hidden_one * hidden_one, axis=1, keepdims=True) + EPS)
    unit_two = hidden_one * scale_two
    normed_two = (unit_two * norm_gains[1]).astype(jnp.bfloat16)
    gate_value = jnp.dot(normed_two, gate_low[0], preferred_element_type=jnp.float32)
    up_value = jnp.dot(normed_two, gate_low[1], preferred_element_type=jnp.float32)
    activated = jax.nn.silu(gate_value)
    hidden_low = (activated * up_value).astype(jnp.bfloat16)
    ffn_out = lax.psum(
        jnp.dot(hidden_low, down_low, preferred_element_type=jnp.float32).astype(jnp.bfloat16),
        "feat",
    ).astype(jnp.float32)
    mixed = (hidden_one + ffn_out).astype(jnp.bfloat16)
    grad_down = jnp.einsum("tf,td->fd", hidden_low, cotangent, preferred_element_type=jnp.float32)
    grad_hidden_units = jnp.einsum(
        "td,fd->tf", cotangent, down_low, preferred_element_type=jnp.float32
    )
    sigmoid_gate = jax.nn.sigmoid(gate_value)
    slope = sigmoid_gate * (1.0 + gate_value * (1.0 - sigmoid_gate))
    grad_gate = (grad_hidden_units * up_value * slope).astype(jnp.bfloat16)
    grad_up = (grad_hidden_units * activated).astype(jnp.bfloat16)
    grad_gate_up = jnp.stack(
        [
            jnp.einsum("td,tf->df", normed_two, grad_gate, preferred_element_type=jnp.float32),
            jnp.einsum("td,tf->df", normed_two, grad_up, preferred_element_type=jnp.float32),
        ]
    )
    normed_two_part = jnp.einsum(
        "tf,df->td", grad_gate, gate_low[0], preferred_element_type=jnp.float32
    ) + jnp.einsum("tf,df->td", grad_up, gate_low[1], preferred_element_type=jnp.float32)
    grad_normed_two = lax.psum(normed_two_part.astype(jnp.bfloat16), "feat").astype(jnp.float32)
    gain_two = jnp.sum(grad_normed_two * unit_two, axis=0)
    grad_unit_two = grad_normed_two * norm_gains[1]
    grad_hidden = cotangent.astype(jnp.float32) + scale_two * (
        grad_unit_two - unit_two * jnp.mean(grad_unit_two * unit_two, axis=1, keepdims=True)
    )
    grad_attended = grad_hidden.astype(jnp.bfloat16)
    own_attn = lax.dynamic_slice_in_dim(attn_low, feat * value_cols, value_cols, 1)
    grad_out = jnp.einsum("tv,td->vd", own_attn, grad_attended, preferred_element_type=F32)
    grad_queries, grad_keys, grad_values = attn_bwd(
        doc_starts, queries, keys, values, attn_low, recip, grad_attended, all_out
    )
    grad_pairs_all = jnp.concatenate([grad_queries, grad_keys], axis=1)
    own_pairs = lax.dynamic_slice_in_dim(grad_pairs_all, feat * pair_cols, pair_cols, 1)
    own_values = lax.dynamic_slice_in_dim(grad_values, feat * value_cols, value_cols, 1)
    grad_pairs = jnp.einsum("td,tq->dq", normed_one, own_pairs, preferred_element_type=F32)
    grad_value = jnp.einsum("td,tv->dv", normed_one, own_values, preferred_element_type=F32)
    grad_normed_one = jnp.einsum(
        "tq,dq->td", grad_pairs_all, pairs_full, preferred_element_type=F32
    ) + jnp.einsum("tv,dv->td", grad_values, values_full, preferred_element_type=F32)
    gain_one = jnp.sum(grad_normed_one * unit_one, axis=0)
    grad_unit_one = grad_normed_one * norm_gains[0]
    input_gradient = grad_hidden + scale_one * (
        grad_unit_one - unit_one * jnp.mean(grad_unit_one * unit_one, axis=1, keepdims=True)
    )
    gain_one, gain_two = lax.psum((gain_one, gain_two), "dp")
    grad_gate_up, grad_down = lax.psum((grad_gate_up.astype(BF16), grad_down.astype(BF16)), "dp")
    grad_pairs, grad_value, grad_out = lax.psum(
        (grad_pairs.astype(BF16), grad_value.astype(BF16), grad_out.astype(BF16)), "dp"
    )
    grad_gains = jnp.stack([gain_one, gain_two])
    first = update(
        queries_keys, grad_pairs, queries_moment, queries_average, (D * total_tokens) ** (-0.5)
    )
    second = update(
        value_weight, grad_value, value_moment, value_average, (D * total_tokens) ** (-0.5)
    )
    third = update(
        out_weight, grad_out, out_moment, out_average, (HEADS * HV * total_tokens) ** (-0.5)
    )
    fourth = update(gate_up, grad_gate_up, gate_moment, gate_average, (D * total_tokens) ** (-0.5))
    fifth = update(down_weight, grad_down, down_moment, down_average, (FF * total_tokens) ** (-0.5))
    sixth = update(
        norm_gains, grad_gains, gains_moment, gains_average, 0.2 * total_tokens ** (-0.5)
    )
    return (
        mixed,
        input_gradient,
        first[0],
        first[1],
        first[2],
        second[0],
        second[1],
        second[2],
        third[0],
        third[1],
        third[2],
        fourth[0],
        fourth[1],
        fourth[2],
        fifth[0],
        fifth[1],
        fifth[2],
        sixth[0],
        sixth[1],
        sixth[2],
    )


def solution(mesh):
    in_specs = (
        P("dp", None),
        P("dp", None),
        P("dp", None),
        P(None, "feat"),
        P(None, "feat"),
        P("feat", None),
        P(None, None, "feat"),
        P("feat", None),
        P(),
        P(None, "feat"),
        P(None, "feat"),
        P("feat", None),
        P(None, None, "feat"),
        P("feat", None),
        P(),
        P(None, "feat"),
        P(None, "feat"),
        P("feat", None),
        P(None, None, "feat"),
        P("feat", None),
        P(),
    )
    out_specs = (
        P("dp", None),
        P("dp", None),
        P(None, "feat"),
        P(None, "feat"),
        P(None, "feat"),
        P(None, "feat"),
        P(None, "feat"),
        P(None, "feat"),
        P("feat", None),
        P("feat", None),
        P("feat", None),
        P(None, None, "feat"),
        P(None, None, "feat"),
        P(None, None, "feat"),
        P("feat", None),
        P("feat", None),
        P("feat", None),
        P(),
        P(),
        P(),
    )
    return jax.shard_map(
        on_device, mesh=mesh, in_specs=in_specs, out_specs=out_specs, check_vma=False
    )
```

```python
import functools
import jax
import jax.numpy as jnp
from jax import lax
from jax.experimental import pallas as pl
from jax.experimental.pallas import tpu as pltpu
from jax.sharding import PartitionSpec as P

D = 1024
HEADS = 16
QK = 16
HV = 64
FF = 2752
STEP = 4
BT = 256
F32 = jnp.float32
BF16 = jnp.bfloat16

MESH = pl.DeviceIdType.MESH
EPS = 1e-06
MOMENTUM = 0.9


def nt(a, b):
    return lax.dot_general(a, b, (((1,), (1,)), ((), ())), preferred_element_type=F32)


def nn(a, b):
    return lax.dot_general(a, b, (((1,), (0,)), ((), ())), preferred_element_type=F32)


def first_start(starts_ref, t):
    begin = jnp.int32(0)
    for n in range(starts_ref.shape[1]):
        begin = jnp.where(starts_ref[0, n] <= t, jnp.maximum(begin, starts_ref[0, n]), begin)
    return begin


def fill_mask(starts_ref, mask_ref, block, low_block):
    t = block * BT + lax.broadcasted_iota(jnp.int32, (BT, 1), 0)
    begin = jnp.zeros((BT, 1), jnp.int32)
    for n in range(starts_ref.shape[1]):
        begin = jnp.where(starts_ref[0, n] <= t, jnp.maximum(begin, starts_ref[0, n]), begin)

    def one(j, carry):
        s = j * BT + lax.broadcasted_iota(jnp.int32, (BT, BT), 1)
        keep = jnp.logical_and(s <= t, s >= begin)
        mask_ref[j] = keep.astype(F32).astype(BF16)
        return carry
    lax.fori_loop(low_block, block + 1, one, 0)


def attn_fwd_kernel(hb, starts_ref, q_ref, k_ref, v_ref, o_ref, rd_ref, mask_ref):
    block = pl.program_id(0)
    low_block = first_start(starts_ref, block * BT) // BT
    fill_mask(starts_ref, mask_ref, block, low_block)
    lane = lax.broadcasted_iota(jnp.int32, (1, 128), 1)

    def group(g, carry):
        qlanes = pl.ds(pl.multiple_of((g * hb) // 8 * 128, 128), 128)
        q = q_ref[:, qlanes]
        qms = []
        for n in range(hb):
            h8 = lax.rem(g * hb + n, 8)
            qms.append(jnp.where(lane // QK == h8, q, jnp.zeros_like(q)))

        def step(j, accs):
            rows = pl.ds(pl.multiple_of(j * BT, BT), BT)
            k = k_ref[rows, qlanes]
            mask = mask_ref[j]
            out = []
            for n in range(hb):
                vl = pl.ds(pl.multiple_of((g * hb + n) // 2 * 128, 128), 128)
                v = v_ref[rows, vl]
                v = jnp.where(lane // HV == n % 2, v, jnp.ones_like(v))
                t1 = nt(qms[n], k) + 1.0
                p = (t1 * t1 + 1.0).astype(BF16) * mask
                out.append(accs[n] + nn(p, v))
            return tuple(out)
        accs = lax.fori_loop(low_block, block + 1, step, tuple(jnp.zeros((BT, 128), F32) for _ in range(hb)))
        for m in range(hb // 2):
            vl = pl.ds(pl.multiple_of((g * hb + 2 * m) // 2 * 128, 128), 128)
            first, second = accs[2 * m], accs[2 * m + 1]
            numer = jnp.where(lane < HV, first, second)
            denom = pltpu.roll(jnp.where(lane < HV, second, first), HV, 1)
            recip = 1.0 / denom
            o_ref[:, vl] = (numer * recip).astype(BF16)
            rd_ref[:, vl] = recip
        return carry
    lax.fori_loop(0, HEADS // hb, group, 0)


def attn_fwd(starts, q, k, v, hb=4):
    length = q.shape[0]
    return pl.pallas_call(
        functools.partial(attn_fwd_kernel, hb),
        grid=(length // BT,),
        out_shape=(jax.ShapeDtypeStruct((length, HEADS * HV), BF16), jax.ShapeDtypeStruct((length, HEADS * HV), F32)),
        in_specs=[pl.BlockSpec(memory_space=pltpu.SMEM), pl.BlockSpec((BT, HEADS * QK), lambda i: (i, 0)),
                  pl.BlockSpec((length, HEADS * QK), lambda i: (0, 0)), pl.BlockSpec((length, HEADS * HV), lambda i: (0, 0))],
        out_specs=(pl.BlockSpec((BT, HEADS * HV), lambda i: (i, 0)), pl.BlockSpec((BT, HEADS * HV), lambda i: (i, 0))),
        scratch_shapes=[pltpu.VMEM((length // BT, BT, BT), BF16)],
        compiler_params=pltpu.CompilerParams(vmem_limit_bytes=40 * 2**20),
    )(starts, q, k, v)


def gather_kernel(bits, own_ref, all_ref, send_sem, recv_sem, own_sem):
    dp = lax.axis_index("dp")
    f = lax.axis_index("feat")
    last = lax.axis_size("feat") - 1
    pieces = 2 ** len(bits)
    j = lax.rem(dp, pieces)
    base = dp - j

    def flip(k, bit):
        return k + bit - 2 * bit * lax.rem(k // bit, 2)

    barrier = pltpu.get_barrier_semaphore()
    for bit in bits:
        pl.semaphore_signal(barrier, inc=1, device_id=(base + flip(j, bit), f), device_id_type=MESH)

    @pl.when(f > 0)
    def _():
        pl.semaphore_signal(barrier, inc=1, device_id=(dp, f - 1), device_id_type=MESH)

    @pl.when(f < last)
    def _():
        pl.semaphore_signal(barrier, inc=1, device_id=(dp, f + 1), device_id_type=MESH)

    pl.semaphore_wait(barrier, len(bits) + jnp.where(f > 0, 1, 0) + jnp.where(f < last, 1, 0))

    def copy(z, colour, k, slot, device, own=False):
        source = own_ref.at[k, colour] if own else all_ref.at[z, k, colour]
        return pltpu.make_async_remote_copy(
            src_ref=source, dst_ref=all_ref.at[z, k, colour], send_sem=send_sem.at[z, colour, slot],
            recv_sem=recv_sem.at[z, colour, k], device_id=device, device_id_type=MESH)

    here = (dp, f)
    for colour in range(2):
        @pl.when(f > 0)
        def _():
            copy(f, colour, j, 0, (dp, f - 1), True).start()

        @pl.when(f < last)
        def _():
            copy(f, colour, j, 1, (dp, f + 1), True).start()
    mine = pltpu.make_async_copy(own_ref, all_ref.at[f], own_sem)
    mine.start()

    order = [
        jnp.where(f == 0, 1, f - 1),
        jnp.where(f < 2, 2, jnp.where(f == 2, 3, 1)),
        jnp.where(f < 2, 3, 0),
    ]
    colour_bits = [list(bits[1:]) + [bits[0]], list(bits[1:])[::-1] + [bits[0]]]

    def held(colour, step):
        out = [j]
        for bit in colour_bits[colour][:step]:
            out = out + [flip(k, bit) for k in out]
        return out

    def start_step(z, step):
        for colour in range(2):
            first = 2 + 2 ** step - 1
            partner = (base + flip(j, colour_bits[colour][step]), f)
            for n, k in enumerate(held(colour, step)):
                copy(z, colour, k, first + n, partner).start()

    def wait_step(z, step):
        for colour in range(2):
            for k in held(colour, step):
                copy(z, colour, flip(k, colour_bits[colour][step]), 0, here).wait_recv()

    def arrive(z):
        ahead = jnp.where(z < f, f + 1, f - 1)
        onward = jnp.logical_and(ahead >= 0, ahead <= last)
        for colour in range(2):
            copy(z, colour, j, 0, here).wait_recv()

            @pl.when(onward)
            def _():
                copy(z, colour, j, jnp.where(z < f, 1, 0), (dp, ahead)).start()
        start_step(z, 0)

    steps = len(bits)
    arrive(order[0])
    for z, step in [(1, None), (0, 0), (2, None), (1, 0), (0, 1), (2, 0), (1, 1), (0, 2), (2, 1), (1, 2), (2, 2)]:
        if step is None:
            arrive(order[z])
        else:
            wait_step(order[z], step)
            if step + 1 < steps:
                start_step(order[z], step + 1)
    for z in order:
        ahead = jnp.where(z < f, f + 1, f - 1)
        onward = jnp.logical_and(ahead >= 0, ahead <= last)
        for colour in range(2):
            @pl.when(onward)
            def _():
                copy(z, colour, j, jnp.where(z < f, 1, 0), here).wait_send()
            for step in range(steps):
                for n, k in enumerate(held(colour, step)):
                    copy(z, colour, k, 2 + 2 ** step - 1 + n, here).wait_send()
    for colour in range(2):
        @pl.when(f > 0)
        def _():
            copy(f, colour, j, 0, here, True).wait_send()

        @pl.when(f < last)
        def _():
            copy(f, colour, j, 1, here, True).wait_send()
    mine.wait()


def gather_all(own, cid):
    rows, cols = own.shape
    bits = (1, 2, 4)
    shape = (8, 2, rows // 16, cols)
    out = pl.pallas_call(
        functools.partial(gather_kernel, bits),
        out_shape=jax.ShapeDtypeStruct((4,) + shape, BF16),
        in_specs=[pl.BlockSpec(memory_space=pltpu.VMEM)],
        out_specs=pl.BlockSpec(memory_space=pltpu.VMEM),
        scratch_shapes=[pltpu.SemaphoreType.DMA((4, 2, 9)), pltpu.SemaphoreType.DMA((4, 2, 8)), pltpu.SemaphoreType.DMA],
        compiler_params=pltpu.CompilerParams(collective_id=cid, has_side_effects=True, vmem_limit_bytes=32 * 2**20),
        name="gather_weights",
    )(own.reshape(shape))
    return out.reshape(4, rows, cols)


class LineSum:
    def __init__(self, part, leaf, mid, total, send, recv, rows, lags=(0, 2, 4)):
        self.part, self.leaf, self.mid, self.total, self.send, self.recv = part, leaf, mid, total, send, recv
        self.rows, self.lags = rows, lags
        self.count = part.shape[0] // rows
        self.dp, self.f = lax.axis_index("dp"), lax.axis_index("feat")

    def barrier(self):
        sem = pltpu.get_barrier_semaphore()
        dp, f = self.dp, self.f

        @pl.when(f > 0)
        def _():
            pl.semaphore_signal(sem, inc=1, device_id=(dp, f - 1), device_id_type=MESH)

        @pl.when(f < 3)
        def _():
            pl.semaphore_signal(sem, inc=1, device_id=(dp, f + 1), device_id_type=MESH)
        pl.semaphore_wait(sem, jnp.where(f > 0, 1, 0) + jnp.where(f < 3, 1, 0))

    def place(self, c):
        odd = lax.rem(c, 2)
        return self.f + odd * (3 - 2 * self.f), 1 - 2 * odd

    def copy(self, c, src, dst, kind, slot, to):
        at = pl.ds(pl.multiple_of(c * self.rows, self.rows), self.rows)
        return pltpu.make_async_remote_copy(
            src_ref=src.at[at], dst_ref=dst.at[at], send_sem=self.send.at[slot, c], recv_sem=self.recv.at[kind, c],
            device_id=(self.dp, to), device_id_type=MESH)

    def leaves(self, c):
        p, up = self.place(c)

        @pl.when(p == 3)
        def _():
            self.copy(c, self.part, self.leaf, 0, 0, self.f - up).start()

        @pl.when(p == 0)
        def _():
            self.copy(c, self.part, self.leaf, 0, 0, self.f + up).start()

    def middle(self, c):
        p, up = self.place(c)
        at = pl.ds(pl.multiple_of(c * self.rows, self.rows), self.rows)

        @pl.when(p == 2)
        def _():
            self.copy(c, self.part, self.leaf, 0, 0, self.f).wait_recv()
            self.part[at, :] = (self.part[at, :].astype(F32) + self.leaf[at, :].astype(F32)).astype(BF16)
            self.copy(c, self.part, self.mid, 1, 0, self.f - up).start()

    def root(self, c):
        p, up = self.place(c)
        at = pl.ds(pl.multiple_of(c * self.rows, self.rows), self.rows)

        @pl.when(p == 1)
        def _():
            self.copy(c, self.part, self.leaf, 0, 0, self.f).wait_recv()
            self.copy(c, self.part, self.mid, 1, 0, self.f).wait_recv()
            self.total[at, :] = (
                self.part[at, :].astype(F32) + self.leaf[at, :].astype(F32) + self.mid[at, :].astype(F32)
            ).astype(BF16)
            self.copy(c, self.total, self.total, 2, 1, self.f + up).start()
            self.copy(c, self.total, self.total, 2, 0, self.f - up).start()

    def onward(self, c):
        p, up = self.place(c)

        @pl.when(p == 2)
        def _():
            self.copy(c, self.total, self.total, 2, 0, self.f).wait_recv()
            self.copy(c, self.total, self.total, 2, 1, self.f + up).start()

    def serve(self, i):
        for lag, act in zip(self.lags, (self.middle, self.root, self.onward)):
            c = i - lag

            @pl.when(jnp.logical_and(c >= 0, c < self.count))
            def _():
                act(c)

    def steps(self):
        return self.count + self.lags[-1]

    def arrived(self, c):
        p, up = self.place(c)

        @pl.when(jnp.logical_or(p == 0, p == 3))
        def _():
            self.copy(c, self.total, self.total, 2, 0, self.f).wait_recv()

    def drain(self, c):
        p, up = self.place(c)
        self.copy(c, self.part, self.part, 0, 0, self.f).wait_send()

        @pl.when(jnp.logical_or(p == 1, p == 2))
        def _():
            self.copy(c, self.part, self.part, 0, 1, self.f).wait_send()


def line_sum_kernel(rows, lags, in_ref, total_ref, part, leaf, mid, send, recv):
    line = LineSum(part, leaf, mid, total_ref, send, recv, rows, lags)
    line.barrier()
    part[...] = in_ref[...]

    def each(act, n):
        def body(c, carry):
            act(c)
            return carry
        lax.fori_loop(0, n, body, 0)
    each(line.leaves, line.count)
    each(line.serve, line.steps())
    each(line.arrived, line.count)
    each(line.drain, line.count)


def line_sum(x, cid, rows=32, lags=(0, 2, 4)):
    length = x.shape[0]
    count = length // rows
    return pl.pallas_call(
        functools.partial(line_sum_kernel, rows, lags),
        out_shape=jax.ShapeDtypeStruct(x.shape, BF16),
        in_specs=[pl.BlockSpec(memory_space=pltpu.VMEM)],
        out_specs=pl.BlockSpec(memory_space=pltpu.VMEM),
        scratch_shapes=[pltpu.VMEM(x.shape, BF16)] * 3 + [pltpu.SemaphoreType.DMA((2, count)), pltpu.SemaphoreType.DMA((3, count))],
        compiler_params=pltpu.CompilerParams(collective_id=cid, has_side_effects=True, vmem_limit_bytes=32 * 2**20),
        name="line_sum",
    )(x)


class CubeSum:
    def __init__(self, work, recv, out, send_sem, recv_sem, pieces, bits):
        self.work, self.recv, self.out, self.send_sem, self.recv_sem = work, recv, out, send_sem, recv_sem
        self.pieces, self.nb = pieces, len(bits)
        self.dp, self.f = lax.axis_index("dp"), lax.axis_index("feat")
        self.orders = [list(bits), [bits[0]] + list(bits[1:])[::-1]]
        self.bits = bits

    def partner(self, bit):
        return self.dp + bit - 2 * bit * lax.rem(self.dp // bit, 2)

    def barrier(self):
        sem = pltpu.get_barrier_semaphore()
        for bit in self.bits:
            pl.semaphore_signal(sem, inc=1, device_id=(self.partner(bit), self.f), device_id_type=MESH)
        pl.semaphore_wait(sem, len(self.bits))

    def lanes(self, colour):
        half = self.work.shape[1] // 2
        return pl.ds(colour * half, half)

    def segment(self, piece, colour, k):
        first, rows = self.pieces[piece]
        start = first
        for bit in self.orders[colour][:k]:
            rows = rows // 2
            start = start + rows * lax.rem(self.dp // bit, 2)
        return start, rows

    def at(self, start, rows):
        return pl.ds(pl.multiple_of(start, 16), rows)

    def halve(self, piece, colour, k):
        start, rows = self.segment(piece, colour, k)
        rows = rows // 2
        bit = self.orders[colour][k]
        own = lax.rem(self.dp // bit, 2)
        first, whole = self.pieces[piece]
        landing = first + whole - 2 * rows
        return pltpu.make_async_remote_copy(
            src_ref=self.work.at[self.at(start + rows * (1 - own), rows), self.lanes(colour)],
            dst_ref=self.recv.at[self.at(landing, rows), self.lanes(colour)],
            send_sem=self.send_sem.at[piece, colour, k], recv_sem=self.recv_sem.at[piece, colour, k],
            device_id=(self.partner(bit), self.f), device_id_type=MESH)

    def add(self, piece, colour, k):
        start, rows = self.segment(piece, colour, k + 1)
        first, whole = self.pieces[piece]
        landing = first + whole - 2 * rows
        target = self.out if k + 1 == self.nb else self.work
        mine = self.work[self.at(start, rows), self.lanes(colour)].astype(F32)
        target[self.at(start, rows), self.lanes(colour)] = (
            mine + self.recv[self.at(landing, rows), self.lanes(colour)].astype(F32)
        ).astype(BF16)

    def double(self, piece, colour, k):
        start, rows = self.segment(piece, colour, k + 1)
        bit = self.orders[colour][k]
        at = self.at(start, rows)
        slot = 2 * self.nb - 1 - k
        return pltpu.make_async_remote_copy(
            src_ref=self.out.at[at, self.lanes(colour)], dst_ref=self.out.at[at, self.lanes(colour)],
            send_sem=self.send_sem.at[piece, colour, slot], recv_sem=self.recv_sem.at[piece, colour, slot],
            device_id=(self.partner(bit), self.f), device_id_type=MESH)

    def launch(self, piece):
        for colour in range(2):
            self.halve(piece, colour, 0).start()

    def advance(self, piece, t):
        for colour in range(2):
            if t < self.nb:
                self.halve(piece, colour, t).wait_recv()
                self.add(piece, colour, t)
                if t + 1 < self.nb:
                    self.halve(piece, colour, t + 1).start()
                else:
                    self.double(piece, colour, self.nb - 1).start()
            else:
                k = 2 * self.nb - 1 - t
                self.double(piece, colour, k).wait_recv()
                if k > 0:
                    self.double(piece, colour, k - 1).start()

    def drain(self, piece):
        for colour in range(2):
            for k in range(self.nb):
                self.halve(piece, colour, k).wait_send()
                self.double(piece, colour, k).wait_send()


def cube_sum_kernel(pieces, bits, in_ref, out_ref, work, recv, send_sem, recv_sem):
    cube = CubeSum(work, recv, out_ref, send_sem, recv_sem, pieces, bits)
    work[...] = in_ref[...]
    cube.barrier()
    n = len(pieces)
    for p in range(n):
        cube.launch(p)
    for t in range(2 * cube.nb):
        for p in range(n):
            cube.advance(p, t)
    for p in range(n):
        cube.drain(p)


def split_rows(rows, unit, count):
    units = rows // unit
    out, first = [], 0
    for n in range(count):
        take = (units * (n + 1) // count - units * n // count) * unit
        out.append((first, take))
        first += take
    return [p for p in out if p[1]]


def cube_sum(x, dp_size, cid, count=3):
    rows = x.shape[0]
    bits = tuple(2**n for n in range(dp_size.bit_length() - 1))
    pieces = split_rows(rows, 16 * dp_size, count)
    return pl.pallas_call(
        functools.partial(cube_sum_kernel, pieces, bits),
        out_shape=jax.ShapeDtypeStruct(x.shape, BF16),
        in_specs=[pl.BlockSpec(memory_space=pltpu.VMEM)],
        out_specs=pl.BlockSpec(memory_space=pltpu.VMEM),
        scratch_shapes=[pltpu.VMEM(x.shape, BF16)] * 2 + [pltpu.SemaphoreType.DMA((len(pieces), 2, 2 * len(bits)))] * 2,
        compiler_params=pltpu.CompilerParams(collective_id=cid, has_side_effects=True, vmem_limit_bytes=40 * 2**20),
        name="cube_sum",
    )(x)
def attn_bwd_kernel(
    hb, starts_ref, q_ref, k_ref, v_ref, attn_ref, rd_ref, ga_ref, out_w_ref,
    gq_ref, gk_ref, gv_ref, mask_ref, gn_ref, gd_ref, qt_ref, gnt_ref, gkt_ref, gvt_ref,
):
    block = pl.program_id(0)

    @pl.when(block == 0)
    def _():
        gkt_ref[...] = jnp.zeros_like(gkt_ref)
        gvt_ref[...] = jnp.zeros_like(gvt_ref)

    low_block = first_start(starts_ref, block * BT) // BT
    fill_mask(starts_ref, mask_ref, block, low_block)
    lane = lax.broadcasted_iota(jnp.int32, (1, 128), 1)
    qt_ref[...] = q_ref[...].T

    def prepare(m, carry):
        vl = pl.ds(pl.multiple_of(m * 128, 128), 128)
        grad_attn = nt(ga_ref[...], out_w_ref[vl, :])
        grad_numer = grad_attn * (2.0 * rd_ref[:, vl])
        both = grad_numer * attn_ref[:, vl].astype(F32)
        first = jnp.sum(jnp.where(lane < HV, both, 0.0), axis=1, keepdims=True)
        second = jnp.sum(jnp.where(lane < HV, 0.0, both), axis=1, keepdims=True)
        gd_ref[:, vl] = jnp.where(lane < HV, -second, -first).astype(BF16)
        low = grad_numer.astype(BF16)
        gn_ref[:, vl] = low
        gnt_ref[vl, :] = low.T
        return carry

    lax.fori_loop(0, HEADS // 2, prepare, 0)

    def group(g, carry):
        first = g * hb
        qlanes = pl.ds(pl.multiple_of(first // 8 * 128, 128), 128)
        q = q_ref[:, qlanes]
        qms, gns = [], []
        for n in range(hb):
            h8 = lax.rem(first + n, 8)
            qms.append(jnp.where(lane // QK == h8, q, jnp.zeros_like(q)))
            vl = pl.ds(pl.multiple_of((first + n) // 2 * 128, 128), 128)
            gn = gn_ref[:, vl]
            gn = jnp.where(lane // HV == n % 2, gn, jnp.zeros_like(gn))
            gns.append(jnp.where(lane == HV * (1 - n % 2), gd_ref[:, vl], gn))

        def step(j, gq):
            rows = pl.ds(pl.multiple_of(j * BT, BT), BT)
            k = k_ref[rows, qlanes]
            mask = mask_ref[j]
            for n in range(hb):
                h = first + n
                vl = pl.ds(pl.multiple_of(h // 2 * 128, 128), 128)
                v = v_ref[rows, vl]
                v = jnp.where(lane // HV == n % 2, v, jnp.ones_like(v))
                t1 = nt(qms[n], k) + 1.0
                p = (t1 * t1 + 1.0).astype(BF16) * mask
                dp = nt(gns[n], v).astype(BF16) * mask
                gs = (dp.astype(F32) * t1).astype(BF16)
                h8 = lax.rem(h, 8)
                km = jnp.where(lane // QK == h8, k, jnp.zeros_like(k))
                gq = gq + nn(gs, km)
                qrows = pl.ds(pl.multiple_of(h * QK, QK), QK)
                vrows = pl.ds(pl.multiple_of(h * HV, HV), HV)
                gkt_ref[qrows, rows] += nn(qt_ref[qrows, :], gs)
                gvt_ref[vrows, rows] += nn(gnt_ref[vrows, :], p)
            return gq

        gq = lax.fori_loop(low_block, block + 1, step, jnp.zeros((BT, 128), F32))
        gq_ref[:, qlanes] = (gq * 0.25).astype(BF16)
        return carry

    lax.fori_loop(0, HEADS // hb, group, 0)

    @pl.when(block == pl.num_programs(0) - 1)
    def _():
        gk_ref[...] = gkt_ref[...].T.astype(BF16)

        def turn(m, carry):
            vl = pl.ds(pl.multiple_of(m * 128, 128), 128)
            gv_ref[:, vl] = (gvt_ref[vl, :] * 0.5).T.astype(BF16)
            return carry

        lax.fori_loop(0, HEADS // 2, turn, 0)


def attn_bwd(starts, q, k, v, attn, rd, ga, out_w):
    hb = 8
    length = q.shape[0]
    nq, nv = HEADS * QK, HEADS * HV

    def whole(rows, cols):
        return pl.BlockSpec((rows, cols), lambda i: (0, 0))

    def rowblk(cols):
        return pl.BlockSpec((BT, cols), lambda i: (i, 0))

    return pl.pallas_call(
        functools.partial(attn_bwd_kernel, hb),
        grid=(length // BT,),
        out_shape=(
            jax.ShapeDtypeStruct((length, nq), BF16),
            jax.ShapeDtypeStruct((length, nq), BF16),
            jax.ShapeDtypeStruct((length, nv), BF16),
        ),
        in_specs=[
            pl.BlockSpec(memory_space=pltpu.SMEM),
            rowblk(nq), whole(length, nq), whole(length, nv), rowblk(nv), rowblk(nv), rowblk(nv), whole(nv, D),
        ],
        out_specs=(rowblk(nq), whole(length, nq), whole(length, nv)),
        scratch_shapes=[
            pltpu.VMEM((length // BT, BT, BT), BF16),
            pltpu.VMEM((BT, nv), BF16),
            pltpu.VMEM((BT, nv), BF16),
            pltpu.VMEM((nq, BT), BF16),
            pltpu.VMEM((nv, BT), BF16),
            pltpu.VMEM((nq, length), F32),
            pltpu.VMEM((nv, length), F32),
        ],
        compiler_params=pltpu.CompilerParams(vmem_limit_bytes=50 * 2**20),
        name="attn_bwd",
    )(starts, q, k, v, attn, rd, ga, out_w)


def update(weight, grad_total, moment, average, rate):
    moment_next = MOMENTUM * moment + grad_total
    weight_next = weight - rate * (grad_total + MOMENTUM * moment_next)
    average_next = average + (weight_next - average) / STEP
    return (moment_next, weight_next, average_next)


def on_device(
    tokens,
    cotangent,
    doc_starts,
    queries_keys,
    value_weight,
    out_weight,
    gate_up,
    down_weight,
    norm_gains,
    queries_moment,
    value_moment,
    out_moment,
    gate_moment,
    down_moment,
    gains_moment,
    queries_average,
    value_average,
    out_average,
    gate_average,
    down_average,
    gains_average,
):
    groups = lax.axis_size("feat")
    length = tokens.shape[0]
    total_tokens = float(length * lax.axis_size("dp"))
    half = HEADS * QK
    pair_cols = queries_keys.shape[1]
    value_cols = value_weight.shape[1]
    feat = lax.axis_index("feat")
    gate_low = gate_up.astype(BF16)
    down_low = down_weight.astype(BF16)
    own = jnp.concatenate(
        [queries_keys.astype(BF16), value_weight.astype(BF16), out_weight.astype(BF16).T], axis=1
    )
    gathered = gather_all(own, 1)
    pairs_full = gathered[:, :, :pair_cols].transpose(1, 0, 2).reshape(D, 2 * half)
    values_full = gathered[:, :, pair_cols : pair_cols + value_cols].transpose(1, 0, 2).reshape(D, HEADS * HV)
    all_out = gathered[:, :, pair_cols + value_cols :].transpose(0, 2, 1).reshape(HEADS * HV, D)
    inputs = tokens.astype(F32)
    scale_one = lax.rsqrt(jnp.mean(inputs * inputs, axis=1, keepdims=True) + EPS)
    unit_one = inputs * scale_one
    normed_one = (unit_one * norm_gains[0]).astype(BF16)
    pairs = jnp.dot(normed_one, pairs_full, preferred_element_type=F32).astype(BF16)
    values = jnp.dot(normed_one, values_full, preferred_element_type=F32).astype(BF16)
    queries = pairs[:, :half] * jnp.bfloat16(0.25)
    keys = pairs[:, half:]
    attn_low, recip = attn_fwd(doc_starts, queries, keys, values, 8)
    attended = jnp.dot(attn_low, all_out, preferred_element_type=F32)
    hidden_one = inputs + attended
    scale_two = lax.rsqrt(jnp.mean(hidden_one * hidden_one, axis=1, keepdims=True) + EPS)
    unit_two = hidden_one * scale_two
    normed_two = (unit_two * norm_gains[1]).astype(jnp.bfloat16)
    gate_value = jnp.dot(normed_two, gate_low[0], preferred_element_type=jnp.float32)
    up_value = jnp.dot(normed_two, gate_low[1], preferred_element_type=jnp.float32)
    activated = jax.nn.silu(gate_value)
    hidden_low = (activated * up_value).astype(jnp.bfloat16)
    ffn_out = line_sum(jnp.dot(hidden_low, down_low, preferred_element_type=F32).astype(BF16), 2).astype(F32)
    mixed = (hidden_one + ffn_out).astype(jnp.bfloat16)
    grad_down = jnp.einsum("tf,td->fd", hidden_low, cotangent, preferred_element_type=jnp.float32)
    grad_hidden_units = jnp.einsum(
        "td,fd->tf", cotangent, down_low, preferred_element_type=jnp.float32
    )
    sigmoid_gate = jax.nn.sigmoid(gate_value)
    slope = sigmoid_gate * (1.0 + gate_value * (1.0 - sigmoid_gate))
    grad_gate = (grad_hidden_units * up_value * slope).astype(jnp.bfloat16)
    grad_up = (grad_hidden_units * activated).astype(jnp.bfloat16)
    grad_gate_turned = jnp.einsum("tf,td->fd", grad_gate, normed_two, preferred_element_type=F32)
    grad_up_turned = jnp.einsum("tf,td->fd", grad_up, normed_two, preferred_element_type=F32)
    normed_two_part = jnp.einsum(
        "tf,df->td", grad_gate, gate_low[0], preferred_element_type=jnp.float32
    ) + jnp.einsum("tf,df->td", grad_up, gate_low[1], preferred_element_type=jnp.float32)
    grad_normed_two = line_sum(normed_two_part.astype(BF16), 2).astype(F32)
    gain_two = jnp.sum(grad_normed_two * unit_two, axis=0)
    grad_unit_two = grad_normed_two * norm_gains[1]
    grad_hidden = cotangent.astype(jnp.float32) + scale_two * (
        grad_unit_two - unit_two * jnp.mean(grad_unit_two * unit_two, axis=1, keepdims=True)
    )
    grad_attended = grad_hidden.astype(jnp.bfloat16)
    own_attn = lax.dynamic_slice_in_dim(attn_low, feat * value_cols, value_cols, 1)
    grad_out = jnp.einsum("tv,td->vd", own_attn, grad_attended, preferred_element_type=F32)
    grad_queries, grad_keys, grad_values = attn_bwd(
        doc_starts, queries, keys, values, attn_low, recip, grad_attended, all_out
    )
    grad_pairs_all = jnp.concatenate([grad_queries, grad_keys], axis=1)
    own_pairs = lax.dynamic_slice_in_dim(grad_pairs_all, feat * pair_cols, pair_cols, 1)
    own_values = lax.dynamic_slice_in_dim(grad_values, feat * value_cols, value_cols, 1)
    grad_pairs_turned = jnp.einsum("tq,td->qd", own_pairs, normed_one, preferred_element_type=F32)
    grad_value_turned = jnp.einsum("tv,td->vd", own_values, normed_one, preferred_element_type=F32)
    grad_normed_one = jnp.einsum(
        "tq,dq->td", grad_pairs_all, pairs_full, preferred_element_type=F32
    ) + jnp.einsum("tv,dv->td", grad_values, values_full, preferred_element_type=F32)
    gain_one = jnp.sum(grad_normed_one * unit_one, axis=0)
    grad_unit_one = grad_normed_one * norm_gains[0]
    input_gradient = grad_hidden + scale_one * (
        grad_unit_one - unit_one * jnp.mean(grad_unit_one * unit_one, axis=1, keepdims=True)
    )
    dp_size = lax.axis_size("dp")
    units = [grad_down, grad_gate_turned, grad_up_turned, grad_out, grad_value_turned, grad_pairs_turned]
    units = [u.astype(BF16) for u in units] + [jnp.stack([gain_one, gain_two]).astype(BF16)]
    stacked = jnp.concatenate(units, axis=0)
    rows = stacked.shape[0]
    unit = 16 * dp_size
    stacked = jnp.pad(stacked, ((0, (rows + unit - 1) // unit * unit - rows), (0, 0)))
    summed = cube_sum(stacked, dp_size, 3, 4)
    parts, at = [], 0
    for u in units:
        parts.append(summed[at : at + u.shape[0]].astype(F32))
        at += u.shape[0]
    grad_down, grad_out, grad_gains = parts[0], parts[3], parts[6]
    grad_gate_up = jnp.stack([parts[1].T, parts[2].T])
    grad_value, grad_pairs = parts[4].T, parts[5].T
    first = update(
        queries_keys, grad_pairs, queries_moment, queries_average, (D * total_tokens) ** (-0.5)
    )
    second = update(
        value_weight, grad_value, value_moment, value_average, (D * total_tokens) ** (-0.5)
    )
    third = update(
        out_weight, grad_out, out_moment, out_average, (HEADS * HV * total_tokens) ** (-0.5)
    )
    fourth = update(gate_up, grad_gate_up, gate_moment, gate_average, (D * total_tokens) ** (-0.5))
    fifth = update(down_weight, grad_down, down_moment, down_average, (FF * total_tokens) ** (-0.5))
    sixth = update(
        norm_gains, grad_gains, gains_moment, gains_average, 0.2 * total_tokens ** (-0.5)
    )
    return (
        mixed,
        input_gradient,
        first[0],
        first[1],
        first[2],
        second[0],
        second[1],
        second[2],
        third[0],
        third[1],
        third[2],
        fourth[0],
        fourth[1],
        fourth[2],
        fifth[0],
        fifth[1],
        fifth[2],
        sixth[0],
        sixth[1],
        sixth[2],
    )


def solution(mesh):
    in_specs = (
        P("dp", None),
        P("dp", None),
        P("dp", None),
        P(None, "feat"),
        P(None, "feat"),
        P("feat", None),
        P(None, None, "feat"),
        P("feat", None),
        P(),
        P(None, "feat"),
        P(None, "feat"),
        P("feat", None),
        P(None, None, "feat"),
        P("feat", None),
        P(),
        P(None, "feat"),
        P(None, "feat"),
        P("feat", None),
        P(None, None, "feat"),
        P("feat", None),
        P(),
    )
    out_specs = (
        P("dp", None),
        P("dp", None),
        P(None, "feat"),
        P(None, "feat"),
        P(None, "feat"),
        P(None, "feat"),
        P(None, "feat"),
        P(None, "feat"),
        P("feat", None),
        P("feat", None),
        P("feat", None),
        P(None, None, "feat"),
        P(None, None, "feat"),
        P(None, None, "feat"),
        P("feat", None),
        P("feat", None),
        P("feat", None),
        P(),
        P(),
        P(),
    )
    return jax.shard_map(
        on_device, mesh=mesh, in_specs=in_specs, out_specs=out_specs, check_vma=False
    )
```

```python
import functools
import jax
import jax.numpy as jnp
from jax import lax
from jax.experimental import pallas as pl
from jax.experimental.pallas import tpu as pltpu
from jax.sharding import PartitionSpec as P

D = 1024
HEADS = 16
QK = 16
HV = 64
FF = 2752
STEP = 4
BT = 256
F32 = jnp.float32
BF16 = jnp.bfloat16

MESH = pl.DeviceIdType.MESH
EPS = 1e-06
MOMENTUM = 0.9


def nt(a, b):
    return lax.dot_general(a, b, (((1,), (1,)), ((), ())), preferred_element_type=F32)


def nn(a, b):
    return lax.dot_general(a, b, (((1,), (0,)), ((), ())), preferred_element_type=F32)


def first_start(starts_ref, t):
    begin = jnp.int32(0)
    for n in range(starts_ref.shape[1]):
        begin = jnp.where(starts_ref[0, n] <= t, jnp.maximum(begin, starts_ref[0, n]), begin)
    return begin


def fill_mask(starts_ref, mask_ref, block, low_block):
    t = block * BT + lax.broadcasted_iota(jnp.int32, (BT, 1), 0)
    begin = jnp.zeros((BT, 1), jnp.int32)
    for n in range(starts_ref.shape[1]):
        begin = jnp.where(starts_ref[0, n] <= t, jnp.maximum(begin, starts_ref[0, n]), begin)

    def one(j, carry):
        s = j * BT + lax.broadcasted_iota(jnp.int32, (BT, BT), 1)
        keep = jnp.logical_and(s <= t, s >= begin)
        mask_ref[j] = keep.astype(F32).astype(BF16)
        return carry
    lax.fori_loop(low_block, block + 1, one, 0)


def attn_fwd_kernel(hb, starts_ref, q_ref, k_ref, v_ref, o_ref, rd_ref, mask_ref):
    block = pl.program_id(0)
    low_block = first_start(starts_ref, block * BT) // BT
    fill_mask(starts_ref, mask_ref, block, low_block)
    lane = lax.broadcasted_iota(jnp.int32, (1, 128), 1)

    def group(g, carry):
        qlanes = pl.ds(pl.multiple_of((g * hb) // 8 * 128, 128), 128)
        q = q_ref[:, qlanes]
        qms = []
        for n in range(hb):
            h8 = lax.rem(g * hb + n, 8)
            qms.append(jnp.where(lane // QK == h8, q, jnp.zeros_like(q)))

        def step(j, accs):
            rows = pl.ds(pl.multiple_of(j * BT, BT), BT)
            k = k_ref[rows, qlanes]
            mask = mask_ref[j]
            out = []
            for n in range(hb):
                vl = pl.ds(pl.multiple_of((g * hb + n) // 2 * 128, 128), 128)
                v = v_ref[rows, vl]
                v = jnp.where(lane // HV == n % 2, v, jnp.ones_like(v))
                t1 = nt(qms[n], k) + 1.0
                p = (t1 * t1 + 1.0).astype(BF16) * mask
                out.append(accs[n] + nn(p, v))
            return tuple(out)
        accs = lax.fori_loop(low_block, block + 1, step, tuple(jnp.zeros((BT, 128), F32) for _ in range(hb)))
        for m in range(hb // 2):
            vl = pl.ds(pl.multiple_of((g * hb + 2 * m) // 2 * 128, 128), 128)
            first, second = accs[2 * m], accs[2 * m + 1]
            numer = jnp.where(lane < HV, first, second)
            denom = pltpu.roll(jnp.where(lane < HV, second, first), HV, 1)
            recip = 1.0 / denom
            o_ref[:, vl] = (numer * recip).astype(BF16)
            rd_ref[:, vl] = recip
        return carry
    lax.fori_loop(0, HEADS // hb, group, 0)


def attn_fwd(starts, pairs, v, hb):
    length = pairs.shape[0]
    return pl.pallas_call(
        functools.partial(attn_fwd_kernel, hb),
        grid=(length // BT,),
        out_shape=(jax.ShapeDtypeStruct((length, HEADS * HV), BF16), jax.ShapeDtypeStruct((length, HEADS * HV), F32)),
        in_specs=[pl.BlockSpec(memory_space=pltpu.SMEM), pl.BlockSpec((BT, HEADS * QK), lambda i: (i, 0)),
                  pl.BlockSpec((length, HEADS * QK), lambda i: (0, 1)), pl.BlockSpec((length, HEADS * HV), lambda i: (0, 0))],
        out_specs=(pl.BlockSpec((BT, HEADS * HV), lambda i: (i, 0)), pl.BlockSpec((BT, HEADS * HV), lambda i: (i, 0))),
        scratch_shapes=[pltpu.VMEM((length // BT, BT, BT), BF16)],
        compiler_params=pltpu.CompilerParams(vmem_limit_bytes=40 * 2**20),
        name="mixer",
    )(starts, pairs, pairs, v)


class LineSum:
    def __init__(self, part, leaf, mid, total, send, recv, rows, lags=(0, 2, 4)):
        self.part, self.leaf, self.mid, self.total, self.send, self.recv = part, leaf, mid, total, send, recv
        self.rows, self.lags = rows, lags
        self.count = part.shape[0] // rows
        self.dp, self.f = lax.axis_index("dp"), lax.axis_index("feat")

    def barrier(self):
        sem = pltpu.get_barrier_semaphore()
        dp, f = self.dp, self.f

        @pl.when(f > 0)
        def _():
            pl.semaphore_signal(sem, inc=1, device_id=(dp, f - 1), device_id_type=MESH)

        @pl.when(f < 3)
        def _():
            pl.semaphore_signal(sem, inc=1, device_id=(dp, f + 1), device_id_type=MESH)
        pl.semaphore_wait(sem, jnp.where(f > 0, 1, 0) + jnp.where(f < 3, 1, 0))

    def place(self, c):
        odd = lax.rem(c, 2)
        return self.f + odd * (3 - 2 * self.f), 1 - 2 * odd

    def copy(self, c, src, dst, kind, slot, to):
        at = pl.ds(pl.multiple_of(c * self.rows, self.rows), self.rows)
        return pltpu.make_async_remote_copy(
            src_ref=src.at[at], dst_ref=dst.at[at], send_sem=self.send.at[slot, c], recv_sem=self.recv.at[kind, c],
            device_id=(self.dp, to), device_id_type=MESH)

    def leaves(self, c):
        p, up = self.place(c)

        @pl.when(p == 3)
        def _():
            self.copy(c, self.part, self.leaf, 0, 0, self.f - up).start()

        @pl.when(p == 0)
        def _():
            self.copy(c, self.part, self.leaf, 0, 0, self.f + up).start()

    def middle(self, c):
        p, up = self.place(c)
        at = pl.ds(pl.multiple_of(c * self.rows, self.rows), self.rows)

        @pl.when(p == 2)
        def _():
            self.copy(c, self.part, self.leaf, 0, 0, self.f).wait_recv()
            self.part[at, :] = (self.part[at, :].astype(F32) + self.leaf[at, :].astype(F32)).astype(BF16)
            self.copy(c, self.part, self.mid, 1, 0, self.f - up).start()

    def root(self, c):
        p, up = self.place(c)
        at = pl.ds(pl.multiple_of(c * self.rows, self.rows), self.rows)

        @pl.when(p == 1)
        def _():
            self.copy(c, self.part, self.leaf, 0, 0, self.f).wait_recv()
            self.copy(c, self.part, self.mid, 1, 0, self.f).wait_recv()
            self.total[at, :] = (
                self.part[at, :].astype(F32) + self.leaf[at, :].astype(F32) + self.mid[at, :].astype(F32)
            ).astype(BF16)
            self.copy(c, self.total, self.total, 2, 1, self.f + up).start()
            self.copy(c, self.total, self.total, 2, 0, self.f - up).start()

    def onward(self, c):
        p, up = self.place(c)

        @pl.when(p == 2)
        def _():
            self.copy(c, self.total, self.total, 2, 0, self.f).wait_recv()
            self.copy(c, self.total, self.total, 2, 1, self.f + up).start()

    def serve(self, i):
        for lag, act in zip(self.lags, (self.middle, self.root, self.onward)):
            c = i - lag

            @pl.when(jnp.logical_and(c >= 0, c < self.count))
            def _():
                act(c)

    def steps(self):
        return self.count + self.lags[-1]

    def arrived(self, c):
        p, up = self.place(c)

        @pl.when(jnp.logical_or(p == 0, p == 3))
        def _():
            self.copy(c, self.total, self.total, 2, 0, self.f).wait_recv()

    def drain(self, c):
        p, up = self.place(c)
        self.copy(c, self.part, self.part, 0, 0, self.f).wait_send()

        @pl.when(jnp.logical_or(p == 1, p == 2))
        def _():
            self.copy(c, self.part, self.part, 0, 1, self.f).wait_send()


class CubeSum:
    def __init__(self, work, recv, out, send_sem, recv_sem, pieces, bits):
        self.work, self.recv, self.out, self.send_sem, self.recv_sem = work, recv, out, send_sem, recv_sem
        self.pieces, self.nb = pieces, len(bits)
        self.dp, self.f = lax.axis_index("dp"), lax.axis_index("feat")
        self.orders = [list(bits), [bits[0]] + list(bits[1:])[::-1]]
        self.bits = bits

    def partner(self, bit):
        return self.dp + bit - 2 * bit * lax.rem(self.dp // bit, 2)

    def barrier(self):
        sem = pltpu.get_barrier_semaphore()
        for bit in self.bits:
            pl.semaphore_signal(sem, inc=1, device_id=(self.partner(bit), self.f), device_id_type=MESH)
        pl.semaphore_wait(sem, len(self.bits))

    def lanes(self, colour):
        half = self.work.shape[1] // 2
        return pl.ds(colour * half, half)

    def segment(self, piece, colour, k):
        first, rows = self.pieces[piece]
        start = first
        for bit in self.orders[colour][:k]:
            rows = rows // 2
            start = start + rows * lax.rem(self.dp // bit, 2)
        return start, rows

    def at(self, start, rows):
        return pl.ds(pl.multiple_of(start, 16), rows)

    def halve(self, piece, colour, k):
        start, rows = self.segment(piece, colour, k)
        rows = rows // 2
        bit = self.orders[colour][k]
        own = lax.rem(self.dp // bit, 2)
        first, whole = self.pieces[piece]
        landing = first + whole - 2 * rows
        return pltpu.make_async_remote_copy(
            src_ref=self.work.at[self.at(start + rows * (1 - own), rows), self.lanes(colour)],
            dst_ref=self.recv.at[self.at(landing, rows), self.lanes(colour)],
            send_sem=self.send_sem.at[piece, colour, k], recv_sem=self.recv_sem.at[piece, colour, k],
            device_id=(self.partner(bit), self.f), device_id_type=MESH)

    def add(self, piece, colour, k):
        start, rows = self.segment(piece, colour, k + 1)
        first, whole = self.pieces[piece]
        landing = first + whole - 2 * rows
        target = self.out if k + 1 == self.nb else self.work
        mine = self.work[self.at(start, rows), self.lanes(colour)].astype(F32)
        target[self.at(start, rows), self.lanes(colour)] = (
            mine + self.recv[self.at(landing, rows), self.lanes(colour)].astype(F32)
        ).astype(BF16)

    def double(self, piece, colour, k):
        start, rows = self.segment(piece, colour, k + 1)
        bit = self.orders[colour][k]
        at = self.at(start, rows)
        slot = 2 * self.nb - 1 - k
        return pltpu.make_async_remote_copy(
            src_ref=self.out.at[at, self.lanes(colour)], dst_ref=self.out.at[at, self.lanes(colour)],
            send_sem=self.send_sem.at[piece, colour, slot], recv_sem=self.recv_sem.at[piece, colour, slot],
            device_id=(self.partner(bit), self.f), device_id_type=MESH)

    def launch(self, piece):
        for colour in range(2):
            self.halve(piece, colour, 0).start()

    def advance(self, piece, t):
        for colour in range(2):
            if t < self.nb:
                self.halve(piece, colour, t).wait_recv()
                self.add(piece, colour, t)
                if t + 1 < self.nb:
                    self.halve(piece, colour, t + 1).start()
                else:
                    self.double(piece, colour, self.nb - 1).start()
            else:
                k = 2 * self.nb - 1 - t
                self.double(piece, colour, k).wait_recv()
                if k > 0:
                    self.double(piece, colour, k - 1).start()

    def drain(self, piece):
        for colour in range(2):
            for k in range(self.nb):
                self.halve(piece, colour, k).wait_send()
                self.double(piece, colour, k).wait_send()


def split_rows(rows, unit, count):
    units = rows // unit
    out, first = [], 0
    for n in range(count):
        take = (units * (n + 1) // count - units * n // count) * unit
        out.append((first, take))
        first += take
    return [p for p in out if p[1]]


def project_kernel(
    bits, tokens_in, gains_ref, pair_ref, value_ref, out_ref, gate_in, down_in,
    normed_ref, pairs_ref, values_ref, wide_ref, gate_ref, down_ref,
    all_ref, tokens_ref, gate_f32, down_f32, send_sem, recv_sem, load_sem,
):
    dp = lax.axis_index("dp")
    f = lax.axis_index("feat")
    last = lax.axis_size("feat") - 1
    slices = lax.axis_size("feat")
    pieces = 2 ** len(bits)
    j = lax.rem(dp, pieces)
    base = dp - j
    pair_cols, value_cols = pair_ref.shape[1], value_ref.shape[1]
    rows = pair_ref.shape[0] // pieces
    length = tokens_ref.shape[0]
    loads = [
        pltpu.make_async_copy(a, b, load_sem.at[n])
        for n, (a, b) in enumerate([(tokens_in, tokens_ref), (gate_in, gate_f32), (down_in, down_f32)])
    ]
    for load in loads:
        load.start()

    def flip(k, bit):
        return k + bit - 2 * bit * lax.rem(k // bit, 2)

    def cast(k):
        at = pl.ds(pl.multiple_of(k * rows, rows), rows)
        block = jnp.concatenate(
            [pair_ref[at, :].astype(BF16), value_ref[at, :].astype(BF16), out_ref[:, at].T.astype(BF16)], axis=1
        )
        all_ref[f, k, 0] = block[: rows // 2]
        all_ref[f, k, 1] = block[rows // 2 :]

    cast(j)
    barrier = pltpu.get_barrier_semaphore()
    for bit in bits:
        pl.semaphore_signal(barrier, inc=1, device_id=(base + flip(j, bit), f), device_id_type=MESH)

    @pl.when(f > 0)
    def _():
        pl.semaphore_signal(barrier, inc=1, device_id=(dp, f - 1), device_id_type=MESH)

    @pl.when(f < last)
    def _():
        pl.semaphore_signal(barrier, inc=1, device_id=(dp, f + 1), device_id_type=MESH)

    pl.semaphore_wait(barrier, len(bits) + jnp.where(f > 0, 1, 0) + jnp.where(f < last, 1, 0))

    def copy(z, colour, k, slot, device):
        return pltpu.make_async_remote_copy(
            src_ref=all_ref.at[z, k, colour], dst_ref=all_ref.at[z, k, colour], send_sem=send_sem.at[z, colour, slot],
            recv_sem=recv_sem.at[z, colour, k], device_id=device, device_id_type=MESH,
        )

    here = (dp, f)
    for colour in range(2):
        @pl.when(f > 0)
        def _():
            copy(f, colour, j, 0, (dp, f - 1)).start()

        @pl.when(f < last)
        def _():
            copy(f, colour, j, 1, (dp, f + 1)).start()

    order = [
        jnp.where(f == 0, 1, f - 1),
        jnp.where(f < 2, 2, jnp.where(f == 2, 3, 1)),
        jnp.where(f < 2, 3, 0),
    ]
    colour_bits = [list(bits[1:]) + [bits[0]], list(bits[1:])[::-1] + [bits[0]]]

    def held(colour, step):
        out = [j]
        for bit in colour_bits[colour][:step]:
            out = out + [flip(k, bit) for k in out]
        return out

    def start_step(z, step):
        for colour in range(2):
            first = 2 + 2**step - 1
            partner = (base + flip(j, colour_bits[colour][step]), f)
            for n, k in enumerate(held(colour, step)):
                copy(z, colour, k, first + n, partner).start()

    def wait_step(z, step):
        for colour in range(2):
            for k in held(colour, step):
                copy(z, colour, flip(k, colour_bits[colour][step]), 0, here).wait_recv()

    def arrive(z):
        ahead = jnp.where(z < f, f + 1, f - 1)
        onward = jnp.logical_and(ahead >= 0, ahead <= last)
        for colour in range(2):
            copy(z, colour, j, 0, here).wait_recv()

            @pl.when(onward)
            def _():
                copy(z, colour, j, jnp.where(z < f, 1, 0), (dp, ahead)).start()
        start_step(z, 0)

    half_pairs = slices * pair_cols // 2
    pairs_wide, values_wide = slices * pair_cols, slices * value_cols

    def use(z):
        weight = all_ref[z].reshape(pieces * rows, pair_cols + 2 * value_cols)
        pair_at = pl.ds(pl.multiple_of(z * pair_cols, pair_cols), pair_cols)
        value_at = pl.ds(pl.multiple_of(z * value_cols, value_cols), value_cols)
        wide_ref[:, pair_at] = weight[:, :pair_cols]
        wide_ref[:, pl.ds(pl.multiple_of(pairs_wide + z * value_cols, 128), value_cols)] = weight[
            :, pair_cols : pair_cols + value_cols
        ]
        wide_ref[:, pl.ds(pl.multiple_of(pairs_wide + values_wide + z * value_cols, 128), value_cols)] = weight[
            :, pair_cols + value_cols :
        ]
        factor = jnp.where(z * pair_cols < half_pairs, 0.25, 1.0).astype(F32)

        def some(n, carry):
            at = pl.ds(pl.multiple_of(n * BT, BT), BT)
            normed = normed_ref[at, :]
            pairs = nn(normed, wide_ref[:, pair_at])
            pairs_ref[at, pair_at] = (pairs.astype(BF16).astype(F32) * factor).astype(BF16)
            values_ref[at, value_at] = nn(
                normed, wide_ref[:, pl.ds(pl.multiple_of(pairs_wide + z * value_cols, 128), value_cols)]
            ).astype(BF16)
            return carry

        lax.fori_loop(0, length // BT, some, 0)

    def cast_rest(n, carry):
        cast(lax.rem(j + n, pieces))
        return carry

    lax.fori_loop(1, pieces, cast_rest, 0)
    loads[0].wait()

    def norm(n, carry):
        at = pl.ds(pl.multiple_of(n * BT, BT), BT)
        x = tokens_ref[at, :].astype(F32)
        scale = lax.rsqrt(jnp.mean(x * x, axis=1, keepdims=True) + EPS)
        normed_ref[at, :] = (x * scale * gains_ref[0:1, :]).astype(BF16)
        return carry

    lax.fori_loop(0, length // BT, norm, 0)

    steps = len(bits)
    arrive(order[0])
    use(f)
    loads[1].wait()
    loads[2].wait()

    def cast_gate(n):
        def go(m, carry):
            gate_ref[n, pl.ds(pl.multiple_of(m * 16, 16), 16), :] = gate_f32[
                n, pl.ds(pl.multiple_of(m * 16, 16), 16), :
            ].astype(BF16)
            return carry

        lax.fori_loop(0, gate_f32.shape[1] // 16, go, 0)

    def cast_down(m, carry):
        down_ref[pl.ds(pl.multiple_of(m * 16, 16), 16), :] = down_f32[pl.ds(pl.multiple_of(m * 16, 16), 16), :].astype(BF16)
        return carry

    plan = [(1, None), (0, 0), "gate", (2, None), (1, 0), (0, 1), "up", (2, 0), (1, 1), (0, 2), "down", (2, 1), (1, 2), (2, 2)]
    for item in plan:
        if item == "gate":
            cast_gate(0)
        elif item == "up":
            cast_gate(1)
        elif item == "down":
            lax.fori_loop(0, down_f32.shape[0] // 16, cast_down, 0)
        elif item[1] is None:
            arrive(order[item[0]])
        else:
            wait_step(order[item[0]], item[1])
            if item[1] + 1 < steps:
                start_step(order[item[0]], item[1] + 1)
            else:
                use(order[item[0]])
    for z in order:
        ahead = jnp.where(z < f, f + 1, f - 1)
        onward = jnp.logical_and(ahead >= 0, ahead <= last)
        for colour in range(2):
            @pl.when(onward)
            def _():
                copy(z, colour, j, jnp.where(z < f, 1, 0), here).wait_send()

            for step in range(steps):
                for n, k in enumerate(held(colour, step)):
                    copy(z, colour, k, 2 + 2**step - 1 + n, here).wait_send()
    for colour in range(2):
        @pl.when(f > 0)
        def _():
            copy(f, colour, j, 0, here).wait_send()

        @pl.when(f < last)
        def _():
            copy(f, colour, j, 1, here).wait_send()


def project(tokens, gains, pair_w, value_w, out_w, gate_turned, down):
    length = tokens.shape[0]
    ff = down.shape[0]
    slices = 4
    pair_cols, value_cols = pair_w.shape[1], value_w.shape[1]
    cols = pair_cols + 2 * value_cols
    bits = (1, 2, 4)
    hbm = pl.BlockSpec(memory_space=pl.ANY)
    vmem = pl.BlockSpec(memory_space=pltpu.VMEM)
    return pl.pallas_call(
        functools.partial(project_kernel, bits),
        out_shape=(
            jax.ShapeDtypeStruct((length, D), BF16),
            jax.ShapeDtypeStruct((length, slices * pair_cols), BF16),
            jax.ShapeDtypeStruct((length, slices * value_cols), BF16),
            jax.ShapeDtypeStruct((D, slices * cols), BF16),
            jax.ShapeDtypeStruct((2, ff, D), BF16),
            jax.ShapeDtypeStruct((ff, D), BF16),
        ),
        in_specs=[hbm] + [vmem] * 4 + [hbm] * 2,
        out_specs=(vmem,) * 6,
        scratch_shapes=[
            pltpu.VMEM((slices, 8, 2, D // 16, cols), BF16),
            pltpu.VMEM((length, D), BF16),
            pltpu.VMEM((2, ff, D), F32),
            pltpu.VMEM((ff, D), F32),
            pltpu.SemaphoreType.DMA((slices, 2, 9)),
            pltpu.SemaphoreType.DMA((slices, 2, 8)),
            pltpu.SemaphoreType.DMA((3,)),
        ],
        compiler_params=pltpu.CompilerParams(collective_id=1, has_side_effects=True, vmem_limit_bytes=56 * 2**20),
        name="project",
    )(tokens, gains, pair_w, value_w, out_w, gate_turned, down)


def feed_kernel(
    rows, tokens_in, cot_in, attn_in, wide_in, gate_in, down_in, gains_ref,
    hidden_out, grad_hidden_out, ga_ref, ffn_ref, grads_ref,
    tokens_ref, cot_ref, attn_ref, out_w, gate_ref, down_ref,
    hidden_ref, scale_ref, normed_ref, product_t, gate_t, up_t, own_t, gain_ref, gh_ref,
    part, leaf, mid, total, send, recv, load_sem, store_sem,
):
    f = lax.axis_index("feat")
    line = LineSum(part, leaf, mid, total, send, recv, rows, (0, 3, 6))
    length = tokens_ref.shape[0]
    ff = down_ref.shape[0]
    value_cols = own_t.shape[0]
    blocks = length // BT
    first_out = wide_in.shape[1] - attn_ref.shape[1]
    pairs = [(attn_in, attn_ref), (wide_in.at[:, pl.ds(first_out, attn_ref.shape[1])], out_w), (tokens_in, tokens_ref),
             (gate_in, gate_ref), (down_in, down_ref), (cot_in, cot_ref)]
    loads = [pltpu.make_async_copy(a, b, load_sem.at[n]) for n, (a, b) in enumerate(pairs)]
    for load in loads:
        load.start()
    greet(line, None)
    for load in loads:
        load.wait()

    def store(source, target, n, kind):
        at = pl.ds(pl.multiple_of(n * BT, BT), BT)
        return pltpu.make_async_copy(source.at[at], target.at[at], store_sem.at[kind, n])

    def block(b, carry):
        at = pl.ds(pl.multiple_of(b * BT, BT), BT)
        turn = 4 * (b - 1)
        hidden = tokens_ref[at, :].astype(F32) + nt(attn_ref[at, :], out_w[...])
        hidden_ref[at, :] = hidden
        store(hidden_ref, hidden_out, b, 0).start()
        scale = lax.rsqrt(jnp.mean(hidden * hidden, axis=1, keepdims=True) + EPS)
        scale_ref[at, :] = jnp.broadcast_to(scale, (BT, 128))
        normed = (hidden * scale * gains_ref[1:2, :]).astype(BF16)
        normed_ref[at, :] = normed
        line.serve(turn)
        gate = nt(normed, gate_ref[0])
        up = nt(normed, gate_ref[1])
        line.serve(turn + 1)
        back = nt(cot_ref[at, :], down_ref[...])
        sig = 1.0 / (1.0 + jnp.exp(-gate))
        active = gate * sig
        slope = sig * (1.0 + gate * (1.0 - sig))
        product = (active * up).astype(BF16)
        grad_gate = (back * up * slope).astype(BF16)
        grad_up = (back * active).astype(BF16)
        line.serve(turn + 2)
        part[at, :] = (nn(grad_gate, gate_ref[0]) + nn(grad_up, gate_ref[1])).astype(BF16)

        def out(c, carry):
            line.leaves(b * (BT // rows) + c)
            return carry

        lax.fori_loop(0, BT // rows, out, 0)
        ffn_ref[at, :] = nn(product, down_ref[...]).astype(BF16)
        product_t[:, at] = product.T
        gate_t[:, at] = grad_gate.T
        up_t[:, at] = grad_up.T
        line.serve(turn + 3)
        return carry

    lax.fori_loop(0, blocks, block, 0)
    served = 4 * (blocks - 1)
    gain_ref[...] = jnp.zeros_like(gain_ref)
    chunks = []
    at = 0
    while at < ff:
        chunks.append((at, min(176, ff - at)))
        at += chunks[-1][1]
    for n, (turned, right) in enumerate([(product_t, cot_ref), (gate_t, normed_ref), (up_t, normed_ref)]):
        for first, size in chunks:
            grads_ref[n * ff + first : n * ff + first + size, :] = nn(turned[first : first + size, :], right[...]).astype(BF16)
            line.serve(jnp.int32(served))
            served += 1
    own_t[...] = own_column(attn_ref, f, value_cols).T

    def back_rows(n):
        at = pl.ds(pl.multiple_of(n * BT, BT), BT)
        hidden, grad = hidden_ref[at, :], total[at, :].astype(F32)
        scale = scale_ref[at, 0:1]
        unit = hidden * scale
        u = grad * gains_ref[1:2, :]
        gh = cot_ref[at, :].astype(F32) + scale * (u - unit * jnp.mean(u * unit, axis=1, keepdims=True))
        gh_ref[at, :] = gh
        store(gh_ref, grad_hidden_out, n, 1).start()
        ga_ref[at, :] = gh.astype(BF16)
        gain_ref[0:1, :] += jnp.sum(grad * unit, axis=0, keepdims=True)

    per = BT // rows
    for n in range(blocks):
        until = min(per * (n + 1) + line.lags[-1], line.steps())

        def more(i, carry):
            line.serve(i)
            return carry

        lax.fori_loop(min(served, until), until, more, 0)
        served = max(served, until)
        lax.fori_loop(per * n, per * (n + 1), lambda c, carry: (line.arrived(c), carry)[1], 0)
        back_rows(jnp.int32(n))
    first = 3 * ff
    grads_ref[first : first + value_cols, :] = nn(own_t[...], ga_ref[...]).astype(BF16)
    first = first + value_cols
    rest = grads_ref.shape[0] - first
    grads_ref[first:, :] = jnp.zeros((rest, D), BF16)
    grads_ref[first : first + 16, :] = gain_ref[...].astype(BF16)
    each(line.drain, line.count)
    for n in range(blocks):
        store(hidden_ref, hidden_out, jnp.int32(n), 0).wait()
        store(gh_ref, grad_hidden_out, jnp.int32(n), 1).wait()


def feed(tokens, cotangent, attn, wide, gate_turned, down, gains, padded):
    length = tokens.shape[0]
    ff = down.shape[0]
    nv, rows = attn.shape[1], 32
    count = length // rows
    hbm = pl.BlockSpec(memory_space=pl.ANY)
    vmem = pl.BlockSpec(memory_space=pltpu.VMEM)
    return pl.pallas_call(
        functools.partial(feed_kernel, rows),
        out_shape=(
            jax.ShapeDtypeStruct((length, D), F32),
            jax.ShapeDtypeStruct((length, D), F32),
            jax.ShapeDtypeStruct((length, D), BF16),
            jax.ShapeDtypeStruct((length, D), BF16),
            jax.ShapeDtypeStruct((padded, D), BF16),
        ),
        in_specs=[hbm] * 6 + [vmem],
        out_specs=(hbm, hbm, vmem, vmem, vmem),
        scratch_shapes=[
            pltpu.VMEM((length, D), BF16), pltpu.VMEM((length, D), BF16), pltpu.VMEM((length, nv), BF16),
            pltpu.VMEM((D, nv), BF16), pltpu.VMEM((2, ff, D), BF16), pltpu.VMEM((ff, D), BF16),
            pltpu.VMEM((length, D), F32), pltpu.VMEM((length, 128), F32), pltpu.VMEM((length, D), BF16),
            pltpu.VMEM((ff, length), BF16), pltpu.VMEM((ff, length), BF16), pltpu.VMEM((ff, length), BF16),
            pltpu.VMEM((nv // 4, length), BF16), pltpu.VMEM((16, D), F32), pltpu.VMEM((length, D), F32),
            pltpu.VMEM((length, D), BF16), pltpu.VMEM((length, D), BF16), pltpu.VMEM((length, D), BF16),
            pltpu.VMEM((length, D), BF16),
            pltpu.SemaphoreType.DMA((2, count)), pltpu.SemaphoreType.DMA((3, count)),
            pltpu.SemaphoreType.DMA((6,)), pltpu.SemaphoreType.DMA((2, length // BT)),
        ],
        compiler_params=pltpu.CompilerParams(collective_id=2, has_side_effects=True, vmem_limit_bytes=60 * 2**20),
        name="feed",
    )(tokens, cotangent, attn, wide, gate_turned, down, gains)


def own_column(ref, f, width):
    return ref[:, pl.ds(pl.multiple_of(f * width, width), width)]


def mixer_back_kernel(
    pieces, bits, hb, rows,
    starts_ref, pairs_in, v_in, attn_in, rd_in, ga_in, wide_in, ffn_in, grads_in,
    gp_ref, gv_ref, total_ref, sums_ref,
    q_ref, k_ref, v_ref, attn_ref, rd_ref, ga_ref, out_ref,
    part, leaf, mid, work, landing,
    mask_ref, gn_ref, gd_ref, qt_ref, gnt_ref, gq_ref, gkt_ref, gvt_ref,
    line_send, line_recv, cube_send, cube_recv, load_sem,
):
    f = lax.axis_index("feat")
    line = LineSum(part, leaf, mid, total_ref, line_send, line_recv, rows, (0, 3, 6))
    cube = CubeSum(work, landing, sums_ref, cube_send, cube_recv, pieces, bits)
    pairs = [(grads_in, work), (ffn_in, part), (ga_in, ga_ref), (wide_in.at[:, pl.ds(wide_in.shape[1] - out_ref.shape[1], out_ref.shape[1])], out_ref), (rd_in, rd_ref), (attn_in, attn_ref),
             (pairs_in.at[:, pl.ds(0, HEADS * QK)], q_ref), (pairs_in.at[:, pl.ds(HEADS * QK, HEADS * QK)], k_ref), (v_in, v_ref)]
    loads = [pltpu.make_async_copy(a, b, load_sem.at[n]) for n, (a, b) in enumerate(pairs)]
    for load in loads:
        load.start()
    greet(line, cube)
    loads[0].wait()
    for p in range(len(pieces)):
        cube.launch(p)
    loads[1].wait()
    each(line.leaves, line.count)
    gkt_ref[...] = jnp.zeros_like(gkt_ref)
    gvt_ref[...] = jnp.zeros_like(gvt_ref)
    for load in loads[2:]:
        load.wait()

    lane = lax.broadcasted_iota(jnp.int32, (1, 128), 1)
    blocks = q_ref.shape[0] // BT
    groups = HEADS // hb

    def at_block(n):
        return pl.ds(pl.multiple_of(n * BT, BT), BT)

    def prepare(i):
        here = at_block(i)
        qt_ref[...] = q_ref[here, :].T
        gq_ref[...] = jnp.zeros_like(gq_ref)

        def one(m, carry):
            vl = pl.ds(pl.multiple_of(m * 128, 128), 128)
            grad_attn = nn(ga_ref[here, :], out_ref[:, vl])
            grad_numer = grad_attn * (2.0 * rd_ref[here, vl])
            both = grad_numer * attn_ref[here, vl].astype(F32)
            first = jnp.sum(jnp.where(lane < HV, both, 0.0), axis=1, keepdims=True)
            second = jnp.sum(jnp.where(lane < HV, 0.0, both), axis=1, keepdims=True)
            gd_ref[:, vl] = jnp.where(lane < HV, -second, -first).astype(BF16)
            low = grad_numer.astype(BF16)
            gn_ref[:, vl] = low
            gnt_ref[vl, :] = low.T
            return carry

        lax.fori_loop(0, HEADS // 2, one, 0)

    def make_mask(i, j):
        t = i * BT + lax.broadcasted_iota(jnp.int32, (BT, 1), 0)
        begin = jnp.zeros((BT, 1), jnp.int32)
        for n in range(starts_ref.shape[1]):
            begin = jnp.where(starts_ref[0, n] <= t, jnp.maximum(begin, starts_ref[0, n]), begin)
        s = j * BT + lax.broadcasted_iota(jnp.int32, (BT, BT), 1)
        mask_ref[...] = jnp.logical_and(s <= t, s >= begin).astype(F32).astype(BF16)

    steps = blocks * (blocks + 1) // 2 * groups
    sequence = [(p, t) for t in range(2 * cube.nb) for p in range(len(pieces))]
    slots = {}
    for n, item in enumerate(sequence):
        slots.setdefault(min(steps - 1, 2 + n * (steps - 4) // len(sequence)), []).append(item)

    def step(n, carry):
        m, g = n // groups, lax.rem(n, groups)
        i = jnp.int32(0)
        for b in range(1, blocks):
            i = i + jnp.where(m >= b * (b + 1) // 2, 1, 0)
        j = m - i * (i + 1) // 2

        @pl.when(jnp.logical_and(g == 0, j == 0))
        def _():
            prepare(i)

        @pl.when(g == 0)
        def _():
            make_mask(i, j)

        here, there = at_block(i), at_block(j)
        first = g * hb
        qlanes = pl.ds(pl.multiple_of(first // 8 * 128, 128), 128)
        q = q_ref[here, qlanes]
        k = k_ref[there, qlanes]
        mask = mask_ref[...]
        gq = jnp.zeros((BT, 128), F32)
        for a in range(hb):
            h = first + a
            own_lanes = lane // QK == lax.rem(h, 8)
            vl = pl.ds(pl.multiple_of(h // 2 * 128, 128), 128)
            gn = jnp.where(lane // HV == a % 2, gn_ref[:, vl], jnp.zeros((BT, 128), BF16))
            gn = jnp.where(lane == HV * (1 - a % 2), gd_ref[:, vl], gn)
            v = v_ref[there, vl]
            v = jnp.where(lane // HV == a % 2, v, jnp.ones_like(v))
            t1 = nt(jnp.where(own_lanes, q, jnp.zeros_like(q)), k) + 1.0
            p = (t1 * t1 + 1.0).astype(BF16) * mask
            dp = nt(gn, v).astype(BF16) * mask
            gs = (dp.astype(F32) * t1).astype(BF16)
            gq = gq + nn(gs, jnp.where(own_lanes, k, jnp.zeros_like(k)))
            qrows = pl.ds(pl.multiple_of(h * QK, QK), QK)
            vrows = pl.ds(pl.multiple_of(h * HV, HV), HV)
            gkt_ref[qrows, there] += nn(qt_ref[qrows, :], gs)
            gvt_ref[vrows, there] += nn(gnt_ref[vrows, :], p)
        gq_ref[:, qlanes] += gq

        @pl.when(jnp.logical_and(g == groups - 1, j == i))
        def _():
            gp_ref[here, : HEADS * QK] = (gq_ref[...] * 0.25).astype(BF16)

        line.serve(n)
        for slot, items in slots.items():
            @pl.when(n == slot)
            def _():
                for p, t in items:
                    cube.advance(p, t)
        return carry

    lax.fori_loop(0, steps, step, 0)
    gp_ref[:, HEADS * QK :] = gkt_ref[...].T.astype(BF16)

    def turn(m, carry):
        vl = pl.ds(pl.multiple_of(m * 128, 128), 128)
        gv_ref[:, vl] = (gvt_ref[vl, :] * 0.5).T.astype(BF16)
        return carry

    lax.fori_loop(0, HEADS // 2, turn, 0)
    for n in range(steps, line.steps()):
        line.serve(jnp.int32(n))
    each(line.arrived, line.count)
    each(line.drain, line.count)
    for p in range(len(pieces)):
        cube.drain(p)


def greet(line, cube):
    sem = pltpu.get_barrier_semaphore()
    f = lax.axis_index("feat")
    count = jnp.int32(0)
    if cube is not None:
        for bit in cube.bits:
            pl.semaphore_signal(sem, inc=1, device_id=(cube.partner(bit), f), device_id_type=MESH)
        count = count + len(cube.bits)
    if line is not None:
        @pl.when(f > 0)
        def _():
            pl.semaphore_signal(sem, inc=1, device_id=(line.dp, f - 1), device_id_type=MESH)

        @pl.when(f < 3)
        def _():
            pl.semaphore_signal(sem, inc=1, device_id=(line.dp, f + 1), device_id_type=MESH)
        count = count + jnp.where(f > 0, 1, 0) + jnp.where(f < 3, 1, 0)
    pl.semaphore_wait(sem, count)


def each(act, n):
    def body(c, carry):
        act(c)
        return carry

    lax.fori_loop(0, n, body, 0)


def cube_shape(rows, dp_size, count):
    unit = 16 * dp_size
    padded = (rows + unit - 1) // unit * unit
    bits = tuple(2**n for n in range(dp_size.bit_length() - 1))
    return padded, split_rows(padded, unit, count), bits


def mixer_back(starts, pairs, v, attn, rd, ga, wide, ffn, grads, pieces, bits):
    length = v.shape[0]
    nq, nv, hb, rows = HEADS * QK, HEADS * HV, 4, 32
    count = length // rows
    hbm = pl.BlockSpec(memory_space=pl.ANY)
    vmem = pl.BlockSpec(memory_space=pltpu.VMEM)
    return pl.pallas_call(
        functools.partial(mixer_back_kernel, pieces, bits, hb, rows),
        out_shape=(
            jax.ShapeDtypeStruct((length, 2 * nq), BF16),
            jax.ShapeDtypeStruct((length, nv), BF16),
            jax.ShapeDtypeStruct((length, D), BF16),
            jax.ShapeDtypeStruct(grads.shape, BF16),
        ),
        in_specs=[pl.BlockSpec(memory_space=pltpu.SMEM)] + [hbm] * 8,
        out_specs=(vmem,) * 4,
        scratch_shapes=[
            pltpu.VMEM((length, nq), BF16), pltpu.VMEM((length, nq), BF16), pltpu.VMEM((length, nv), BF16),
            pltpu.VMEM((length, nv), BF16), pltpu.VMEM((length, nv), F32), pltpu.VMEM((length, D), BF16),
            pltpu.VMEM((D, nv), BF16),
            pltpu.VMEM((length, D), BF16), pltpu.VMEM((length, D), BF16), pltpu.VMEM((length, D), BF16),
            pltpu.VMEM(grads.shape, BF16), pltpu.VMEM(grads.shape, BF16),
            pltpu.VMEM((BT, BT), BF16), pltpu.VMEM((BT, nv), BF16), pltpu.VMEM((BT, nv), BF16),
            pltpu.VMEM((nq, BT), BF16), pltpu.VMEM((nv, BT), BF16), pltpu.VMEM((BT, nq), F32),
            pltpu.VMEM((nq, length), F32), pltpu.VMEM((nv, length), F32),
            pltpu.SemaphoreType.DMA((2, count)), pltpu.SemaphoreType.DMA((3, count)),
            pltpu.SemaphoreType.DMA((len(pieces), 2, 2 * len(bits))), pltpu.SemaphoreType.DMA((len(pieces), 2, 2 * len(bits))),
            pltpu.SemaphoreType.DMA((9,)),
        ],
        compiler_params=pltpu.CompilerParams(collective_id=4, has_side_effects=True, vmem_limit_bytes=60 * 2**20),
        name="mixer_back",
    )(starts, pairs, v, attn, rd, ga, wide, ffn, grads)


def project_back_kernel(
    pieces, bits, gp_ref, gv_ref, normed_ref, wide_ref, tokens_ref,
    gn_ref, sums_ref, work, landing, gain_ref, send, recv,
):
    f = lax.axis_index("feat")
    cube = CubeSum(work, landing, sums_ref, send, recv, pieces, bits)
    length = gp_ref.shape[0]
    pair_cols, value_cols = 2 * HEADS * QK // 4, HEADS * HV // 4
    own_values = own_column(gv_ref, f, value_cols).T
    work[0:value_cols, :] = nn(own_values, normed_ref[...]).astype(BF16)
    greet(None, cube)
    cube.launch(0)
    own_pairs = own_column(gp_ref, f, pair_cols).T
    work[value_cols : value_cols + pair_cols, :] = nn(own_pairs, normed_ref[...]).astype(BF16)
    gain_ref[...] = jnp.zeros_like(gain_ref)

    def rows(n, carry):
        at = pl.ds(pl.multiple_of(n * BT, BT), BT)
        grad = nt(gp_ref[at, :], wide_ref[:, : gp_ref.shape[1]]) + nt(
            gv_ref[at, :], wide_ref[:, gp_ref.shape[1] : gp_ref.shape[1] + gv_ref.shape[1]]
        )
        gn_ref[at, :] = grad.astype(BF16)
        x = tokens_ref[at, :].astype(F32)
        scale = lax.rsqrt(jnp.mean(x * x, axis=1, keepdims=True) + EPS)
        gain_ref[0:1, :] += jnp.sum(grad * (x * scale), axis=0, keepdims=True)
        return carry

    lax.fori_loop(0, length // BT, rows, 0)
    rest = value_cols + pair_cols
    work[rest:, :] = jnp.zeros((work.shape[0] - rest, D), BF16)
    work[rest : rest + 16, :] = gain_ref[...].astype(BF16)
    for p in range(1, len(pieces)):
        cube.launch(p)
    for t in range(2 * cube.nb):
        for p in range(len(pieces)):
            cube.advance(p, t)
    for p in range(len(pieces)):
        cube.drain(p)


def project_back(gp, gv, normed, wide, tokens, dp_size):
    length = gp.shape[0]
    padded, _, bits = cube_shape(gv.shape[1] // 4 + gp.shape[1] // 4 + 16, dp_size, 1)
    unit = 16 * dp_size
    first = gv.shape[1] // 4 // unit * unit
    pieces = [(0, first), (first, padded - first)] if first else [(0, padded)]
    vmem = pl.BlockSpec(memory_space=pltpu.VMEM)
    return pl.pallas_call(
        functools.partial(project_back_kernel, pieces, bits),
        out_shape=(jax.ShapeDtypeStruct((length, D), BF16), jax.ShapeDtypeStruct((padded, D), BF16)),
        in_specs=[vmem] * 5,
        out_specs=(vmem,) * 2,
        scratch_shapes=[
            pltpu.VMEM((padded, D), BF16), pltpu.VMEM((padded, D), BF16), pltpu.VMEM((16, D), F32),
            pltpu.SemaphoreType.DMA((len(pieces), 2, 2 * len(bits))), pltpu.SemaphoreType.DMA((len(pieces), 2, 2 * len(bits))),
        ],
        compiler_params=pltpu.CompilerParams(collective_id=5, has_side_effects=True, vmem_limit_bytes=50 * 2**20),
        name="project_back",
    )(gp, gv, normed, wide, tokens)


def update_kernel(
    rates,
    down_w, down_m, down_a, gate_w, gate_m, gate_a, out_w, out_m, out_a, value_w, value_m, value_a,
    pair_w, pair_m, pair_a, gain_w, gain_m, gain_a, big, small, hidden, total, grad_hidden, grad_normed, tokens, gains,
    mixed_o, input_o, pair_mo, pair_wo, pair_ao, value_mo, value_wo, value_ao, out_mo, out_wo, out_ao,
    gate_mo, gate_wo, gate_ao, down_mo, down_wo, down_ao, gain_mo, gain_wo, gain_ao,
):
    ff = down_w.shape[0]
    narrow = value_w.shape[1]
    pair_cols = pair_w.shape[1]

    def put(index, outs, grad, w, m, a, rate):
        moment_next, weight_next, average_next = update(w[index], grad, m[index], a[index], rate)
        outs[0][index], outs[1][index], outs[2][index] = moment_next, weight_next, average_next

    put(..., (down_mo, down_wo, down_ao), big[:ff, :].astype(F32), down_w, down_m, down_a, rates[4])
    for n in range(2):
        first = (n + 1) * ff
        put(n, (gate_mo, gate_wo, gate_ao), big[first : first + ff, :].astype(F32), gate_w, gate_m, gate_a, rates[3])
    first = 3 * ff
    put(..., (out_mo, out_wo, out_ao), big[first : first + out_w.shape[0], :].astype(F32), out_w, out_m, out_a, rates[2])
    first = first + out_w.shape[0]
    put(..., (value_mo, value_wo, value_ao), small[:narrow, :].astype(F32).T, value_w, value_m, value_a, rates[1])
    put(..., (pair_mo, pair_wo, pair_ao), small[narrow : narrow + pair_cols, :].astype(F32).T, pair_w, pair_m, pair_a, rates[0])
    gain_one = small[narrow + pair_cols : narrow + pair_cols + 16, :].astype(F32)[0:1, :]
    gain_two = big[first : first + 16, :].astype(F32)[0:1, :]
    put(slice(0, 1), (gain_mo, gain_wo, gain_ao), gain_one, gain_w, gain_m, gain_a, rates[5])
    put(slice(1, 2), (gain_mo, gain_wo, gain_ao), gain_two, gain_w, gain_m, gain_a, rates[5])

    mixed_o[...] = (hidden[...] + total[...].astype(F32)).astype(BF16)
    x = tokens[...].astype(F32)
    scale = lax.rsqrt(jnp.mean(x * x, axis=1, keepdims=True) + EPS)
    unit = x * scale
    u = grad_normed[...].astype(F32) * gains[0:1, :]
    input_o[...] = grad_hidden[...] + scale * (u - unit * jnp.mean(u * unit, axis=1, keepdims=True))


def finish(rates, weights, big, small, hidden, total, grad_hidden, grad_normed, tokens, gains):
    length = tokens.shape[0]
    steps = D // 128
    rows = length // steps
    ff = weights[0][0].shape[0]
    narrow, pair_cols = weights[3][0].shape[1], weights[4][0].shape[1]

    def cols(n):
        return pl.BlockSpec((n, 128), lambda i: (0, i))

    def tall(n):
        return pl.BlockSpec((128, n), lambda i: (i, 0))

    token = pl.BlockSpec((rows, D), lambda i: (i, 0))
    specs = [cols(ff), pl.BlockSpec((2, ff, 128), lambda i: (0, 0, i)), cols(weights[2][0].shape[0]), tall(narrow), tall(pair_cols), cols(2)]
    order = [4, 3, 2, 1, 0, 5]
    flat = [a for group in weights for a in group]
    out_shape = [jax.ShapeDtypeStruct((length, D), BF16), jax.ShapeDtypeStruct((length, D), F32)]
    out_specs = [token, token]
    for n in order:
        out_shape += [jax.ShapeDtypeStruct(weights[n][0].shape, F32)] * 3
        out_specs += [specs[n]] * 3
    in_specs = [specs[n] for n in range(6) for _ in range(3)]
    in_specs += [cols(big.shape[0]), cols(small.shape[0])] + [token] * 5 + [pl.BlockSpec((2, D), lambda i: (0, 0))]
    return pl.pallas_call(
        functools.partial(update_kernel, rates),
        grid=(steps,),
        out_shape=out_shape,
        in_specs=in_specs,
        out_specs=out_specs,
        compiler_params=pltpu.CompilerParams(vmem_limit_bytes=50 * 2**20),
        name="finish",
    )(*flat, big, small, hidden, total, grad_hidden, grad_normed, tokens, gains)


def update(weight, grad_total, moment, average, rate):
    moment_next = MOMENTUM * moment + grad_total
    weight_next = weight - rate * (grad_total + MOMENTUM * moment_next)
    average_next = average + (weight_next - average) / STEP
    return (moment_next, weight_next, average_next)


def on_device(
    tokens,
    cotangent,
    doc_starts,
    queries_keys,
    value_weight,
    out_weight,
    gate_up,
    down_weight,
    norm_gains,
    queries_moment,
    value_moment,
    out_moment,
    gate_moment,
    down_moment,
    gains_moment,
    queries_average,
    value_average,
    out_average,
    gate_average,
    down_average,
    gains_average,
):
    total_tokens = float(tokens.shape[0] * lax.axis_size("dp"))
    dp_size = lax.axis_size("dp")
    ff = down_weight.shape[0]
    gate_turned = gate_up.transpose(0, 2, 1)
    normed_one, pairs, values, wide, gate_low, down_low = project(
        tokens, norm_gains, queries_keys, value_weight, out_weight, gate_turned, down_weight
    )
    attn_low, recip = attn_fwd(doc_starts, pairs, values, 8)
    padded, pieces, bits = cube_shape(3 * ff + out_weight.shape[0] + 16, dp_size, 4)
    hidden_one, grad_hidden, grad_attended, ffn_part, big = feed(
        tokens, cotangent, attn_low, wide, gate_low, down_low, norm_gains, padded
    )
    grad_pairs, grad_values, total, big = mixer_back(
        doc_starts, pairs, values, attn_low, recip, grad_attended, wide, ffn_part, big, pieces, bits
    )
    grad_normed_one, small = project_back(grad_pairs, grad_values, normed_one, wide, tokens, dp_size)
    rates = (
        (D * total_tokens) ** (-0.5),
        (D * total_tokens) ** (-0.5),
        (HEADS * HV * total_tokens) ** (-0.5),
        (D * total_tokens) ** (-0.5),
        (FF * total_tokens) ** (-0.5),
        0.2 * total_tokens ** (-0.5),
    )
    weights = (
        (down_weight, down_moment, down_average),
        (gate_turned, gate_moment.transpose(0, 2, 1), gate_average.transpose(0, 2, 1)),
        (out_weight, out_moment, out_average),
        (value_weight, value_moment, value_average),
        (queries_keys, queries_moment, queries_average),
        (norm_gains, gains_moment, gains_average),
    )
    outs = list(finish(rates, weights, big, small, hidden_one, total, grad_hidden, grad_normed_one, tokens, norm_gains))
    outs[11:14] = [o.transpose(0, 2, 1) for o in outs[11:14]]
    return tuple(outs)


def solution(mesh):
    in_specs = (
        P("dp", None),
        P("dp", None),
        P("dp", None),
        P(None, "feat"),
        P(None, "feat"),
        P("feat", None),
        P(None, None, "feat"),
        P("feat", None),
        P(),
        P(None, "feat"),
        P(None, "feat"),
        P("feat", None),
        P(None, None, "feat"),
        P("feat", None),
        P(),
        P(None, "feat"),
        P(None, "feat"),
        P("feat", None),
        P(None, None, "feat"),
        P("feat", None),
        P(),
    )
    out_specs = (
        P("dp", None),
        P("dp", None),
        P(None, "feat"),
        P(None, "feat"),
        P(None, "feat"),
        P(None, "feat"),
        P(None, "feat"),
        P(None, "feat"),
        P("feat", None),
        P("feat", None),
        P("feat", None),
        P(None, None, "feat"),
        P(None, None, "feat"),
        P(None, None, "feat"),
        P("feat", None),
        P("feat", None),
        P("feat", None),
        P(),
        P(),
        P(),
    )
    return jax.shard_map(
        on_device, mesh=mesh, in_specs=in_specs, out_specs=out_specs, check_vma=False
    )
```

```python
import functools
import jax
import jax.numpy as jnp
from jax import lax
from jax.experimental import pallas as pl
from jax.experimental.pallas import tpu as pltpu
from jax.sharding import PartitionSpec as P

D = 1024
HEADS = 16
QK = 16
HV = 64
FF = 2752
STEP = 4
BT = 256
F32 = jnp.float32
BF16 = jnp.bfloat16

MESH = pl.DeviceIdType.MESH
EPS = 1e-06
MOMENTUM = 0.9


def nt(a, b):
    return lax.dot_general(a, b, (((1,), (1,)), ((), ())), preferred_element_type=F32)


def nn(a, b):
    return lax.dot_general(a, b, (((1,), (0,)), ((), ())), preferred_element_type=F32)


class LineSum:
    def __init__(self, part, leaf, mid, total, send, recv, rows, lags=(0, 2, 4)):
        self.part, self.leaf, self.mid, self.total, self.send, self.recv = part, leaf, mid, total, send, recv
        self.rows, self.lags = rows, lags
        self.count = part.shape[0] // rows
        self.dp, self.f = lax.axis_index("dp"), lax.axis_index("feat")

    def barrier(self):
        sem = pltpu.get_barrier_semaphore()
        dp, f = self.dp, self.f

        @pl.when(f > 0)
        def _():
            pl.semaphore_signal(sem, inc=1, device_id=(dp, f - 1), device_id_type=MESH)

        @pl.when(f < 3)
        def _():
            pl.semaphore_signal(sem, inc=1, device_id=(dp, f + 1), device_id_type=MESH)
        pl.semaphore_wait(sem, jnp.where(f > 0, 1, 0) + jnp.where(f < 3, 1, 0))

    def place(self, c):
        odd = lax.rem(c, 2)
        return self.f + odd * (3 - 2 * self.f), 1 - 2 * odd

    def copy(self, c, src, dst, kind, slot, to):
        at = pl.ds(pl.multiple_of(c * self.rows, self.rows), self.rows)
        return pltpu.make_async_remote_copy(
            src_ref=src.at[at], dst_ref=dst.at[at], send_sem=self.send.at[slot, c], recv_sem=self.recv.at[kind, c],
            device_id=(self.dp, to), device_id_type=MESH)

    def leaves(self, c):
        p, up = self.place(c)

        @pl.when(p == 3)
        def _():
            self.copy(c, self.part, self.leaf, 0, 0, self.f - up).start()

        @pl.when(p == 0)
        def _():
            self.copy(c, self.part, self.leaf, 0, 0, self.f + up).start()

    def middle(self, c):
        p, up = self.place(c)
        at = pl.ds(pl.multiple_of(c * self.rows, self.rows), self.rows)

        @pl.when(p == 2)
        def _():
            self.copy(c, self.part, self.leaf, 0, 0, self.f).wait_recv()
            self.part[at, :] = (self.part[at, :].astype(F32) + self.leaf[at, :].astype(F32)).astype(BF16)
            self.copy(c, self.part, self.mid, 1, 0, self.f - up).start()

    def root(self, c):
        p, up = self.place(c)
        at = pl.ds(pl.multiple_of(c * self.rows, self.rows), self.rows)

        @pl.when(p == 1)
        def _():
            self.copy(c, self.part, self.leaf, 0, 0, self.f).wait_recv()
            self.copy(c, self.part, self.mid, 1, 0, self.f).wait_recv()
            self.total[at, :] = (
                self.part[at, :].astype(F32) + self.leaf[at, :].astype(F32) + self.mid[at, :].astype(F32)
            ).astype(BF16)
            self.copy(c, self.total, self.total, 2, 1, self.f + up).start()
            self.copy(c, self.total, self.total, 2, 0, self.f - up).start()

    def onward(self, c):
        p, up = self.place(c)

        @pl.when(p == 2)
        def _():
            self.copy(c, self.total, self.total, 2, 0, self.f).wait_recv()
            self.copy(c, self.total, self.total, 2, 1, self.f + up).start()

    def serve(self, i):
        for lag, act in zip(self.lags, (self.middle, self.root, self.onward)):
            c = i - lag

            @pl.when(jnp.logical_and(c >= 0, c < self.count))
            def _():
                act(c)

    def steps(self):
        return self.count + self.lags[-1]

    def arrived(self, c):
        p, up = self.place(c)

        @pl.when(jnp.logical_or(p == 0, p == 3))
        def _():
            self.copy(c, self.total, self.total, 2, 0, self.f).wait_recv()

    def drain(self, c):
        p, up = self.place(c)
        self.copy(c, self.part, self.part, 0, 0, self.f).wait_send()

        @pl.when(jnp.logical_or(p == 1, p == 2))
        def _():
            self.copy(c, self.part, self.part, 0, 1, self.f).wait_send()


class CubeSum:
    def __init__(self, work, recv, out, send_sem, recv_sem, pieces, bits):
        self.work, self.recv, self.out, self.send_sem, self.recv_sem = work, recv, out, send_sem, recv_sem
        self.pieces, self.nb = pieces, len(bits)
        self.dp, self.f = lax.axis_index("dp"), lax.axis_index("feat")
        self.orders = [list(bits), [bits[0]] + list(bits[1:])[::-1]]
        self.bits = bits

    def partner(self, bit):
        return self.dp + bit - 2 * bit * lax.rem(self.dp // bit, 2)

    def barrier(self):
        sem = pltpu.get_barrier_semaphore()
        for bit in self.bits:
            pl.semaphore_signal(sem, inc=1, device_id=(self.partner(bit), self.f), device_id_type=MESH)
        pl.semaphore_wait(sem, len(self.bits))

    def lanes(self, colour):
        half = self.work.shape[1] // 2
        return pl.ds(colour * half, half)

    def segment(self, piece, colour, k):
        first, rows = self.pieces[piece]
        start = first
        for bit in self.orders[colour][:k]:
            rows = rows // 2
            start = start + rows * lax.rem(self.dp // bit, 2)
        return start, rows

    def at(self, start, rows):
        return pl.ds(pl.multiple_of(start, 16), rows)

    def halve(self, piece, colour, k):
        start, rows = self.segment(piece, colour, k)
        rows = rows // 2
        bit = self.orders[colour][k]
        own = lax.rem(self.dp // bit, 2)
        first, whole = self.pieces[piece]
        landing = first + whole - 2 * rows
        return pltpu.make_async_remote_copy(
            src_ref=self.work.at[self.at(start + rows * (1 - own), rows), self.lanes(colour)],
            dst_ref=self.recv.at[self.at(landing, rows), self.lanes(colour)],
            send_sem=self.send_sem.at[piece, colour, k], recv_sem=self.recv_sem.at[piece, colour, k],
            device_id=(self.partner(bit), self.f), device_id_type=MESH)

    def add(self, piece, colour, k):
        start, rows = self.segment(piece, colour, k + 1)
        first, whole = self.pieces[piece]
        landing = first + whole - 2 * rows
        target = self.out if k + 1 == self.nb else self.work
        mine = self.work[self.at(start, rows), self.lanes(colour)].astype(F32)
        target[self.at(start, rows), self.lanes(colour)] = (
            mine + self.recv[self.at(landing, rows), self.lanes(colour)].astype(F32)
        ).astype(BF16)

    def double(self, piece, colour, k):
        start, rows = self.segment(piece, colour, k + 1)
        bit = self.orders[colour][k]
        at = self.at(start, rows)
        slot = 2 * self.nb - 1 - k
        return pltpu.make_async_remote_copy(
            src_ref=self.out.at[at, self.lanes(colour)], dst_ref=self.out.at[at, self.lanes(colour)],
            send_sem=self.send_sem.at[piece, colour, slot], recv_sem=self.recv_sem.at[piece, colour, slot],
            device_id=(self.partner(bit), self.f), device_id_type=MESH)

    def launch(self, piece):
        for colour in range(2):
            self.halve(piece, colour, 0).start()

    def advance(self, piece, t):
        for colour in range(2):
            if t < self.nb:
                self.halve(piece, colour, t).wait_recv()
                self.add(piece, colour, t)
                if t + 1 < self.nb:
                    self.halve(piece, colour, t + 1).start()
                else:
                    self.double(piece, colour, self.nb - 1).start()
            else:
                k = 2 * self.nb - 1 - t
                self.double(piece, colour, k).wait_recv()
                if k > 0:
                    self.double(piece, colour, k - 1).start()

    def drain(self, piece):
        for colour in range(2):
            for k in range(self.nb):
                self.halve(piece, colour, k).wait_send()
                self.double(piece, colour, k).wait_send()


def split_rows(rows, unit, count):
    units = rows // unit
    out, first = [], 0
    for n in range(count):
        take = (units * (n + 1) // count - units * n // count) * unit
        out.append((first, take))
        first += take
    return [p for p in out if p[1]]


def own_column(ref, f, width):
    return ref[:, pl.ds(pl.multiple_of(f * width, width), width)]


def greet(line, cube):
    sem = pltpu.get_barrier_semaphore()
    f = lax.axis_index("feat")
    count = jnp.int32(0)
    if cube is not None:
        for bit in cube.bits:
            pl.semaphore_signal(sem, inc=1, device_id=(cube.partner(bit), f), device_id_type=MESH)
        count = count + len(cube.bits)
    if line is not None:
        @pl.when(f > 0)
        def _():
            pl.semaphore_signal(sem, inc=1, device_id=(line.dp, f - 1), device_id_type=MESH)

        @pl.when(f < 3)
        def _():
            pl.semaphore_signal(sem, inc=1, device_id=(line.dp, f + 1), device_id_type=MESH)
        count = count + jnp.where(f > 0, 1, 0) + jnp.where(f < 3, 1, 0)
    pl.semaphore_wait(sem, count)


def each(act, n):
    def body(c, carry):
        act(c)
        return carry

    lax.fori_loop(0, n, body, 0)


def cube_shape(rows, dp_size, count):
    unit = 16 * dp_size
    padded = (rows + unit - 1) // unit * unit
    bits = tuple(2**n for n in range(dp_size.bit_length() - 1))
    return padded, split_rows(padded, unit, count), bits


def front_kernel(
    bits, starts_ref, tokens_in, gains_ref, pair_ref, value_ref, out_ref, gate_in, down_in,
    normed_out, pairs_out, values_out, wide_out, gate_out, down_out, attn_out, recip_out, mask_out,
    thin_ref, thick_ref, tokens_ref, gate_f32, down_f32,
    normed_ref, pairs_ref, values_ref, wide_ref, gate_ref, down_ref, attn_ref, recip_ref, mask_ref, acc_ref,
    send_sem, recv_sem, load_sem, store_sem,
):
    dp = lax.axis_index("dp")
    f = lax.axis_index("feat")
    slices = lax.axis_size("feat")
    last = slices - 1
    pieces = 2 ** len(bits)
    j = lax.rem(dp, pieces)
    base = dp - j
    pair_cols, value_cols = pair_ref.shape[1], value_ref.shape[1]
    pairs_wide, values_wide = slices * pair_cols, slices * value_cols
    rows = pair_ref.shape[0] // pieces
    length = tokens_ref.shape[0]
    blocks = length // BT
    loads = [
        pltpu.make_async_copy(a, b, load_sem.at[n])
        for n, (a, b) in enumerate([(tokens_in, tokens_ref), (gate_in, gate_f32), (down_in, down_f32)])
    ]
    for load in loads:
        load.start()

    def flip(k, bit):
        return k + bit - 2 * bit * lax.rem(k // bit, 2)

    def cast(k):
        at = pl.ds(pl.multiple_of(k * rows, rows), rows)
        pair = pair_ref[at, :].astype(BF16)
        thick = jnp.concatenate([value_ref[at, :].astype(BF16), out_ref[:, at].T.astype(BF16)], axis=1)
        for colour in range(2):
            part = slice(colour * rows // 2, (colour + 1) * rows // 2)
            thin_ref[f, k, colour] = pair[part]
            thick_ref[f, k, colour] = thick[part]

    cast(j)
    barrier = pltpu.get_barrier_semaphore()
    for bit in bits:
        pl.semaphore_signal(barrier, inc=1, device_id=(base + flip(j, bit), f), device_id_type=MESH)

    @pl.when(f > 0)
    def _():
        pl.semaphore_signal(barrier, inc=1, device_id=(dp, f - 1), device_id_type=MESH)

    @pl.when(f < last)
    def _():
        pl.semaphore_signal(barrier, inc=1, device_id=(dp, f + 1), device_id_type=MESH)

    pl.semaphore_wait(barrier, len(bits) + jnp.where(f > 0, 1, 0) + jnp.where(f < last, 1, 0))

    def copy(wave, z, colour, k, slot, device):
        ref = (thin_ref, thick_ref)[wave]
        return pltpu.make_async_remote_copy(
            src_ref=ref.at[z, k, colour], dst_ref=ref.at[z, k, colour], send_sem=send_sem.at[wave, z, colour, slot],
            recv_sem=recv_sem.at[wave, z, colour, k], device_id=device, device_id_type=MESH,
        )

    here = (dp, f)
    for wave in range(2):
        for colour in range(2):
            @pl.when(f > 0)
            def _():
                copy(wave, f, colour, j, 0, (dp, f - 1)).start()

            @pl.when(f < last)
            def _():
                copy(wave, f, colour, j, 1, (dp, f + 1)).start()

    order = [
        jnp.where(f == 0, 1, f - 1),
        jnp.where(f < 2, 2, jnp.where(f == 2, 3, 1)),
        jnp.where(f < 2, 3, 0),
    ]
    colour_bits = [list(bits[1:]) + [bits[0]], list(bits[1:])[::-1] + [bits[0]]]

    def held(colour, step):
        out = [j]
        for bit in colour_bits[colour][:step]:
            out = out + [flip(k, bit) for k in out]
        return out

    def start_step(wave, z, step):
        for colour in range(2):
            first = 2 + 2**step - 1
            partner = (base + flip(j, colour_bits[colour][step]), f)
            for n, k in enumerate(held(colour, step)):
                copy(wave, z, colour, k, first + n, partner).start()

    def step(wave, a, n):
        z = order[a]
        for colour in range(2):
            for k in held(colour, n):
                copy(wave, z, colour, flip(k, colour_bits[colour][n]), 0, here).wait_recv()
        if n + 1 < len(bits):
            start_step(wave, z, n + 1)

    def arrive(wave, a):
        z = order[a]
        ahead = jnp.where(z < f, f + 1, f - 1)
        onward = jnp.logical_and(ahead >= 0, ahead <= last)
        for colour in range(2):
            copy(wave, z, colour, j, 0, here).wait_recv()

            @pl.when(onward)
            def _():
                copy(wave, z, colour, j, jnp.where(z < f, 1, 0), (dp, ahead)).start()
        start_step(wave, z, 0)

    def put_thin(z):
        at = pl.ds(pl.multiple_of(z * pair_cols, pair_cols), pair_cols)
        wide_ref[:, at] = thin_ref[z].reshape(pieces * rows, pair_cols)

    def lanes(first, z):
        return pl.ds(pl.multiple_of(first + z * value_cols, 128), value_cols)

    def store(n, source, target, at=None):
        if at is not None:
            source, target = source.at[:, at], target.at[:, at]
        return pltpu.make_async_copy(source, target, store_sem.at[n])

    def use(a, z):
        weight = thick_ref[z].reshape(pieces * rows, 2 * value_cols)
        wide_ref[:, lanes(pairs_wide, z)] = weight[:, :value_cols]
        wide_ref[:, lanes(pairs_wide + values_wide, z)] = weight[:, value_cols:]

        def some(n, carry):
            at = pl.ds(pl.multiple_of(n * BT, BT), BT)
            values_ref[at, lanes(0, z)] = nn(normed_ref[at, :], wide_ref[:, lanes(pairs_wide, z)]).astype(BF16)
            return carry

        lax.fori_loop(0, blocks, some, 0)
        store(6 + a, wide_ref, wide_out, lanes(pairs_wide, z)).start()
        store(10 + a, wide_ref, wide_out, lanes(pairs_wide + values_wide, z)).start()
        store(14 + a, values_ref, values_out, lanes(0, z)).start()

    def cast_rest(n, carry):
        cast(lax.rem(j + n, pieces))
        return carry

    lax.fori_loop(1, pieces, cast_rest, 0)
    loads[0].wait()

    def norm(n, carry):
        at = pl.ds(pl.multiple_of(n * BT, BT), BT)
        x = tokens_ref[at, :].astype(F32)
        scale = lax.rsqrt(jnp.mean(x * x, axis=1, keepdims=True) + EPS)
        normed_ref[at, :] = (x * scale * gains_ref[0:1, :]).astype(BF16)
        return carry

    lax.fori_loop(0, blocks, norm, 0)
    store(0, normed_ref, normed_out).start()
    arrive(0, 0)
    put_thin(f)
    use(0, f)
    arrive(0, 1)
    step(0, 0, 0)
    arrive(0, 2)
    step(0, 1, 0)

    begin = jnp.zeros((length, 1), jnp.int32)
    position = lax.broadcasted_iota(jnp.int32, (length, 1), 0)
    for n in range(starts_ref.shape[1]):
        begin = jnp.where(starts_ref[0, n] <= position, jnp.maximum(begin, starts_ref[0, n]), begin)
    for n in range(blocks):
        rest = length - n * BT
        s = n * BT + lax.broadcasted_iota(jnp.int32, (rest, BT), 1)
        keep = jnp.logical_and(s <= position[n * BT :], s >= begin[n * BT :])
        mask_ref[n, :rest, :] = keep.astype(F32).astype(BF16)
        if n:
            mask_ref[n, rest:, :] = jnp.zeros((n * BT, BT), BF16)
    store(1, mask_ref, mask_out).start()
    step(0, 0, 1)
    step(0, 2, 0)
    step(0, 1, 1)
    arrive(1, 0)
    step(0, 0, 2)
    put_thin(order[0])
    step(0, 2, 1)

    def cast_all(source, target):
        def go(m, carry):
            at = pl.ds(pl.multiple_of(m * 16, 16), 16)
            target[at, :] = source[at, :].astype(BF16)
            return carry

        lax.fori_loop(0, source.shape[0] // 16, go, 0)

    loads[1].wait()
    loads[2].wait()
    cast_all(gate_f32.at[0], gate_ref.at[0])
    arrive(1, 1)
    step(1, 0, 0)
    cast_all(gate_f32.at[1], gate_ref.at[1])
    step(0, 1, 2)
    put_thin(order[1])
    step(0, 2, 2)
    put_thin(order[2])
    step(1, 0, 1)
    arrive(1, 2)
    step(1, 1, 0)
    cast_all(down_f32, down_ref)
    store(2, gate_ref, gate_out).start()
    store(3, down_ref, down_out).start()

    half = pairs_wide // 2

    def project_pairs(n, carry):
        at = pl.ds(pl.multiple_of(n * BT, BT), BT)
        pairs = nn(normed_ref[at, :], wide_ref[:, :pairs_wide]).astype(BF16)
        pairs_ref[at, :half] = pairs[:, :half] * jnp.bfloat16(0.25)
        pairs_ref[at, half:] = pairs[:, half:]
        return carry

    lax.fori_loop(0, blocks, project_pairs, 0)
    store(4, pairs_ref, pairs_out).start()
    store(5, wide_ref, wide_out, pl.ds(0, pairs_wide)).start()

    lane = lax.broadcasted_iota(jnp.int32, (1, 128), 1)
    events = {
        1: [(step, 1, 2, 0), (step, 1, 1, 1)],
        2: [(step, 1, 0, 2), (use, 1, order[0])],
        3: [(step, 1, 2, 1)],
        4: [(step, 1, 1, 2), (use, 2, order[1])],
        6: [(step, 1, 2, 2), (use, 3, order[2])],
    }

    def unit(n, carry):
        for at, acts in events.items():
            @pl.when(n == at)
            def _():
                for act in acts:
                    act[0](*act[1:])
        a = n // 2
        z = jnp.where(a == 0, f, jnp.where(a == 1, order[0], jnp.where(a == 2, order[1], order[2])))
        pair = 2 * z + lax.rem(n, 2)
        vl = pl.ds(pl.multiple_of(pair * 128, 128), 128)
        ql = pl.ds(pl.multiple_of(pair // 4 * 128, 128), 128)
        kl = pl.ds(pl.multiple_of(half + pair // 4 * 128, 128), 128)
        for block in range(blocks):
            first = block * BT
            below, there = pl.ds(first, length - first), pl.ds(first, BT)
            q, k, v = pairs_ref[below, ql], pairs_ref[there, kl], values_ref[there, vl]
            mask = mask_ref[block, : length - first, :]
            for m in range(2):
                own = lane // QK == lax.rem(2 * pair + m, 8)
                t1 = nt(q, jnp.where(own, k, jnp.zeros_like(k))) + 1.0
                p = (t1 * t1 + 1.0).astype(BF16) * mask
                out = nn(p, jnp.where(lane // HV == m, v, jnp.ones_like(v)))
                if block:
                    acc_ref[m, below, :] += out
                else:
                    acc_ref[m] = out
        one, two = acc_ref[0], acc_ref[1]
        numer = jnp.where(lane < HV, one, two)
        recip = 1.0 / pltpu.roll(jnp.where(lane < HV, two, one), HV, 1)
        attn_ref[:, vl] = (numer * recip).astype(BF16)
        recip_ref[:, vl] = recip
        store(18 + n, attn_ref, attn_out, vl).start()
        store(26 + n, recip_ref, recip_out, vl).start()
        return carry

    lax.fori_loop(0, 2 * slices, unit, 0)
    for wave in range(2):
        for z in order:
            ahead = jnp.where(z < f, f + 1, f - 1)
            onward = jnp.logical_and(ahead >= 0, ahead <= last)
            for colour in range(2):
                @pl.when(onward)
                def _():
                    copy(wave, z, colour, j, jnp.where(z < f, 1, 0), here).wait_send()

                for n in range(len(bits)):
                    for m, k in enumerate(held(colour, n)):
                        copy(wave, z, colour, k, 2 + 2**n - 1 + m, here).wait_send()
        for colour in range(2):
            @pl.when(f > 0)
            def _():
                copy(wave, f, colour, j, 0, here).wait_send()

            @pl.when(f < last)
            def _():
                copy(wave, f, colour, j, 1, here).wait_send()
    for n, (source, target) in enumerate([
        (normed_ref, normed_out), (mask_ref, mask_out), (gate_ref, gate_out), (down_ref, down_out), (pairs_ref, pairs_out),
    ]):
        store(n, source, target).wait()
    store(5, wide_ref, wide_out, pl.ds(0, pairs_wide)).wait()
    for a in range(slices):
        store(6 + a, wide_ref, wide_out, pl.ds(0, value_cols)).wait()
        store(10 + a, wide_ref, wide_out, pl.ds(0, value_cols)).wait()
        store(14 + a, values_ref, values_out, pl.ds(0, value_cols)).wait()
    for n in range(2 * slices):
        store(18 + n, attn_ref, attn_out, pl.ds(0, 128)).wait()
        store(26 + n, recip_ref, recip_out, pl.ds(0, 128)).wait()


def front(starts, tokens, gains, pair_w, value_w, out_w, gate_turned, down):
    length = tokens.shape[0]
    ff = down.shape[0]
    slices = 4
    pair_cols, value_cols = pair_w.shape[1], value_w.shape[1]
    bits = (1, 2, 4)
    hbm = pl.BlockSpec(memory_space=pl.ANY)
    vmem = pl.BlockSpec(memory_space=pltpu.VMEM)
    shapes = [
        ((length, D), BF16),
        ((length, slices * pair_cols), BF16),
        ((length, slices * value_cols), BF16),
        ((D, slices * (pair_cols + 2 * value_cols)), BF16),
        ((2, ff, D), BF16),
        ((ff, D), BF16),
        ((length, slices * value_cols), BF16),
        ((length, slices * value_cols), F32),
        ((length // BT, length, BT), BF16),
    ]
    return pl.pallas_call(
        functools.partial(front_kernel, bits),
        out_shape=tuple(jax.ShapeDtypeStruct(*s) for s in shapes),
        in_specs=[pl.BlockSpec(memory_space=pltpu.SMEM), hbm] + [vmem] * 4 + [hbm] * 2,
        out_specs=(hbm,) * 9,
        scratch_shapes=[
            pltpu.VMEM((slices, 8, 2, D // 16, pair_cols), BF16),
            pltpu.VMEM((slices, 8, 2, D // 16, 2 * value_cols), BF16),
            pltpu.VMEM((length, D), BF16),
            pltpu.VMEM((2, ff, D), F32),
            pltpu.VMEM((ff, D), F32),
        ]
        + [pltpu.VMEM(*s) for s in shapes]
        + [
            pltpu.VMEM((2, length, 128), F32),
            pltpu.SemaphoreType.DMA((2, slices, 2, 9)),
            pltpu.SemaphoreType.DMA((2, slices, 2, 8)),
            pltpu.SemaphoreType.DMA((3,)),
            pltpu.SemaphoreType.DMA((18 + 4 * slices,)),
        ],
        compiler_params=pltpu.CompilerParams(collective_id=1, has_side_effects=True, vmem_limit_bytes=60 * 2**20),
        name="front",
    )(starts, tokens, gains, pair_w, value_w, out_w, gate_turned, down)


def feed_kernel(
    rows, tokens_in, cot_in, attn_in, recip_in, wide_in, gate_in, down_in, gains_ref,
    hidden_out, grad_hidden_out, gn_out, gnt_out, gd_out, ffn_out, grads_out,
    tokens_ref, cot_ref, attn_ref, out_w, gate_ref, down_ref, recip_ref,
    hidden_ref, scale_ref, normed_ref, product_t, gate_t, up_t, own_t, gain_ref, ga_ref, gn_ref, gnt_ref, gd_ref, ffn_ref, grads_ref,
    part, leaf, mid, total, send, recv, load_sem, store_sem,
):
    f = lax.axis_index("feat")
    line = LineSum(part, leaf, mid, total, send, recv, rows, (0, 3, 6))
    length = tokens_ref.shape[0]
    ff = down_ref.shape[0]
    value_cols = own_t.shape[0]
    blocks = length // BT
    first_out = wide_in.shape[1] - attn_ref.shape[1]
    pairs = [(attn_in, attn_ref), (wide_in.at[:, pl.ds(first_out, attn_ref.shape[1])], out_w), (tokens_in, tokens_ref),
             (gate_in, gate_ref), (down_in, down_ref), (cot_in, cot_ref), (recip_in, recip_ref)]
    loads = [pltpu.make_async_copy(a, b, load_sem.at[n]) for n, (a, b) in enumerate(pairs)]
    for load in loads:
        load.start()
    greet(line, None)
    for load in loads[:-1]:
        load.wait()

    def store(source, target, n, kind):
        at = pl.ds(pl.multiple_of(n * BT, BT), BT)
        return pltpu.make_async_copy(source.at[at], target.at[at], store_sem.at[kind, n])

    def block(b, carry):
        at = pl.ds(pl.multiple_of(b * BT, BT), BT)
        turn = 4 * (b - 1)
        hidden = tokens_ref[at, :].astype(F32) + nt(attn_ref[at, :], out_w[...])
        hidden_ref[at, :] = hidden
        store(hidden_ref, hidden_out, b, 0).start()
        scale = lax.rsqrt(jnp.mean(hidden * hidden, axis=1, keepdims=True) + EPS)
        scale_ref[at, :] = jnp.broadcast_to(scale, (BT, 128))
        normed = (hidden * scale * gains_ref[1:2, :]).astype(BF16)
        normed_ref[at, :] = normed
        line.serve(turn)
        gate = nt(normed, gate_ref[0])
        up = nt(normed, gate_ref[1])
        line.serve(turn + 1)
        back = nt(cot_ref[at, :], down_ref[...])
        sig = 1.0 / (1.0 + jnp.exp(-gate))
        active = gate * sig
        slope = sig * (1.0 + gate * (1.0 - sig))
        product = (active * up).astype(BF16)
        grad_gate = (back * up * slope).astype(BF16)
        grad_up = (back * active).astype(BF16)
        line.serve(turn + 2)
        part[at, :] = (nn(grad_gate, gate_ref[0]) + nn(grad_up, gate_ref[1])).astype(BF16)

        def out(c, carry):
            line.leaves(b * (BT // rows) + c)
            return carry

        lax.fori_loop(0, BT // rows, out, 0)
        ffn_ref[at, :] = nn(product, down_ref[...]).astype(BF16)
        product_t[:, at] = product.T
        gate_t[:, at] = grad_gate.T
        up_t[:, at] = grad_up.T
        line.serve(turn + 3)
        return carry

    lax.fori_loop(0, blocks, block, 0)
    served = 4 * (blocks - 1)
    gain_ref[...] = jnp.zeros_like(gain_ref)
    chunks = []
    at = 0
    while at < ff:
        chunks.append((at, min(176, ff - at)))
        at += chunks[-1][1]
    for n, (turned, right) in enumerate([(product_t, cot_ref), (gate_t, normed_ref), (up_t, normed_ref)]):
        for first, size in chunks:
            at = slice(n * ff + first, n * ff + first + size)
            grads_ref[at, :] = nn(turned[first : first + size, :], right[...]).astype(BF16)
            line.serve(jnp.int32(served))
            served += 1
    ffn_store = pltpu.make_async_copy(ffn_ref, ffn_out, store_sem.at[0, blocks])
    ffn_store.start()
    grads_store = pltpu.make_async_copy(
        grads_ref.at[pl.ds(0, 3 * ff)], grads_out.at[pl.ds(0, 3 * ff)], store_sem.at[1, blocks]
    )
    grads_store.start()
    own_t[...] = own_column(attn_ref, f, value_cols).T
    loads[-1].wait()
    same = lax.broadcasted_iota(jnp.int32, (128, 128), 0) // HV == lax.broadcasted_iota(jnp.int32, (128, 128), 1) // HV
    negate = jnp.where(same, -1.0, 0.0).astype(BF16)

    def back_rows(n):
        at = pl.ds(pl.multiple_of(n * BT, BT), BT)
        hidden, grad = hidden_ref[at, :], total[at, :].astype(F32)
        scale = scale_ref[at, 0:1]
        unit = hidden * scale
        u = grad * gains_ref[1:2, :]
        gh = cot_ref[at, :].astype(F32) + scale * (u - unit * jnp.mean(u * unit, axis=1, keepdims=True))
        store(hidden_ref, hidden_out, n, 0).wait()
        hidden_ref[at, :] = gh
        store(hidden_ref, grad_hidden_out, n, 1).start()
        ga = gh.astype(BF16)
        ga_ref[at, :] = ga
        gain_ref[0:1, :] += jnp.sum(grad * unit, axis=0, keepdims=True)

        def pair(m, carry):
            wide = pl.ds(pl.multiple_of(m * 256, 256), 256)
            numer = nn(ga, out_w[:, wide]) * (2.0 * recip_ref[at, wide])
            low = numer.astype(BF16)
            both = (numer * attn_ref[at, wide].astype(F32)).astype(BF16)
            gn_ref[at, wide] = low
            gnt_ref[wide, at] = low.T
            gd_ref[at, wide] = jnp.concatenate([nn(both[:, :128], negate), nn(both[:, 128:], negate)], axis=1).astype(BF16)
            return carry

        lax.fori_loop(0, attn_ref.shape[1] // 256, pair, 0)
        store(gn_ref, gn_out, n, 2).start()
        store(gd_ref, gd_out, n, 3).start()
        turned_store(n).start()

    def turned_store(n):
        at = pl.ds(pl.multiple_of(n * BT, BT), BT)
        return pltpu.make_async_copy(gnt_ref.at[:, at], gnt_out.at[:, at], store_sem.at[4, n])

    per = BT // rows
    for n in range(blocks):
        until = min(per * (n + 1) + line.lags[-1], line.steps())

        def more(i, carry):
            line.serve(i)
            return carry

        lax.fori_loop(min(served, until), until, more, 0)
        served = max(served, until)
        lax.fori_loop(per * n, per * (n + 1), lambda c, carry: (line.arrived(c), carry)[1], 0)
        back_rows(jnp.int32(n))
    first = 3 * ff
    grads_ref[first : first + value_cols, :] = nn(own_t[...], ga_ref[...]).astype(BF16)
    first = first + value_cols
    rest = grads_ref.shape[0] - first
    grads_ref[first:, :] = jnp.zeros((rest, D), BF16)
    grads_ref[first : first + 16, :] = gain_ref[...].astype(BF16)
    each(line.drain, line.count)
    last = pl.ds(3 * ff, grads_ref.shape[0] - 3 * ff)
    last_store = pltpu.make_async_copy(grads_ref.at[last], grads_out.at[last], store_sem.at[2, blocks])
    last_store.start()
    for n in range(blocks):
        n = jnp.int32(n)
        store(hidden_ref, grad_hidden_out, n, 1).wait()
        store(gn_ref, gn_out, n, 2).wait()
        store(gd_ref, gd_out, n, 3).wait()
        turned_store(n).wait()
    ffn_store.wait()
    grads_store.wait()
    last_store.wait()


def feed(tokens, cotangent, attn, recip, wide, gate_turned, down, gains, padded):
    length = tokens.shape[0]
    ff = down.shape[0]
    nv, rows = attn.shape[1], 32
    count = length // rows
    hbm = pl.BlockSpec(memory_space=pl.ANY)
    vmem = pl.BlockSpec(memory_space=pltpu.VMEM)
    return pl.pallas_call(
        functools.partial(feed_kernel, rows),
        out_shape=(
            jax.ShapeDtypeStruct((length, D), F32),
            jax.ShapeDtypeStruct((length, D), F32),
            jax.ShapeDtypeStruct((length, nv), BF16),
            jax.ShapeDtypeStruct((nv, length), BF16),
            jax.ShapeDtypeStruct((length, nv), BF16),
            jax.ShapeDtypeStruct((length, D), BF16),
            jax.ShapeDtypeStruct((padded, D), BF16),
        ),
        in_specs=[hbm] * 7 + [vmem],
        out_specs=(hbm,) * 7,
        scratch_shapes=[
            pltpu.VMEM((length, D), BF16), pltpu.VMEM((length, D), BF16), pltpu.VMEM((length, nv), BF16),
            pltpu.VMEM((D, nv), BF16), pltpu.VMEM((2, ff, D), BF16), pltpu.VMEM((ff, D), BF16), pltpu.VMEM((length, nv), F32),
            pltpu.VMEM((length, D), F32), pltpu.VMEM((length, 128), F32), pltpu.VMEM((length, D), BF16),
            pltpu.VMEM((ff, length), BF16), pltpu.VMEM((ff, length), BF16), pltpu.VMEM((ff, length), BF16),
            pltpu.VMEM((nv // 4, length), BF16), pltpu.VMEM((16, D), F32), pltpu.VMEM((length, D), BF16),
            pltpu.VMEM((length, nv), BF16), pltpu.VMEM((nv, length), BF16), pltpu.VMEM((length, nv), BF16),
            pltpu.VMEM((length, D), BF16), pltpu.VMEM((padded, D), BF16),
            pltpu.VMEM((length, D), BF16), pltpu.VMEM((length, D), BF16), pltpu.VMEM((length, D), BF16),
            pltpu.VMEM((length, D), BF16),
            pltpu.SemaphoreType.DMA((2, count)), pltpu.SemaphoreType.DMA((3, count)),
            pltpu.SemaphoreType.DMA((7,)), pltpu.SemaphoreType.DMA((5, length // BT + 1)),
        ],
        compiler_params=pltpu.CompilerParams(collective_id=2, has_side_effects=True, vmem_limit_bytes=60 * 2**20),
        name="feed",
    )(tokens, cotangent, attn, recip, wide, gate_turned, down, gains)


def back_kernel(
    pieces, small_pieces, bits, rows,
    pairs_in, values_in, gn_in, gnt_in, gd_in, mask_in, ffn_in, grads_in, normed_in, wide_in, tokens_in,
    total_out, sums_out, grad_out, small_out,
    q_ref, k_ref, v_ref, gn_ref, gnt_ref, gd_ref, mask_ref, normed_ref, wide_ref, tokens_ref,
    part, leaf, mid, total, work, landing, sums, small_work, small_landing, small_sums,
    qt_ref, gq_ref, gkt_ref, gvt_ref, gp_ref, gv_ref, grad_ref, gain_ref,
    line_send, line_recv, cube_send, cube_recv, small_send, small_recv, load_sem, store_sem,
):
    f = lax.axis_index("feat")
    line = LineSum(part, leaf, mid, total, line_send, line_recv, rows, (0, 3, 6))
    cube = CubeSum(work, landing, sums, cube_send, cube_recv, pieces, bits)
    small = CubeSum(small_work, small_landing, small_sums, small_send, small_recv, small_pieces, bits)
    half = HEADS * QK
    first_loads = [
        pltpu.make_async_copy(grads_in.at[pl.ds(a, n)], work.at[pl.ds(a, n)], load_sem.at[m]) for m, (a, n) in enumerate(pieces)
    ] + [pltpu.make_async_copy(ffn_in, part, load_sem.at[len(pieces)])]
    sources = [
        (pairs_in.at[:, pl.ds(0, half)], q_ref), (pairs_in.at[:, pl.ds(half, half)], k_ref), (values_in, v_ref),
        (mask_in, mask_ref), (gn_in, gn_ref), (gd_in, gd_ref), (gnt_in, gnt_ref), (normed_in, normed_ref),
        (wide_in.at[:, pl.ds(0, wide_ref.shape[1])], wide_ref), (tokens_in, tokens_ref),
    ]
    loads = [pltpu.make_async_copy(a, b, load_sem.at[len(pieces) + 1 + n]) for n, (a, b) in enumerate(sources)]
    for load in first_loads:
        load.start()
    greet(line, cube)
    for p in range(len(pieces)):
        first_loads[p].wait()
        cube.launch(p)
    for load in loads:
        load.start()
    first_loads[-1].wait()
    each(line.leaves, line.count)
    gq_ref[...] = jnp.zeros_like(gq_ref)
    for load in loads[:7]:
        load.wait()
    qt_ref[...] = q_ref[...].T

    lane = lax.broadcasted_iota(jnp.int32, (1, 128), 1)
    length = q_ref.shape[0]
    blocks = length // BT
    hb = 2
    groups = HEADS // hb
    lengths = [(blocks - n // groups) + 0.3 for n in range(blocks * groups)]
    whole = sum(lengths)
    sequence = [(p, t) for t in range(2 * cube.nb) for p in range(len(pieces))]
    line_share, cube_share = PASS_LINE, PASS_CUBE

    def due(n, count, share):
        return int(sum(lengths[:n]) / whole * count * share)

    for block in range(blocks):
        lo = block * BT
        below, there = pl.ds(lo, length - lo), pl.ds(lo, BT)

        def group(g, carry):
            h = g * hb
            ql = pl.ds(pl.multiple_of(h // 8 * 128, 128), 128)
            vl = pl.ds(pl.multiple_of(g * 128, 128), 128)
            q, k, v = q_ref[below, ql], k_ref[there, ql], v_ref[there, vl]
            both = jnp.concatenate([gn_ref[below, vl], gd_ref[below, vl]], axis=1)
            mask = mask_ref[block, : length - lo, :]
            gq, turned = None, []
            for a in range(hb):
                km = jnp.where(lane // QK == lax.rem(h + a, 8), k, jnp.zeros_like(k))
                vm = jnp.where(lane // HV == a, v, jnp.zeros_like(v))
                pick = jnp.where(lane == HV * a, jnp.ones_like(v), jnp.zeros_like(v))
                t1 = nt(q, km) + 1.0
                p = (t1 * t1 + 1.0).astype(BF16) * mask
                dp = nt(both, jnp.concatenate([vm, pick], axis=1)).astype(BF16) * mask
                gs = (dp.astype(F32) * t1).astype(BF16)
                out = nn(gs, km)
                gq = out if gq is None else gq + out
                qrows = pl.ds(pl.multiple_of((h + a) * QK, QK), QK)
                vrows = pl.ds(pl.multiple_of((h + a) * HV, HV), HV)
                gkt_ref[qrows, there] = nn(qt_ref[qrows, below], gs)
                turned.append(nn(gnt_ref[vrows, below], p) * 0.5)
            gq_ref[below, ql] += gq
            gvt = jnp.concatenate(turned, axis=0)
            gvt_ref[vl, there] = gvt.astype(BF16)
            gv_ref[there, vl] = gvt.T.astype(BF16)
            for n in range(groups):
                m = block * groups + n
                steps = list(range(due(m, line.steps(), line_share), due(m + 1, line.steps(), line_share)))
                items = sequence[due(m, len(sequence), cube_share) : due(m + 1, len(sequence), cube_share)]
                if steps or items:
                    @pl.when(g == n)
                    def _():
                        for i in range(max(len(steps), len(items))):
                            if i < len(steps):
                                line.serve(jnp.int32(steps[i]))
                            if i < len(items):
                                cube.advance(*items[i])
            return carry

        lax.fori_loop(0, groups, group, 0)
    served, advanced = due(blocks * groups, line.steps(), line_share), due(blocks * groups, len(sequence), cube_share)
    gp_ref[:, :half] = (gq_ref[...] * 0.25).astype(BF16)
    gp_ref[:, half:] = gkt_ref[...].T.astype(BF16)
    for load in loads[7:]:
        load.wait()

    pair_cols, value_cols = 2 * half // 4, HEADS * HV // 4
    small_work[0:value_cols, :] = nn(
        gvt_ref[pl.ds(pl.multiple_of(f * value_cols, value_cols), value_cols), :], normed_ref[...]
    ).astype(BF16)
    small.launch(0)
    small_work[value_cols : value_cols + pair_cols, :] = nn(own_column(gp_ref, f, pair_cols).T, normed_ref[...]).astype(BF16)
    gain_ref[...] = jnp.zeros_like(gain_ref)

    def more(count):
        nonlocal served, advanced
        for _ in range(count):
            if served < line.steps():
                line.serve(jnp.int32(served))
                served += 1
            if advanced < len(sequence) and (len(sequence) - advanced) * 3 >= (line.steps() - served) * 2:
                cube.advance(*sequence[advanced])
                advanced += 1

    def back(n, carry):
        at = pl.ds(pl.multiple_of(n * BT, BT), BT)
        grad = nt(gp_ref[at, :], wide_ref[:, : 2 * half]) + nt(gv_ref[at, :], wide_ref[:, 2 * half :])
        grad_ref[at, :] = grad.astype(BF16)
        x = tokens_ref[at, :].astype(F32)
        scale = lax.rsqrt(jnp.mean(x * x, axis=1, keepdims=True) + EPS)
        gain_ref[0:1, :] += jnp.sum(grad * (x * scale), axis=0, keepdims=True)
        return carry

    lax.fori_loop(0, blocks, back, 0)
    grad_store = pltpu.make_async_copy(grad_ref, grad_out, store_sem.at[0])
    grad_store.start()
    rest = value_cols + pair_cols
    small_work[rest:, :] = jnp.zeros((small_work.shape[0] - rest, D), BF16)
    small_work[rest : rest + 16, :] = gain_ref[...].astype(BF16)
    for p in range(1, len(small_pieces)):
        small.launch(p)
    while advanced < len(sequence):
        more(1)
    stores = []
    for m, (a, n) in enumerate(pieces):
        stores.append(pltpu.make_async_copy(sums.at[pl.ds(a, n)], sums_out.at[pl.ds(a, n)], store_sem.at[2 + m]))
        stores[-1].start()
    for t in range(2 * small.nb):
        for p in range(len(small_pieces)):
            more(1)
            small.advance(p, t)
    small_store = pltpu.make_async_copy(small_sums, small_out, store_sem.at[1])
    small_store.start()
    while served < line.steps():
        more(1)
    each(line.arrived, line.count)
    total_store = pltpu.make_async_copy(total, total_out, store_sem.at[2 + len(pieces)])
    total_store.start()
    each(line.drain, line.count)
    for p in range(len(pieces)):
        cube.drain(p)
    for p in range(len(small_pieces)):
        small.drain(p)
    for s in stores + [grad_store, small_store, total_store]:
        s.wait()


PASS_LINE, PASS_CUBE = 0.7, 0.8


def back(pairs, values, gn, gnt, gd, mask, ffn, grads, normed, wide, tokens, pieces, bits, dp_size):
    length = tokens.shape[0]
    nq, nv, rows = HEADS * QK, HEADS * HV, 32
    count = length // rows
    unit = 16 * dp_size
    small_rows, small_pieces = 0, []
    for n in (nv // 4, nq // 2 + 16):
        n = (n + unit - 1) // unit * unit if small_pieces else n // unit * unit
        if n:
            small_pieces.append((small_rows, n))
            small_rows += n
    need = nv // 4 + nq // 2 + 16
    if small_rows < need:
        small_rows = (need + unit - 1) // unit * unit
        small_pieces = [(0, small_rows)]
    hbm = pl.BlockSpec(memory_space=pl.ANY)

    def buf(*shape, dtype=BF16):
        return pltpu.VMEM(shape, dtype)

    sems = [pltpu.SemaphoreType.DMA((len(p), 2, 2 * len(bits))) for p in (pieces, pieces, small_pieces, small_pieces)]
    return pl.pallas_call(
        functools.partial(back_kernel, pieces, small_pieces, bits, rows),
        out_shape=(
            jax.ShapeDtypeStruct((length, D), BF16),
            jax.ShapeDtypeStruct(grads.shape, BF16),
            jax.ShapeDtypeStruct((length, D), BF16),
            jax.ShapeDtypeStruct((small_rows, D), BF16),
        ),
        in_specs=[hbm] * 11,
        out_specs=(hbm,) * 4,
        scratch_shapes=[
            buf(length, nq), buf(length, nq), buf(length, nv), buf(length, nv), buf(nv, length), buf(length, nv),
            buf(*mask.shape), buf(length, D), buf(D, 2 * nq + nv), buf(length, D),
            buf(length, D), buf(length, D), buf(length, D), buf(length, D),
            buf(*grads.shape), buf(*grads.shape), buf(*grads.shape),
            buf(small_rows, D), buf(small_rows, D), buf(small_rows, D),
            buf(nq, length), buf(length, nq, dtype=F32), buf(nq, length, dtype=F32), buf(nv, length), buf(length, 2 * nq), buf(length, nv),
            buf(length, D), buf(16, D, dtype=F32),
            pltpu.SemaphoreType.DMA((2, count)), pltpu.SemaphoreType.DMA((3, count)), *sems,
            pltpu.SemaphoreType.DMA((len(pieces) + 11,)), pltpu.SemaphoreType.DMA((3 + len(pieces),)),
        ],
        compiler_params=pltpu.CompilerParams(collective_id=4, has_side_effects=True, vmem_limit_bytes=62 * 2**20),
        name="back",
    )(pairs, values, gn, gnt, gd, mask, ffn, grads, normed, wide, tokens)


def update_kernel(
    rates,
    down_w, down_m, down_a, gate_w, gate_m, gate_a, out_w, out_m, out_a, value_w, value_m, value_a,
    pair_w, pair_m, pair_a, gain_w, gain_m, gain_a, big, small, hidden, total, grad_hidden, grad_normed, tokens, gains,
    mixed_o, input_o, pair_mo, pair_wo, pair_ao, value_mo, value_wo, value_ao, out_mo, out_wo, out_ao,
    gate_mo, gate_wo, gate_ao, down_mo, down_wo, down_ao, gain_mo, gain_wo, gain_ao,
):
    ff = down_w.shape[0]
    narrow = value_w.shape[1]
    pair_cols = pair_w.shape[1]

    def put(index, outs, grad, w, m, a, rate):
        moment_next, weight_next, average_next = update(w[index], grad, m[index], a[index], rate)
        outs[0][index], outs[1][index], outs[2][index] = moment_next, weight_next, average_next

    put(..., (down_mo, down_wo, down_ao), big[:ff, :].astype(F32), down_w, down_m, down_a, rates[4])
    for n in range(2):
        first = (n + 1) * ff
        put(n, (gate_mo, gate_wo, gate_ao), big[first : first + ff, :].astype(F32), gate_w, gate_m, gate_a, rates[3])
    first = 3 * ff
    put(..., (out_mo, out_wo, out_ao), big[first : first + out_w.shape[0], :].astype(F32), out_w, out_m, out_a, rates[2])
    first = first + out_w.shape[0]
    put(..., (value_mo, value_wo, value_ao), small[:narrow, :].astype(F32).T, value_w, value_m, value_a, rates[1])
    put(..., (pair_mo, pair_wo, pair_ao), small[narrow : narrow + pair_cols, :].astype(F32).T, pair_w, pair_m, pair_a, rates[0])
    gain_one = small[narrow + pair_cols : narrow + pair_cols + 16, :].astype(F32)[0:1, :]
    gain_two = big[first : first + 16, :].astype(F32)[0:1, :]
    put(slice(0, 1), (gain_mo, gain_wo, gain_ao), gain_one, gain_w, gain_m, gain_a, rates[5])
    put(slice(1, 2), (gain_mo, gain_wo, gain_ao), gain_two, gain_w, gain_m, gain_a, rates[5])

    mixed_o[...] = (hidden[...] + total[...].astype(F32)).astype(BF16)
    x = tokens[...].astype(F32)
    scale = lax.rsqrt(jnp.mean(x * x, axis=1, keepdims=True) + EPS)
    unit = x * scale
    u = grad_normed[...].astype(F32) * gains[0:1, :]
    input_o[...] = grad_hidden[...] + scale * (u - unit * jnp.mean(u * unit, axis=1, keepdims=True))


def finish(rates, weights, big, small, hidden, total, grad_hidden, grad_normed, tokens, gains):
    length = tokens.shape[0]
    steps = D // 128
    rows = length // steps
    ff = weights[0][0].shape[0]
    narrow, pair_cols = weights[3][0].shape[1], weights[4][0].shape[1]

    def cols(n):
        return pl.BlockSpec((n, 128), lambda i: (0, i))

    def tall(n):
        return pl.BlockSpec((128, n), lambda i: (i, 0))

    token = pl.BlockSpec((rows, D), lambda i: (i, 0))
    specs = [cols(ff), pl.BlockSpec((2, ff, 128), lambda i: (0, 0, i)), cols(weights[2][0].shape[0]), tall(narrow), tall(pair_cols), cols(2)]
    order = [4, 3, 2, 1, 0, 5]
    flat = [a for group in weights for a in group]
    out_shape = [jax.ShapeDtypeStruct((length, D), BF16), jax.ShapeDtypeStruct((length, D), F32)]
    out_specs = [token, token]
    for n in order:
        out_shape += [jax.ShapeDtypeStruct(weights[n][0].shape, F32)] * 3
        out_specs += [specs[n]] * 3
    in_specs = [specs[n] for n in range(6) for _ in range(3)]
    in_specs += [cols(big.shape[0]), cols(small.shape[0])] + [token] * 5 + [pl.BlockSpec((2, D), lambda i: (0, 0))]
    return pl.pallas_call(
        functools.partial(update_kernel, rates),
        grid=(steps,),
        out_shape=out_shape,
        in_specs=in_specs,
        out_specs=out_specs,
        compiler_params=pltpu.CompilerParams(vmem_limit_bytes=50 * 2**20),
        name="finish",
    )(*flat, big, small, hidden, total, grad_hidden, grad_normed, tokens, gains)


def update(weight, grad_total, moment, average, rate):
    moment_next = MOMENTUM * moment + grad_total
    weight_next = weight - rate * (grad_total + MOMENTUM * moment_next)
    average_next = average + (weight_next - average) / STEP
    return (moment_next, weight_next, average_next)


def on_device(
    tokens,
    cotangent,
    doc_starts,
    queries_keys,
    value_weight,
    out_weight,
    gate_up,
    down_weight,
    norm_gains,
    queries_moment,
    value_moment,
    out_moment,
    gate_moment,
    down_moment,
    gains_moment,
    queries_average,
    value_average,
    out_average,
    gate_average,
    down_average,
    gains_average,
):
    total_tokens = float(tokens.shape[0] * lax.axis_size("dp"))
    dp_size = lax.axis_size("dp")
    ff = down_weight.shape[0]
    gate_turned = gate_up.transpose(0, 2, 1)
    normed_one, pairs, values, wide, gate_low, down_low, attn_low, recip, mask = front(
        doc_starts, tokens, norm_gains, queries_keys, value_weight, out_weight, gate_turned, down_weight
    )
    padded, pieces, bits = cube_shape(3 * ff + out_weight.shape[0] + 16, dp_size, 4)
    hidden_one, grad_hidden, grad_numer, grad_numer_turned, grad_denom, ffn_part, big = feed(
        tokens, cotangent, attn_low, recip, wide, gate_low, down_low, norm_gains, padded
    )
    total, big, grad_normed_one, small = back(
        pairs, values, grad_numer, grad_numer_turned, grad_denom, mask, ffn_part, big, normed_one, wide, tokens,
        pieces, bits, dp_size,
    )
    rates = (
        (D * total_tokens) ** (-0.5),
        (D * total_tokens) ** (-0.5),
        (HEADS * HV * total_tokens) ** (-0.5),
        (D * total_tokens) ** (-0.5),
        (FF * total_tokens) ** (-0.5),
        0.2 * total_tokens ** (-0.5),
    )
    weights = (
        (down_weight, down_moment, down_average),
        (gate_turned, gate_moment.transpose(0, 2, 1), gate_average.transpose(0, 2, 1)),
        (out_weight, out_moment, out_average),
        (value_weight, value_moment, value_average),
        (queries_keys, queries_moment, queries_average),
        (norm_gains, gains_moment, gains_average),
    )
    outs = list(finish(rates, weights, big, small, hidden_one, total, grad_hidden, grad_normed_one, tokens, norm_gains))
    outs[11:14] = [o.transpose(0, 2, 1) for o in outs[11:14]]
    return tuple(outs)


def solution(mesh):
    in_specs = (
        P("dp", None),
        P("dp", None),
        P("dp", None),
        P(None, "feat"),
        P(None, "feat"),
        P("feat", None),
        P(None, None, "feat"),
        P("feat", None),
        P(),
        P(None, "feat"),
        P(None, "feat"),
        P("feat", None),
        P(None, None, "feat"),
        P("feat", None),
        P(),
        P(None, "feat"),
        P(None, "feat"),
        P("feat", None),
        P(None, None, "feat"),
        P("feat", None),
        P(),
    )
    out_specs = (
        P("dp", None),
        P("dp", None),
        P(None, "feat"),
        P(None, "feat"),
        P(None, "feat"),
        P(None, "feat"),
        P(None, "feat"),
        P(None, "feat"),
        P("feat", None),
        P("feat", None),
        P("feat", None),
        P(None, None, "feat"),
        P(None, None, "feat"),
        P(None, None, "feat"),
        P("feat", None),
        P("feat", None),
        P("feat", None),
        P(),
        P(),
        P(),
    )
    return jax.shard_map(
        on_device, mesh=mesh, in_specs=in_specs, out_specs=out_specs, check_vma=False
    )
```

```python
import functools
import jax
import jax.numpy as jnp
from jax import lax
from jax.experimental import pallas as pl
from jax.experimental.pallas import tpu as pltpu
from jax.sharding import PartitionSpec as P

D = 1024
HEADS = 16
QK = 16
HV = 64
FF = 2752
STEP = 4
BT = 256
F32 = jnp.float32
BF16 = jnp.bfloat16

MESH = pl.DeviceIdType.MESH
EPS = 1e-06
MOMENTUM = 0.9


def nt(a, b):
    return lax.dot_general(a, b, (((1,), (1,)), ((), ())), preferred_element_type=F32)


def nn(a, b):
    return lax.dot_general(a, b, (((1,), (0,)), ((), ())), preferred_element_type=F32)


class LineSum:
    def __init__(self, part, leaf, mid, total, send, recv, rows, lags=(0, 2, 4)):
        self.part, self.leaf, self.mid, self.total, self.send, self.recv = part, leaf, mid, total, send, recv
        self.rows, self.lags = rows, lags
        self.count = part.shape[0] // rows
        self.dp, self.f = lax.axis_index("dp"), lax.axis_index("feat")

    def place(self, c):
        odd = lax.rem(c, 2)
        return self.f + odd * (3 - 2 * self.f), 1 - 2 * odd

    def copy(self, c, src, dst, kind, slot, to):
        at = pl.ds(pl.multiple_of(c * self.rows, self.rows), self.rows)
        return pltpu.make_async_remote_copy(
            src_ref=src.at[at], dst_ref=dst.at[at], send_sem=self.send.at[slot], recv_sem=self.recv.at[min(kind, 1), c],
            device_id=(self.dp, to), device_id_type=MESH)

    def leaves(self, c):
        p, up = self.place(c)

        @pl.when(p == 3)
        def _():
            self.copy(c, self.part, self.leaf, 0, 0, self.f - up).start()

        @pl.when(p == 0)
        def _():
            self.copy(c, self.part, self.leaf, 0, 0, self.f + up).start()

    def middle(self, c):
        p, up = self.place(c)
        at = pl.ds(pl.multiple_of(c * self.rows, self.rows), self.rows)

        @pl.when(p == 2)
        def _():
            self.copy(c, self.part, self.leaf, 0, 0, self.f).wait_recv()
            self.part[at, :] = (self.part[at, :].astype(F32) + self.leaf[at, :].astype(F32)).astype(BF16)
            self.copy(c, self.part, self.mid, 1, 0, self.f - up).start()

    def root(self, c):
        p, up = self.place(c)
        at = pl.ds(pl.multiple_of(c * self.rows, self.rows), self.rows)

        @pl.when(p == 1)
        def _():
            self.copy(c, self.part, self.leaf, 0, 0, self.f).wait_recv()
            self.copy(c, self.part, self.mid, 1, 0, self.f).wait_recv()
            self.total[at, :] = (
                self.part[at, :].astype(F32) + self.leaf[at, :].astype(F32) + self.mid[at, :].astype(F32)
            ).astype(BF16)
            self.copy(c, self.total, self.total, 2, 1, self.f + up).start()
            self.copy(c, self.total, self.total, 2, 0, self.f - up).start()

    def onward(self, c):
        p, up = self.place(c)

        @pl.when(p == 2)
        def _():
            self.copy(c, self.total, self.total, 2, 0, self.f).wait_recv()
            self.copy(c, self.total, self.total, 2, 1, self.f + up).start()

    def serve(self, i):
        for lag, act in zip(self.lags, (self.middle, self.root, self.onward)):
            c = i - lag

            @pl.when(jnp.logical_and(c >= 0, c < self.count))
            def _():
                act(c)

    def steps(self):
        return self.count + self.lags[-1]

    def arrived(self, c):
        p, up = self.place(c)

        @pl.when(jnp.logical_or(p == 0, p == 3))
        def _():
            self.copy(c, self.total, self.total, 2, 0, self.f).wait_recv()

    def drain(self):
        def all_sent(slot):
            pltpu.make_async_remote_copy(
                src_ref=self.part, dst_ref=self.part, send_sem=self.send.at[slot], recv_sem=self.recv.at[0, 0],
                device_id=(self.dp, self.f), device_id_type=MESH,
            ).wait_send()

        all_sent(0)

        @pl.when(jnp.logical_or(self.f == 1, self.f == 2))
        def _():
            all_sent(1)


class CubeSum:
    def __init__(self, work, recv, out, send_sem, recv_sem, pieces, bits):
        self.work, self.recv, self.out, self.send_sem, self.recv_sem = work, recv, out, send_sem, recv_sem
        self.pieces, self.nb = pieces, len(bits)
        self.dp, self.f = lax.axis_index("dp"), lax.axis_index("feat")
        self.orders = [list(bits), [bits[0]] + list(bits[1:])[::-1]]
        self.bits = bits

    def partner(self, bit):
        return self.dp + bit - 2 * bit * lax.rem(self.dp // bit, 2)

    def lanes(self, colour):
        half = self.work.shape[1] // 2
        return pl.ds(colour * half, half)

    def segment(self, piece, colour, k):
        first, rows = self.pieces[piece]
        start = first
        for bit in self.orders[colour][:k]:
            rows = rows // 2
            start = start + rows * lax.rem(self.dp // bit, 2)
        return start, rows

    def at(self, start, rows):
        return pl.ds(pl.multiple_of(start, 16), rows)

    def halve(self, piece, colour, k):
        start, rows = self.segment(piece, colour, k)
        rows = rows // 2
        bit = self.orders[colour][k]
        own = lax.rem(self.dp // bit, 2)
        first, whole = self.pieces[piece]
        landing = first + whole - 2 * rows
        return pltpu.make_async_remote_copy(
            src_ref=self.work.at[self.at(start + rows * (1 - own), rows), self.lanes(colour)],
            dst_ref=self.recv.at[self.at(landing, rows), self.lanes(colour)],
            send_sem=self.send_sem.at[0], recv_sem=self.recv_sem.at[piece, colour, k],
            device_id=(self.partner(bit), self.f), device_id_type=MESH)

    def add(self, piece, colour, k):
        start, rows = self.segment(piece, colour, k + 1)
        first, whole = self.pieces[piece]
        landing = first + whole - 2 * rows
        target = self.out if k + 1 == self.nb else self.work
        mine = self.work[self.at(start, rows), self.lanes(colour)].astype(F32)
        target[self.at(start, rows), self.lanes(colour)] = (
            mine + self.recv[self.at(landing, rows), self.lanes(colour)].astype(F32)
        ).astype(BF16)

    def double(self, piece, colour, k):
        start, rows = self.segment(piece, colour, k + 1)
        bit = self.orders[colour][k]
        at = self.at(start, rows)
        slot = 2 * self.nb - 1 - k
        return pltpu.make_async_remote_copy(
            src_ref=self.out.at[at, self.lanes(colour)], dst_ref=self.out.at[at, self.lanes(colour)],
            send_sem=self.send_sem.at[1], recv_sem=self.recv_sem.at[piece, colour, slot],
            device_id=(self.partner(bit), self.f), device_id_type=MESH)

    def launch(self, piece):
        for colour in range(2):
            self.halve(piece, colour, 0).start()

    def advance(self, piece, t):
        for colour in range(2):
            if t < self.nb:
                self.halve(piece, colour, t).wait_recv()
                self.add(piece, colour, t)
                if t + 1 < self.nb:
                    self.halve(piece, colour, t + 1).start()
                else:
                    self.double(piece, colour, self.nb - 1).start()
            else:
                k = 2 * self.nb - 1 - t
                self.double(piece, colour, k).wait_recv()
                if k > 0:
                    self.double(piece, colour, k - 1).start()

    def drain(self):
        rows = self.work.shape[0]
        sent = pl.ds(0, rows - rows // 2**self.nb)
        for n, ref in enumerate((self.work, self.out)):
            pltpu.make_async_remote_copy(
                src_ref=ref.at[sent], dst_ref=ref.at[sent], send_sem=self.send_sem.at[n], recv_sem=self.recv_sem.at[0, 0, 0],
                device_id=(self.dp, self.f), device_id_type=MESH,
            ).wait_send()


def split_rows(rows, unit, count):
    units = rows // unit
    out, first = [], 0
    for n in range(count):
        take = (units * (n + 1) // count - units * n // count) * unit
        out.append((first, take))
        first += take
    return [p for p in out if p[1]]


def own_column(ref, f, width):
    return ref[:, pl.ds(pl.multiple_of(f * width, width), width)]


def greet(line, cube):
    sem = pltpu.get_barrier_semaphore()
    f = lax.axis_index("feat")
    count = jnp.int32(0)
    if cube is not None:
        for bit in cube.bits:
            pl.semaphore_signal(sem, inc=1, device_id=(cube.partner(bit), f), device_id_type=MESH)
        count = count + len(cube.bits)
    if line is not None:
        @pl.when(f > 0)
        def _():
            pl.semaphore_signal(sem, inc=1, device_id=(line.dp, f - 1), device_id_type=MESH)

        @pl.when(f < 3)
        def _():
            pl.semaphore_signal(sem, inc=1, device_id=(line.dp, f + 1), device_id_type=MESH)
        count = count + jnp.where(f > 0, 1, 0) + jnp.where(f < 3, 1, 0)
    pl.semaphore_wait(sem, count)


def each(act, n):
    def body(c, carry):
        act(c)
        return carry

    lax.fori_loop(0, n, body, 0)


def cube_shape(rows, dp_size, count):
    unit = 16 * dp_size
    padded = (rows + unit - 1) // unit * unit
    bits = tuple(2**n for n in range(dp_size.bit_length() - 1))
    return padded, split_rows(padded, unit, count), bits


class Weaver:
    def __init__(self, now, margin=0.5, cost=0.35):
        self.now, self.margin, self.cost = now, margin, cost
        self.streams = {}

    def add(self, name, floors, leads):
        self.streams[name] = [list(floors), list(leads), 0, self.now]

    def ready(self, name):
        floors, leads, n, last = self.streams[name]
        return max(floors[n], last + leads[n])

    def open(self):
        return [name for name, s in self.streams.items() if s[2] < len(s[0])]

    def take(self, name):
        stream = self.streams[name]
        self.now = max(self.now, self.ready(name)) + self.cost
        stream[2] += 1
        stream[3] = self.now
        return name, stream[2] - 1

    def unit(self, length):
        self.now += length
        out = []
        while self.open():
            name = min(self.open(), key=self.ready)
            if self.ready(name) > self.now - self.margin:
                break
            out.append(self.take(name))
        return out

    def until(self, names):
        out = []
        while any(name in names for name in self.open()):
            out.append(self.take(min(self.open(), key=self.ready)))
        return out


def line_floors(line, start):
    pace = line.rows * line.part.shape[1] * 2 / 40e3
    return [start + pace * (n + 1) + 3.0 for n in range(line.steps())]


def cube_floors(cube, start):
    count = 2 * cube.nb
    ends, floors, times = [start] * len(cube.pieces), [[] for _ in cube.pieces], [[] for _ in cube.pieces]
    for t in range(count):
        near = t in (0, count - 1)
        share = 2 ** (min(t, count - 1 - t) + 1)
        busy = max(ends) if t not in (0, 1, count - 1) else start
        for p, (_, rows) in enumerate(cube.pieces):
            size = rows / share * 1024
            own = 2 * size / 430e3 if near else size / 30e3
            begin = ends[p] + (3.3 if t else 0.0)
            busy = max(busy, begin) + own
            ends[p] = busy
            floors[p].append(busy + 3.0)
            times[p].append(own + 3.0)
    return floors, times


def front_kernel(
    bits, starts_ref, tokens_in, gains_ref, pair_ref, value_ref, out_ref, gate_in, down_in,
    normed_out, pairs_out, values_out, wide_out, gate_out, down_out, attn_out, recip_out, mask_out,
    thin_ref, thick_ref, turned_ref, tokens_ref, gate_f32, down_f32,
    normed_ref, pairs_ref, values_ref, wide_ref, gate_ref, down_ref, attn_ref, recip_ref, mask_ref, acc_ref,
    send_sem, recv_sem, load_sem, store_sem,
):
    dp = lax.axis_index("dp")
    f = lax.axis_index("feat")
    slices = lax.axis_size("feat")
    last = 3
    pieces = 2 ** len(bits)
    j = lax.rem(dp, pieces)
    base = dp - j
    pair_cols, value_cols = pair_ref.shape[1], value_ref.shape[1]
    pairs_wide, values_wide = slices * pair_cols, slices * value_cols
    rows = pair_ref.shape[0] // pieces
    length = tokens_ref.shape[0]
    blocks = length // BT
    loads = [
        pltpu.make_async_copy(a, b, load_sem.at[n])
        for n, (a, b) in enumerate([(tokens_in, tokens_ref), (gate_in, gate_f32), (down_in, down_f32)])
    ]
    for load in loads:
        load.start()

    def flip(k, bit):
        return k + bit - 2 * bit * lax.rem(k // bit, 2)

    colour_bits = [list(bits[1:]) + [bits[0]], list(bits[1:])[::-1] + [bits[0]]]

    def place(k, colour):
        return sum(k // bit % 2 * 2**n for n, bit in enumerate(colour_bits[colour]))

    def cast(k):
        at = pl.ds(pl.multiple_of(k * rows, rows), rows)
        pair = pair_ref[at, :].astype(BF16)
        thick = value_ref[at, :].astype(BF16)
        turned = out_ref[:, at].T.astype(BF16)
        for colour in range(2):
            part = slice(colour * rows // 2, (colour + 1) * rows // 2)
            thin_ref[colour, place(k, colour), 0] = pair[part]
            thick_ref[colour, place(k, colour), 0] = thick[part]
            turned_ref[colour, place(k, colour), 0] = turned[part]

    cast(j)
    order = [
        jnp.where(f == 0, 1, f - 1),
        jnp.where(f < 2, 2, jnp.where(f == 2, 3, 1)),
        jnp.where(f < 2, 3, 0),
    ]
    barrier = pltpu.get_barrier_semaphore()
    for bit in bits:
        pl.semaphore_signal(barrier, inc=1, device_id=(base + flip(j, bit), f), device_id_type=MESH)
    for z in order:
        pl.semaphore_signal(barrier, inc=1, device_id=(dp, z), device_id_type=MESH)
    pl.semaphore_wait(barrier, len(bits) + last)

    bufs = (thin_ref, thick_ref, turned_ref)
    here = (dp, f)

    def copy(wave, source, target, colour, kind, device, r=None):
        group = 0 if r is None or wave != 1 else r - 1
        return pltpu.make_async_remote_copy(
            src_ref=source, dst_ref=target, send_sem=send_sem.at[wave], recv_sem=recv_sem.at[wave, colour, kind, group],
            device_id=device, device_id_type=MESH,
        )

    for wave in range(3):
        for z in order:
            for colour in range(2):
                at = bufs[wave].at[colour, place(j, colour)]
                r = lax.rem(f - z + slices, slices)
                copy(wave, at.at[0], at.at[r], colour, 0, (dp, z), r).start()

    def held(wave, k, colour, n, r):
        first = place(k, colour) // 2**n * 2**n
        which = pl.ds(1, last) if r is None else pl.ds(r, 1)
        return bufs[wave].at[colour, pl.ds(first, 2**n), which]

    def start_step(wave, n, r):
        for colour in range(2):
            at = held(wave, j, colour, n, r)
            copy(wave, at, at, colour, 1 + n, (base + flip(j, colour_bits[colour][n]), f), r).start()

    def arrive(wave, a=None):
        r = None if a is None else relative[a]
        for colour in range(2):
            at = held(wave, j, colour, 0, r)
            copy(wave, at, at, colour, 0, here, r).wait_recv()
        start_step(wave, 0, r)

    def step(wave, n, a=None):
        r = None if a is None else relative[a]
        for colour in range(2):
            at = held(wave, flip(j, colour_bits[colour][n]), colour, n, r)
            copy(wave, at, at, colour, 1 + n, here, r).wait_recv()
        if n + 1 < len(bits):
            start_step(wave, n + 1, r)

    relative = [lax.rem(z - f + slices, slices) for z in order]

    def put(wave, r, lanes):
        for k in range(pieces):
            for colour in range(2):
                first = k * rows + colour * rows // 2
                wide_ref[first : first + rows // 2, lanes] = bufs[wave][colour, place(k, colour), r]

    def owner(r):
        return lax.rem(f + r, slices)

    def put_thin(r):
        put(0, r, pl.ds(pl.multiple_of(owner(r) * pair_cols, pair_cols), pair_cols))

    def lanes(first, z):
        return pl.ds(pl.multiple_of(first + z * value_cols, 128), value_cols)

    def store(n, source, target, at=None):
        if at is not None:
            source, target = source.at[:, at], target.at[:, at]
        return pltpu.make_async_copy(source, target, store_sem.at[n])

    def use(r):
        z = owner(r)
        put(1, r, lanes(pairs_wide, z))

        def some(n, carry):
            at = pl.ds(pl.multiple_of(n * BT, BT), BT)
            values_ref[at, lanes(0, z)] = nn(normed_ref[at, :], wide_ref[:, lanes(pairs_wide, z)]).astype(BF16)
            return carry

        lax.fori_loop(0, blocks, some, 0)
        store(5, wide_ref, wide_out, lanes(pairs_wide, z)).start()
        store(6, values_ref, values_out, lanes(0, z)).start()

    def put_turned(r):
        at = lanes(pairs_wide + values_wide, owner(r))
        put(2, r, at)
        store(5, wide_ref, wide_out, at).start()

    def cast_rest(n, carry):
        cast(lax.rem(j + n, pieces))
        return carry

    lax.fori_loop(1, pieces, cast_rest, 0)
    loads[0].wait()

    def norm(n, carry):
        at = pl.ds(pl.multiple_of(n * BT, BT), BT)
        x = tokens_ref[at, :].astype(F32)
        scale = lax.rsqrt(jnp.mean(x * x, axis=1, keepdims=True) + EPS)
        normed_ref[at, :] = (x * scale * gains_ref[0:1, :]).astype(BF16)
        return carry

    lax.fori_loop(0, blocks, norm, 0)
    store(0, normed_ref, normed_out).start()
    put_thin(0)
    arrive(0)
    use(0)
    step(0, 0)

    begin = jnp.zeros((length, 1), jnp.int32)
    position = lax.broadcasted_iota(jnp.int32, (length, 1), 0)
    for n in range(starts_ref.shape[1]):
        begin = jnp.where(starts_ref[0, n] <= position, jnp.maximum(begin, starts_ref[0, n]), begin)
    for n in range(blocks):
        rest = length - n * BT
        s = n * BT + lax.broadcasted_iota(jnp.int32, (rest, BT), 1)
        keep = jnp.logical_and(s <= position[n * BT :], s >= begin[n * BT :])
        mask_ref[n, :rest, :] = keep.astype(F32).astype(BF16)
        if n:
            mask_ref[n, rest:, :] = jnp.zeros((n * BT, BT), BF16)
    store(1, mask_ref, mask_out).start()
    def cast_all(source, target):
        def go(m, carry):
            at = pl.ds(pl.multiple_of(m * 16, 16), 16)
            target[at, :] = source[at, :].astype(BF16)
            return carry

        lax.fori_loop(0, source.shape[0] // 16, go, 0)

    step(0, 1)
    arrive(1, 0)
    arrive(1, 1)
    put_turned(0)
    loads[1].wait()
    loads[2].wait()
    cast_all(gate_f32.at[0], gate_ref.at[0])
    step(0, 2)
    step(1, 0, 0)
    arrive(1, 2)
    step(1, 0, 1)
    for r in range(1, slices):
        put_thin(r)

    half = pairs_wide // 2

    def project_pairs(n, carry):
        at = pl.ds(pl.multiple_of(n * BT, BT), BT)
        pairs = nn(normed_ref[at, :], wide_ref[:, :pairs_wide]).astype(BF16)
        pairs_ref[at, :half] = pairs[:, :half] * jnp.bfloat16(0.25)
        pairs_ref[at, half:] = pairs[:, half:]
        return carry

    lax.fori_loop(0, blocks, project_pairs, 0)
    store(4, pairs_ref, pairs_out).start()
    store(5, wide_ref, wide_out, pl.ds(0, pairs_wide)).start()

    lane = lax.broadcasted_iota(jnp.int32, (1, 128), 1)
    def cast_last():
        cast_all(down_f32, down_ref)
        store(2, gate_ref, gate_out).start()
        store(3, down_ref, down_out).start()

    def put_others():
        for r in range(1, slices):
            put_turned(r)

    def cast_up():
        cast_all(gate_f32.at[1], gate_ref.at[1])

    events = {
        1: [(step, 1, 1, 0), (step, 1, 0, 2), (arrive, 2)],
        2: [(cast_up,), (step, 1, 1, 1), (step, 1, 2, 0), (use, relative[0])],
        3: [(step, 1, 1, 2), (step, 2, 0)],
        4: [(step, 1, 2, 1), (use, relative[1])],
        5: [(cast_last,), (step, 2, 1)],
        6: [(step, 1, 2, 2), (use, relative[2])],
        7: [(step, 2, 2), (put_others,)],
    }

    def unit(n, carry):
        for at, acts in events.items():
            @pl.when(n == at)
            def _():
                for act in acts:
                    act[0](*act[1:])
        a = n // 2
        z = jnp.where(a == 0, f, jnp.where(a == 1, order[0], jnp.where(a == 2, order[1], order[2])))
        pair = 2 * z + lax.rem(n, 2)
        vl = pl.ds(pl.multiple_of(pair * 128, 128), 128)
        ql = pl.ds(pl.multiple_of(pair // 4 * 128, 128), 128)
        kl = pl.ds(pl.multiple_of(half + pair // 4 * 128, 128), 128)
        for block in range(blocks):
            first = block * BT
            below, there = pl.ds(first, length - first), pl.ds(first, BT)
            q, k, v = pairs_ref[below, ql], pairs_ref[there, kl], values_ref[there, vl]
            mask = mask_ref[block, : length - first, :]
            for m in range(2):
                own = lane // QK == lax.rem(2 * pair + m, 8)
                t1 = nt(q, jnp.where(own, k, jnp.zeros_like(k))) + 1.0
                p = (t1 * t1 + 1.0).astype(BF16) * mask
                out = nn(p, jnp.where(lane // HV == m, v, jnp.ones_like(v)))
                if block:
                    acc_ref[m, below, :] += out
                else:
                    acc_ref[m] = out
        one, two = acc_ref[0], acc_ref[1]
        numer = jnp.where(lane < HV, one, two)
        recip = 1.0 / pltpu.roll(jnp.where(lane < HV, two, one), HV, 1)
        attn_ref[:, vl] = (numer * recip).astype(BF16)
        recip_ref[:, vl] = recip
        store(7, attn_ref, attn_out, vl).start()
        store(8, recip_ref, recip_out, vl).start()
        return carry

    lax.fori_loop(0, 2 * slices, unit, 0)
    for wave in range(3):
        at = bufs[wave].at[:, :, pl.ds(0, last)]
        copy(wave, at, at, 0, 0, here).wait_send()
    for n, (source, target) in enumerate([
        (normed_ref, normed_out), (mask_ref, mask_out), (gate_ref, gate_out), (down_ref, down_out), (pairs_ref, pairs_out),
        (wide_ref, wide_out), (values_ref, values_out), (attn_ref, attn_out), (recip_ref, recip_out),
    ]):
        store(n, source, target).wait()


def front(starts, tokens, gains, pair_w, value_w, out_w, gate_turned, down):
    length = tokens.shape[0]
    ff = down.shape[0]
    slices = 4
    pair_cols, value_cols = pair_w.shape[1], value_w.shape[1]
    bits = (1, 2, 4)
    hbm = pl.BlockSpec(memory_space=pl.ANY)
    vmem = pl.BlockSpec(memory_space=pltpu.VMEM)
    shapes = [
        ((length, D), BF16),
        ((length, slices * pair_cols), BF16),
        ((length, slices * value_cols), BF16),
        ((D, slices * (pair_cols + 2 * value_cols)), BF16),
        ((2, ff, D), BF16),
        ((ff, D), BF16),
        ((length, slices * value_cols), BF16),
        ((length, slices * value_cols), F32),
        ((length // BT, length, BT), BF16),
    ]
    return pl.pallas_call(
        functools.partial(front_kernel, bits),
        out_shape=tuple(jax.ShapeDtypeStruct(*s) for s in shapes),
        in_specs=[pl.BlockSpec(memory_space=pltpu.SMEM), hbm] + [vmem] * 4 + [hbm] * 2,
        out_specs=(hbm,) * 9,
        scratch_shapes=[
            pltpu.VMEM((2, 8, slices, D // 16, pair_cols), BF16),
            pltpu.VMEM((2, 8, slices, D // 16, value_cols), BF16),
            pltpu.VMEM((2, 8, slices, D // 16, value_cols), BF16),
            pltpu.VMEM((length, D), BF16),
            pltpu.VMEM((2, ff, D), F32),
            pltpu.VMEM((ff, D), F32),
        ]
        + [pltpu.VMEM(*s) for s in shapes]
        + [
            pltpu.VMEM((2, length, 128), F32),
            pltpu.SemaphoreType.DMA((3,)),
            pltpu.SemaphoreType.DMA((3, 2, 4, 3)),
            pltpu.SemaphoreType.DMA((3,)),
            pltpu.SemaphoreType.DMA((9,)),
        ],
        compiler_params=pltpu.CompilerParams(collective_id=1, has_side_effects=True, vmem_limit_bytes=60 * 2**20),
        name="front",
    )(starts, tokens, gains, pair_w, value_w, out_w, gate_turned, down)


def feed_kernel(
    rows, tokens_in, cot_in, attn_in, recip_in, wide_in, gate_in, down_in, gains_ref,
    hidden_out, grad_hidden_out, gn_out, gnt_out, gd_out, ffn_out, grads_out,
    tokens_ref, cot_ref, attn_ref, out_w, gate_ref, down_ref, recip_ref,
    hidden_ref, scale_ref, normed_ref, product_t, gate_t, up_t, own_t, gain_ref, ga_ref, gn_ref, gnt_ref, gd_ref, ffn_ref, grads_ref,
    part, leaf, mid, total, send, recv, load_sem, store_sem,
):
    f = lax.axis_index("feat")
    line = LineSum(part, leaf, mid, total, send, recv, rows, (0, 3, 6))
    length = tokens_ref.shape[0]
    ff = down_ref.shape[0]
    value_cols = own_t.shape[0]
    blocks = length // BT
    first_out = wide_in.shape[1] - attn_ref.shape[1]
    top, others = pl.ds(0, BT), pl.ds(BT, length - BT)
    pairs = [
        (attn_in.at[top], attn_ref.at[top]), (wide_in.at[:, pl.ds(first_out, attn_ref.shape[1])], out_w),
        (tokens_in.at[top], tokens_ref.at[top]), (gate_in, gate_ref), (cot_in.at[top], cot_ref.at[top]), (down_in, down_ref),
        (attn_in.at[others], attn_ref.at[others]), (tokens_in.at[others], tokens_ref.at[others]),
        (cot_in.at[others], cot_ref.at[others]), (recip_in, recip_ref),
    ]
    loads = [pltpu.make_async_copy(a, b, load_sem.at[n]) for n, (a, b) in enumerate(pairs)]
    for load in loads:
        load.start()
    greet(line, None)
    for load in loads[:6]:
        load.wait()

    def store(source, target, n):
        at = pl.ds(pl.multiple_of(n * BT, BT), BT)
        return pltpu.make_async_copy(source.at[at], target.at[at], store_sem.at[n])

    def block(b, carry):
        at = pl.ds(pl.multiple_of(b * BT, BT), BT)
        turn = 4 * (b - 1)

        @pl.when(b == 1)
        def _():
            for load in loads[6:9]:
                load.wait()

        hidden = tokens_ref[at, :].astype(F32) + nt(attn_ref[at, :], out_w[...])
        hidden_ref[at, :] = hidden
        store(hidden_ref, hidden_out, b).start()
        scale = lax.rsqrt(jnp.mean(hidden * hidden, axis=1, keepdims=True) + EPS)
        scale_ref[at, :] = jnp.broadcast_to(scale, (BT, 128))
        normed = (hidden * scale * gains_ref[1:2, :]).astype(BF16)
        normed_ref[at, :] = normed
        line.serve(turn)
        gate = nt(normed, gate_ref[0])
        up = nt(normed, gate_ref[1])
        line.serve(turn + 1)
        back = nt(cot_ref[at, :], down_ref[...])
        sig = 1.0 / (1.0 + jnp.exp(-gate))
        active = gate * sig
        slope = sig * (1.0 + gate * (1.0 - sig))
        product = (active * up).astype(BF16)
        grad_gate = (back * up * slope).astype(BF16)
        grad_up = (back * active).astype(BF16)
        line.serve(turn + 2)
        part[at, :] = (nn(grad_gate, gate_ref[0]) + nn(grad_up, gate_ref[1])).astype(BF16)

        def out(c, carry):
            line.leaves(b * (BT // rows) + c)
            return carry

        lax.fori_loop(0, BT // rows, out, 0)
        ffn_ref[at, :] = nn(product, down_ref[...]).astype(BF16)
        product_t[:, at] = product.T
        gate_t[:, at] = grad_gate.T
        up_t[:, at] = grad_up.T
        line.serve(turn + 3)
        return carry

    lax.fori_loop(0, blocks, block, 0)
    served = 4 * (blocks - 1)
    gain_ref[...] = jnp.zeros_like(gain_ref)
    chunks = []
    at = 0
    while at < ff:
        chunks.append((at, min(176, ff - at)))
        at += chunks[-1][1]
    for n, (turned, right) in enumerate([(product_t, cot_ref), (gate_t, normed_ref), (up_t, normed_ref)]):
        for first, size in chunks:
            at = slice(n * ff + first, n * ff + first + size)
            grads_ref[at, :] = nn(turned[first : first + size, :], right[...]).astype(BF16)
            line.serve(jnp.int32(served))
            served += 1
    ffn_store = pltpu.make_async_copy(ffn_ref, ffn_out, store_sem.at[blocks])
    ffn_store.start()
    grads_store = pltpu.make_async_copy(
        grads_ref.at[pl.ds(0, 3 * ff)], grads_out.at[pl.ds(0, 3 * ff)], store_sem.at[blocks + 1]
    )
    grads_store.start()
    own_t[...] = own_column(attn_ref, f, value_cols).T
    loads[-1].wait()
    same = lax.broadcasted_iota(jnp.int32, (128, 128), 0) // HV == lax.broadcasted_iota(jnp.int32, (128, 128), 1) // HV
    negate = jnp.where(same, -1.0, 0.0).astype(BF16)
    size = 4 * rows
    units = length // size

    def out(n, source, target, at=None):
        if at is not None:
            source, target = source.at[at], target.at[at]
        return pltpu.make_async_copy(source, target, store_sem.at[blocks + 2 + n])

    def back_rows(u):
        at = pl.ds(u * size, size)
        for c in range(4):
            line.arrived(jnp.int32(4 * u + c))
        if u * size % BT == 0:
            store(hidden_ref, hidden_out, jnp.int32(u * size // BT)).wait()
        hidden, grad = hidden_ref[at, :], total[at, :].astype(F32)
        scale = scale_ref[at, 0:1]
        unit = hidden * scale
        u_two = grad * gains_ref[1:2, :]
        gh = cot_ref[at, :].astype(F32) + scale * (u_two - unit * jnp.mean(u_two * unit, axis=1, keepdims=True))
        hidden_ref[at, :] = gh
        out(0, hidden_ref, grad_hidden_out, at).start()
        ga_ref[at, :] = gh.astype(BF16)
        gain_ref[0:1, :] += jnp.sum(grad * unit, axis=0, keepdims=True)

    def prepare(u, half):
        at = pl.ds(u * size, size)
        ga = ga_ref[at, :]
        for m in range(2):
            wide = pl.ds((2 * half + m) * 256, 256)
            numer = nn(ga, out_w[:, wide]) * (2.0 * recip_ref[at, wide])
            low = numer.astype(BF16)
            both = (numer * attn_ref[at, wide].astype(F32)).astype(BF16)
            gn_ref[at, wide] = low
            gnt_ref[wide, at] = low.T
            gd_ref[at, wide] = jnp.concatenate([nn(both[:, :128], negate), nn(both[:, 128:], negate)], axis=1).astype(BF16)
        if half:
            out(1, gn_ref, gn_out, at).start()
            out(2, gd_ref, gd_out, at).start()
            out(3, gnt_ref, gnt_out, (slice(None), at)).start()

    tasks = [(u, q) for u in range(units) for q in range(3)]
    while tasks:
        if served < line.steps():
            line.serve(jnp.int32(served))
            served += 1
        for _ in range(2):
            if tasks and (served >= line.steps() or served > 4 * tasks[0][0] + 4 + line.lags[-1] + tasks[0][1]):
                u, q = tasks.pop(0)
                if q == 0:
                    back_rows(u)
                else:
                    prepare(u, q - 1)
    first = 3 * ff
    grads_ref[first : first + value_cols, :] = nn(own_t[...], ga_ref[...]).astype(BF16)
    first = first + value_cols
    rest = grads_ref.shape[0] - first
    grads_ref[first:, :] = jnp.zeros((rest, D), BF16)
    grads_ref[first : first + 16, :] = gain_ref[...].astype(BF16)
    last = pl.ds(3 * ff, grads_ref.shape[0] - 3 * ff)
    last_store = pltpu.make_async_copy(grads_ref.at[last], grads_out.at[last], store_sem.at[blocks + 6])
    last_store.start()
    line.drain()
    out(0, hidden_ref, grad_hidden_out).wait()
    out(1, gn_ref, gn_out).wait()
    out(2, gd_ref, gd_out).wait()
    out(3, gnt_ref, gnt_out).wait()
    ffn_store.wait()
    grads_store.wait()
    last_store.wait()


def feed(tokens, cotangent, attn, recip, wide, gate_turned, down, gains, padded):
    length = tokens.shape[0]
    ff = down.shape[0]
    nv, rows = attn.shape[1], 32
    count = length // rows
    hbm = pl.BlockSpec(memory_space=pl.ANY)
    vmem = pl.BlockSpec(memory_space=pltpu.VMEM)
    return pl.pallas_call(
        functools.partial(feed_kernel, rows),
        out_shape=(
            jax.ShapeDtypeStruct((length, D), F32),
            jax.ShapeDtypeStruct((length, D), F32),
            jax.ShapeDtypeStruct((length, nv), BF16),
            jax.ShapeDtypeStruct((nv, length), BF16),
            jax.ShapeDtypeStruct((length, nv), BF16),
            jax.ShapeDtypeStruct((length, D), BF16),
            jax.ShapeDtypeStruct((padded, D), BF16),
        ),
        in_specs=[hbm] * 7 + [vmem],
        out_specs=(hbm,) * 7,
        scratch_shapes=[
            pltpu.VMEM((length, D), BF16), pltpu.VMEM((length, D), BF16), pltpu.VMEM((length, nv), BF16),
            pltpu.VMEM((D, nv), BF16), pltpu.VMEM((2, ff, D), BF16), pltpu.VMEM((ff, D), BF16), pltpu.VMEM((length, nv), F32),
            pltpu.VMEM((length, D), F32), pltpu.VMEM((length, 128), F32), pltpu.VMEM((length, D), BF16),
            pltpu.VMEM((ff, length), BF16), pltpu.VMEM((ff, length), BF16), pltpu.VMEM((ff, length), BF16),
            pltpu.VMEM((nv // 4, length), BF16), pltpu.VMEM((16, D), F32), pltpu.VMEM((length, D), BF16),
            pltpu.VMEM((length, nv), BF16), pltpu.VMEM((nv, length), BF16), pltpu.VMEM((length, nv), BF16),
            pltpu.VMEM((length, D), BF16), pltpu.VMEM((padded, D), BF16),
            pltpu.VMEM((length, D), BF16), pltpu.VMEM((length, D), BF16), pltpu.VMEM((length, D), BF16),
            pltpu.VMEM((length, D), BF16),
            pltpu.SemaphoreType.DMA((2,)), pltpu.SemaphoreType.DMA((2, count)),
            pltpu.SemaphoreType.DMA((10,)), pltpu.SemaphoreType.DMA((length // BT + 7,)),
        ],
        compiler_params=pltpu.CompilerParams(collective_id=2, has_side_effects=True, vmem_limit_bytes=60 * 2**20),
        name="feed",
    )(tokens, cotangent, attn, recip, wide, gate_turned, down, gains)


def back_kernel(
    pieces, small_pieces, bits, rows,
    pairs_in, values_in, gn_in, gnt_in, gd_in, mask_in, ffn_in, grads_in, normed_in, wide_in, tokens_in,
    total_out, sums_out, grad_out, small_out,
    q_ref, k_ref, v_ref, gn_ref, gnt_ref, gd_ref, mask_ref, normed_ref, wide_ref, tokens_ref,
    part, leaf, mid, total, work, landing, sums, small_work, small_landing, small_sums,
    qt_ref, gq_ref, gkt_ref, gvt_ref, gp_ref, gv_ref, grad_ref, gain_ref,
    line_send, line_recv, cube_send, cube_recv, small_send, small_recv, load_sem, store_sem,
):
    f = lax.axis_index("feat")
    line = LineSum(part, leaf, mid, total, line_send, line_recv, rows, (0, 3, 6))
    cube = CubeSum(work, landing, sums, cube_send, cube_recv, pieces, bits)
    small = CubeSum(small_work, small_landing, small_sums, small_send, small_recv, small_pieces, bits)
    half = HEADS * QK
    first_loads = [
        pltpu.make_async_copy(grads_in.at[pl.ds(a, n)], work.at[pl.ds(a, n)], load_sem.at[m]) for m, (a, n) in enumerate(pieces)
    ] + [pltpu.make_async_copy(ffn_in, part, load_sem.at[len(pieces)])]
    sources = [
        (pairs_in.at[:, pl.ds(0, half)], q_ref), (pairs_in.at[:, pl.ds(half, half)], k_ref), (values_in, v_ref),
        (mask_in, mask_ref), (gn_in, gn_ref), (gd_in, gd_ref), (gnt_in, gnt_ref), (normed_in, normed_ref),
        (wide_in.at[:, pl.ds(0, wide_ref.shape[1])], wide_ref), (tokens_in, tokens_ref),
    ]
    loads = [pltpu.make_async_copy(a, b, load_sem.at[len(pieces) + 1 + n]) for n, (a, b) in enumerate(sources)]
    for load in first_loads:
        load.start()
    greet(line, cube)
    for p in range(len(pieces)):
        first_loads[p].wait()
        cube.launch(p)
    for load in loads:
        load.start()
    first_loads[-1].wait()
    each(line.leaves, line.count)
    gq_ref[...] = jnp.zeros_like(gq_ref)
    for load in loads[:7]:
        load.wait()
    qt_ref[...] = q_ref[...].T

    lane = lax.broadcasted_iota(jnp.int32, (1, 128), 1)
    length = q_ref.shape[0]
    blocks = length // BT
    hb = 2
    groups = HEADS // hb
    weaver = Weaver(2.0)
    weaver.add("line", line_floors(line, 0.5), [0.0] * line.steps())
    floors, times = cube_floors(cube, 0.0)
    for p in range(len(pieces)):
        weaver.add(("cube", p), floors[p], times[p])

    def take(items):
        for name, n in items:
            if name == "line":
                line.serve(jnp.int32(n))
            elif name[0] == "cube":
                cube.advance(name[1], n)
            else:
                small.advance(name[1], n)

    for block in range(blocks):
        lo = block * BT
        below, there = pl.ds(lo, length - lo), pl.ds(lo, BT)
        plans = [weaver.unit(0.43 * (blocks - block) + 0.1) for _ in range(groups)]

        def group(g, carry):
            h = g * hb
            ql = pl.ds(pl.multiple_of(h // 8 * 128, 128), 128)
            vl = pl.ds(pl.multiple_of(g * 128, 128), 128)
            q, k, v = q_ref[below, ql], k_ref[there, ql], v_ref[there, vl]
            both = jnp.concatenate([gn_ref[below, vl], gd_ref[below, vl]], axis=1)
            mask = mask_ref[block, : length - lo, :]
            gq, turned = None, []
            for a in range(hb):
                km = jnp.where(lane // QK == lax.rem(h + a, 8), k, jnp.zeros_like(k))
                vm = jnp.where(lane // HV == a, v, jnp.zeros_like(v))
                pick = jnp.where(lane == HV * a, jnp.ones_like(v), jnp.zeros_like(v))
                t1 = nt(q, km) + 1.0
                p = (t1 * t1 + 1.0).astype(BF16) * mask
                dp = nt(both, jnp.concatenate([vm, pick], axis=1)).astype(BF16) * mask
                gs = (dp.astype(F32) * t1).astype(BF16)
                out = nn(gs, km)
                gq = out if gq is None else gq + out
                qrows = pl.ds(pl.multiple_of((h + a) * QK, QK), QK)
                vrows = pl.ds(pl.multiple_of((h + a) * HV, HV), HV)
                gkt_ref[qrows, there] = nn(qt_ref[qrows, below], gs)
                turned.append(nn(gnt_ref[vrows, below], p) * 0.5)
            gq_ref[below, ql] += gq
            gvt = jnp.concatenate(turned, axis=0)
            gvt_ref[vl, there] = gvt.astype(BF16)
            gv_ref[there, vl] = gvt.T.astype(BF16)
            for n, plan in enumerate(plans):
                if plan:
                    @pl.when(g == n)
                    def _():
                        take(plan)
            return carry

        lax.fori_loop(0, groups, group, 0)
    gp_ref[:, :half] = (gq_ref[...] * 0.25).astype(BF16)
    gp_ref[:, half:] = gkt_ref[...].T.astype(BF16)
    for load in loads[7:]:
        load.wait()

    pair_cols, value_cols = 2 * half // 4, HEADS * HV // 4
    rest = value_cols + pair_cols

    def open_small(p):
        small.launch(p)
        floors, times = cube_floors(small, 0.0)
        weaver.add(("small", p), [0.0] * len(floors[p]), times[p])

    small_work[0:value_cols, :] = nn(
        gvt_ref[pl.ds(pl.multiple_of(f * value_cols, value_cols), value_cols), :], normed_ref[...]
    ).astype(BF16)
    small_work[value_cols:rest, :] = nn(own_column(gp_ref, f, pair_cols).T, normed_ref[...]).astype(BF16)
    if len(small_pieces) > 1:
        open_small(0)
    take(weaver.unit(3.6))
    gain_ref[...] = jnp.zeros_like(gain_ref)
    for n in range(blocks):
        at = slice(n * BT, (n + 1) * BT)
        grad = nt(gp_ref[at, :], wide_ref[:, : 2 * half]) + nt(gv_ref[at, :], wide_ref[:, 2 * half :])
        grad_ref[at, :] = grad.astype(BF16)
        x = tokens_ref[at, :].astype(F32)
        scale = lax.rsqrt(jnp.mean(x * x, axis=1, keepdims=True) + EPS)
        gain_ref[0:1, :] += jnp.sum(grad * (x * scale), axis=0, keepdims=True)
        if n < blocks - 1:
            take(weaver.unit(1.4))
    grad_store = pltpu.make_async_copy(grad_ref, grad_out, store_sem.at[0])
    grad_store.start()
    small_work[rest:, :] = jnp.zeros((small_work.shape[0] - rest, D), BF16)
    small_work[rest : rest + 16, :] = gain_ref[...].astype(BF16)
    open_small(len(small_pieces) - 1)
    take(weaver.unit(1.6))
    take(weaver.until([("cube", p) for p in range(len(pieces))]))
    sums_store = pltpu.make_async_copy(sums, sums_out, store_sem.at[2])
    sums_store.start()
    take(weaver.until([("small", p) for p in range(len(small_pieces))]))
    small_store = pltpu.make_async_copy(small_sums, small_out, store_sem.at[1])
    small_store.start()
    take(weaver.until(["line"]))
    each(line.arrived, line.count)
    total_store = pltpu.make_async_copy(total, total_out, store_sem.at[3])
    total_store.start()
    line.drain()
    cube.drain()
    small.drain()
    for s in (sums_store, grad_store, small_store, total_store):
        s.wait()


def back(pairs, values, gn, gnt, gd, mask, ffn, grads, normed, wide, tokens, pieces, bits, dp_size):
    length = tokens.shape[0]
    nq, nv, rows = HEADS * QK, HEADS * HV, 32
    count = length // rows
    unit = 16 * dp_size
    first = (nv // 4 + nq // 2) // unit * unit
    small_pieces = [(0, first), (first, unit)] if first else []
    small_rows = first + unit
    need = nv // 4 + nq // 2 + 16
    if small_rows < need or not small_pieces:
        small_rows = (need + unit - 1) // unit * unit
        small_pieces = [(0, small_rows)]
    hbm = pl.BlockSpec(memory_space=pl.ANY)

    def buf(*shape, dtype=BF16):
        return pltpu.VMEM(shape, dtype)

    sems = []
    for p in (pieces, small_pieces):
        sems += [pltpu.SemaphoreType.DMA((2,)), pltpu.SemaphoreType.DMA((len(p), 2, 2 * len(bits)))]
    return pl.pallas_call(
        functools.partial(back_kernel, pieces, small_pieces, bits, rows),
        out_shape=(
            jax.ShapeDtypeStruct((length, D), BF16),
            jax.ShapeDtypeStruct(grads.shape, BF16),
            jax.ShapeDtypeStruct((length, D), BF16),
            jax.ShapeDtypeStruct((small_rows, D), BF16),
        ),
        in_specs=[hbm] * 11,
        out_specs=(hbm,) * 4,
        scratch_shapes=[
            buf(length, nq), buf(length, nq), buf(length, nv), buf(length, nv), buf(nv, length), buf(length, nv),
            buf(*mask.shape), buf(length, D), buf(D, 2 * nq + nv), buf(length, D),
            buf(length, D), buf(length, D), buf(length, D), buf(length, D),
            buf(*grads.shape), buf(*grads.shape), buf(*grads.shape),
            buf(small_rows, D), buf(small_rows, D), buf(small_rows, D),
            buf(nq, length), buf(length, nq, dtype=F32), buf(nq, length, dtype=F32), buf(nv, length), buf(length, 2 * nq), buf(length, nv),
            buf(length, D), buf(16, D, dtype=F32),
            pltpu.SemaphoreType.DMA((2,)), pltpu.SemaphoreType.DMA((2, count)), *sems,
            pltpu.SemaphoreType.DMA((len(pieces) + 11,)), pltpu.SemaphoreType.DMA((4,)),
        ],
        compiler_params=pltpu.CompilerParams(collective_id=4, has_side_effects=True, vmem_limit_bytes=62 * 2**20),
        name="back",
    )(pairs, values, gn, gnt, gd, mask, ffn, grads, normed, wide, tokens)


def update_kernel(
    rates,
    down_w, down_m, down_a, gate_w, gate_m, gate_a, out_w, out_m, out_a, value_w, value_m, value_a,
    pair_w, pair_m, pair_a, gain_w, gain_m, gain_a, big, small, hidden, total, grad_hidden, grad_normed, tokens, gains,
    mixed_o, input_o, pair_mo, pair_wo, pair_ao, value_mo, value_wo, value_ao, out_mo, out_wo, out_ao,
    gate_mo, gate_wo, gate_ao, down_mo, down_wo, down_ao, gain_mo, gain_wo, gain_ao,
):
    ff = down_w.shape[0]
    narrow = value_w.shape[1]
    pair_cols = pair_w.shape[1]

    def put(index, outs, grad, w, m, a, rate):
        moment_next, weight_next, average_next = update(w[index], grad, m[index], a[index], rate)
        outs[0][index], outs[1][index], outs[2][index] = moment_next, weight_next, average_next

    put(..., (down_mo, down_wo, down_ao), big[:ff, :].astype(F32), down_w, down_m, down_a, rates[4])
    for n in range(2):
        first = (n + 1) * ff
        put(n, (gate_mo, gate_wo, gate_ao), big[first : first + ff, :].astype(F32), gate_w, gate_m, gate_a, rates[3])
    first = 3 * ff
    put(..., (out_mo, out_wo, out_ao), big[first : first + out_w.shape[0], :].astype(F32), out_w, out_m, out_a, rates[2])
    first = first + out_w.shape[0]
    put(..., (value_mo, value_wo, value_ao), small[:narrow, :].astype(F32).T, value_w, value_m, value_a, rates[1])
    put(..., (pair_mo, pair_wo, pair_ao), small[narrow : narrow + pair_cols, :].astype(F32).T, pair_w, pair_m, pair_a, rates[0])
    gain_one = small[narrow + pair_cols : narrow + pair_cols + 16, :].astype(F32)[0:1, :]
    gain_two = big[first : first + 16, :].astype(F32)[0:1, :]
    put(slice(0, 1), (gain_mo, gain_wo, gain_ao), gain_one, gain_w, gain_m, gain_a, rates[5])
    put(slice(1, 2), (gain_mo, gain_wo, gain_ao), gain_two, gain_w, gain_m, gain_a, rates[5])

    mixed_o[...] = (hidden[...] + total[...].astype(F32)).astype(BF16)
    x = tokens[...].astype(F32)
    scale = lax.rsqrt(jnp.mean(x * x, axis=1, keepdims=True) + EPS)
    unit = x * scale
    u = grad_normed[...].astype(F32) * gains[0:1, :]
    input_o[...] = grad_hidden[...] + scale * (u - unit * jnp.mean(u * unit, axis=1, keepdims=True))


def finish(rates, weights, big, small, hidden, total, grad_hidden, grad_normed, tokens, gains):
    length = tokens.shape[0]
    steps = D // 128
    rows = length // steps
    ff = weights[0][0].shape[0]
    narrow, pair_cols = weights[3][0].shape[1], weights[4][0].shape[1]

    def cols(n):
        return pl.BlockSpec((n, 128), lambda i: (0, i))

    def tall(n):
        return pl.BlockSpec((128, n), lambda i: (i, 0))

    token = pl.BlockSpec((rows, D), lambda i: (i, 0))
    specs = [cols(ff), pl.BlockSpec((2, ff, 128), lambda i: (0, 0, i)), cols(weights[2][0].shape[0]), tall(narrow), tall(pair_cols), cols(2)]
    order = [4, 3, 2, 1, 0, 5]
    flat = [a for group in weights for a in group]
    out_shape = [jax.ShapeDtypeStruct((length, D), BF16), jax.ShapeDtypeStruct((length, D), F32)]
    out_specs = [token, token]
    for n in order:
        out_shape += [jax.ShapeDtypeStruct(weights[n][0].shape, F32)] * 3
        out_specs += [specs[n]] * 3
    in_specs = [specs[n] for n in range(6) for _ in range(3)]
    in_specs += [cols(big.shape[0]), cols(small.shape[0])] + [token] * 5 + [pl.BlockSpec((2, D), lambda i: (0, 0))]
    return pl.pallas_call(
        functools.partial(update_kernel, rates),
        grid=(steps,),
        out_shape=out_shape,
        in_specs=in_specs,
        out_specs=out_specs,
        compiler_params=pltpu.CompilerParams(vmem_limit_bytes=62 * 2**20),
        name="finish",
    )(*flat, big, small, hidden, total, grad_hidden, grad_normed, tokens, gains)


def update(weight, grad_total, moment, average, rate):
    moment_next = MOMENTUM * moment + grad_total
    weight_next = weight - rate * (grad_total + MOMENTUM * moment_next)
    average_next = average + (weight_next - average) / STEP
    return (moment_next, weight_next, average_next)


def on_device(
    tokens,
    cotangent,
    doc_starts,
    queries_keys,
    value_weight,
    out_weight,
    gate_up,
    down_weight,
    norm_gains,
    queries_moment,
    value_moment,
    out_moment,
    gate_moment,
    down_moment,
    gains_moment,
    queries_average,
    value_average,
    out_average,
    gate_average,
    down_average,
    gains_average,
):
    total_tokens = float(tokens.shape[0] * lax.axis_size("dp"))
    dp_size = lax.axis_size("dp")
    ff = down_weight.shape[0]
    gate_turned = gate_up.transpose(0, 2, 1)
    normed_one, pairs, values, wide, gate_low, down_low, attn_low, recip, mask = front(
        doc_starts, tokens, norm_gains, queries_keys, value_weight, out_weight, gate_turned, down_weight
    )
    padded, pieces, bits = cube_shape(3 * ff + out_weight.shape[0] + 16, dp_size, 4)
    hidden_one, grad_hidden, grad_numer, grad_numer_turned, grad_denom, ffn_part, big = feed(
        tokens, cotangent, attn_low, recip, wide, gate_low, down_low, norm_gains, padded
    )
    total, big, grad_normed_one, small = back(
        pairs, values, grad_numer, grad_numer_turned, grad_denom, mask, ffn_part, big, normed_one, wide, tokens,
        pieces, bits, dp_size,
    )
    rates = (
        (D * total_tokens) ** (-0.5),
        (D * total_tokens) ** (-0.5),
        (HEADS * HV * total_tokens) ** (-0.5),
        (D * total_tokens) ** (-0.5),
        (FF * total_tokens) ** (-0.5),
        0.2 * total_tokens ** (-0.5),
    )
    weights = (
        (down_weight, down_moment, down_average),
        (gate_turned, gate_moment.transpose(0, 2, 1), gate_average.transpose(0, 2, 1)),
        (out_weight, out_moment, out_average),
        (value_weight, value_moment, value_average),
        (queries_keys, queries_moment, queries_average),
        (norm_gains, gains_moment, gains_average),
    )
    outs = list(finish(rates, weights, big, small, hidden_one, total, grad_hidden, grad_normed_one, tokens, norm_gains))
    outs[11:14] = [o.transpose(0, 2, 1) for o in outs[11:14]]
    return tuple(outs)


def solution(mesh):
    in_specs = (
        P("dp", None),
        P("dp", None),
        P("dp", None),
        P(None, "feat"),
        P(None, "feat"),
        P("feat", None),
        P(None, None, "feat"),
        P("feat", None),
        P(),
        P(None, "feat"),
        P(None, "feat"),
        P("feat", None),
        P(None, None, "feat"),
        P("feat", None),
        P(),
        P(None, "feat"),
        P(None, "feat"),
        P("feat", None),
        P(None, None, "feat"),
        P("feat", None),
        P(),
    )
    out_specs = (
        P("dp", None),
        P("dp", None),
        P(None, "feat"),
        P(None, "feat"),
        P(None, "feat"),
        P(None, "feat"),
        P(None, "feat"),
        P(None, "feat"),
        P("feat", None),
        P("feat", None),
        P("feat", None),
        P(None, None, "feat"),
        P(None, None, "feat"),
        P(None, None, "feat"),
        P("feat", None),
        P("feat", None),
        P("feat", None),
        P(),
        P(),
        P(),
    )
    return jax.shard_map(
        on_device, mesh=mesh, in_specs=in_specs, out_specs=out_specs, check_vma=False
    )
```

```python
import functools
import jax
import jax.numpy as jnp
from jax import lax
from jax.experimental import pallas as pl
from jax.experimental.pallas import tpu as pltpu
from jax.sharding import PartitionSpec as P

D = 1024
HEADS = 16
QK = 16
HV = 64
FF = 2752
STEP = 4
BT = 256
F32 = jnp.float32
BF16 = jnp.bfloat16

MESH = pl.DeviceIdType.MESH
EPS = 1e-06
MOMENTUM = 0.9


def nt(a, b):
    return lax.dot_general(a, b, (((1,), (1,)), ((), ())), preferred_element_type=F32)


def nn(a, b):
    return lax.dot_general(a, b, (((1,), (0,)), ((), ())), preferred_element_type=F32)


class LineSum:
    def __init__(self, part, leaf, mid, total, send, recv, rows, lags=(0, 2, 4)):
        self.part, self.leaf, self.mid, self.total, self.send, self.recv = part, leaf, mid, total, send, recv
        self.rows, self.lags = rows, lags
        self.count = part.shape[0] // rows
        self.dp, self.f = lax.axis_index("dp"), lax.axis_index("feat")

    def place(self, c):
        odd = lax.rem(c, 2)
        return self.f + odd * (3 - 2 * self.f), 1 - 2 * odd

    def copy(self, c, src, dst, kind, slot, to):
        at = pl.ds(pl.multiple_of(c * self.rows, self.rows), self.rows)
        return pltpu.make_async_remote_copy(
            src_ref=src.at[at], dst_ref=dst.at[at], send_sem=self.send.at[slot], recv_sem=self.recv.at[min(kind, 1), c],
            device_id=(self.dp, to), device_id_type=MESH)

    def leaves(self, c):
        p, up = self.place(c)

        @pl.when(p == 3)
        def _():
            self.copy(c, self.part, self.leaf, 0, 0, self.f - up).start()

        @pl.when(p == 0)
        def _():
            self.copy(c, self.part, self.leaf, 0, 0, self.f + up).start()

    def middle(self, c):
        p, up = self.place(c)
        at = pl.ds(pl.multiple_of(c * self.rows, self.rows), self.rows)

        @pl.when(p == 2)
        def _():
            self.copy(c, self.part, self.leaf, 0, 0, self.f).wait_recv()
            self.part[at, :] = self.part[at, :] + self.leaf[at, :]
            self.copy(c, self.part, self.mid, 1, 0, self.f - up).start()

    def root(self, c):
        p, up = self.place(c)
        at = pl.ds(pl.multiple_of(c * self.rows, self.rows), self.rows)

        @pl.when(p == 1)
        def _():
            self.copy(c, self.part, self.leaf, 0, 0, self.f).wait_recv()
            self.copy(c, self.part, self.mid, 1, 0, self.f).wait_recv()
            self.total[at, :] = self.part[at, :] + self.leaf[at, :] + self.mid[at, :]
            self.copy(c, self.total, self.total, 2, 1, self.f + up).start()
            self.copy(c, self.total, self.total, 2, 0, self.f - up).start()

    def onward(self, c):
        p, up = self.place(c)

        @pl.when(p == 2)
        def _():
            self.copy(c, self.total, self.total, 2, 0, self.f).wait_recv()
            self.copy(c, self.total, self.total, 2, 1, self.f + up).start()

    def serve(self, i):
        for lag, act in zip(self.lags, (self.middle, self.root, self.onward)):
            c = i - lag

            @pl.when(jnp.logical_and(c >= 0, c < self.count))
            def _():
                act(c)

    def steps(self):
        return self.count + self.lags[-1]

    def arrived(self, c):
        p, up = self.place(c)

        @pl.when(jnp.logical_or(p == 0, p == 3))
        def _():
            self.copy(c, self.total, self.total, 2, 0, self.f).wait_recv()

    def drain(self):
        def all_sent(slot):
            pltpu.make_async_remote_copy(
                src_ref=self.part, dst_ref=self.part, send_sem=self.send.at[slot], recv_sem=self.recv.at[0, 0],
                device_id=(self.dp, self.f), device_id_type=MESH,
            ).wait_send()

        all_sent(0)

        @pl.when(jnp.logical_or(self.f == 1, self.f == 2))
        def _():
            all_sent(1)


class CubeSum:
    def __init__(self, work, recv, out, send_sem, recv_sem, pieces, bits):
        self.work, self.recv, self.out, self.send_sem, self.recv_sem = work, recv, out, send_sem, recv_sem
        self.pieces, self.nb = pieces, len(bits)
        self.dp, self.f = lax.axis_index("dp"), lax.axis_index("feat")
        self.orders = [list(bits), [bits[0]] + list(bits[1:])[::-1]]
        self.bits = bits

    def partner(self, bit):
        return self.dp + bit - 2 * bit * lax.rem(self.dp // bit, 2)

    def lanes(self, colour):
        half = self.work.shape[1] // 2
        return pl.ds(colour * half, half)

    def segment(self, piece, colour, k):
        first, rows = self.pieces[piece]
        start = first
        for bit in self.orders[colour][:k]:
            rows = rows // 2
            start = start + rows * lax.rem(self.dp // bit, 2)
        return start, rows

    def at(self, start, rows):
        return pl.ds(pl.multiple_of(start, 16), rows)

    def halve(self, piece, colour, k):
        start, rows = self.segment(piece, colour, k)
        rows = rows // 2
        bit = self.orders[colour][k]
        own = lax.rem(self.dp // bit, 2)
        first, whole = self.pieces[piece]
        landing = first + whole - 2 * rows
        return pltpu.make_async_remote_copy(
            src_ref=self.work.at[self.at(start + rows * (1 - own), rows), self.lanes(colour)],
            dst_ref=self.recv.at[self.at(landing, rows), self.lanes(colour)],
            send_sem=self.send_sem.at[0], recv_sem=self.recv_sem.at[piece, colour, k],
            device_id=(self.partner(bit), self.f), device_id_type=MESH)

    def add(self, piece, colour, k):
        start, rows = self.segment(piece, colour, k + 1)
        first, whole = self.pieces[piece]
        landing = first + whole - 2 * rows
        target = self.out if k + 1 == self.nb else self.work
        mine = self.work[self.at(start, rows), self.lanes(colour)]
        target[self.at(start, rows), self.lanes(colour)] = mine + self.recv[self.at(landing, rows), self.lanes(colour)]

    def double(self, piece, colour, k):
        start, rows = self.segment(piece, colour, k + 1)
        bit = self.orders[colour][k]
        at = self.at(start, rows)
        slot = 2 * self.nb - 1 - k
        return pltpu.make_async_remote_copy(
            src_ref=self.out.at[at, self.lanes(colour)], dst_ref=self.out.at[at, self.lanes(colour)],
            send_sem=self.send_sem.at[1], recv_sem=self.recv_sem.at[piece, colour, slot],
            device_id=(self.partner(bit), self.f), device_id_type=MESH)

    def launch(self, piece):
        for colour in range(2):
            self.halve(piece, colour, 0).start()

    def advance(self, piece, t):
        for colour in range(2):
            if t < self.nb:
                self.halve(piece, colour, t).wait_recv()
                self.add(piece, colour, t)
                if t + 1 < self.nb:
                    self.halve(piece, colour, t + 1).start()
                else:
                    self.double(piece, colour, self.nb - 1).start()
            else:
                k = 2 * self.nb - 1 - t
                self.double(piece, colour, k).wait_recv()
                if k > 0:
                    self.double(piece, colour, k - 1).start()

    def drain(self):
        rows = self.work.shape[0]
        sent = pl.ds(0, rows - rows // 2**self.nb)
        for n, ref in enumerate((self.work, self.out)):
            pltpu.make_async_remote_copy(
                src_ref=ref.at[sent], dst_ref=ref.at[sent], send_sem=self.send_sem.at[n], recv_sem=self.recv_sem.at[0, 0, 0],
                device_id=(self.dp, self.f), device_id_type=MESH,
            ).wait_send()


def split_rows(rows, unit, count):
    units = rows // unit
    out, first = [], 0
    for n in range(count):
        take = (units * (n + 1) // count - units * n // count) * unit
        out.append((first, take))
        first += take
    return [p for p in out if p[1]]


def own_column(ref, f, width):
    return ref[:, pl.ds(pl.multiple_of(f * width, width), width)]


def greet(line, cube):
    sem = pltpu.get_barrier_semaphore()
    f = lax.axis_index("feat")
    count = jnp.int32(0)
    if cube is not None:
        for bit in cube.bits:
            pl.semaphore_signal(sem, inc=1, device_id=(cube.partner(bit), f), device_id_type=MESH)
        count = count + len(cube.bits)
    if line is not None:
        @pl.when(f > 0)
        def _():
            pl.semaphore_signal(sem, inc=1, device_id=(line.dp, f - 1), device_id_type=MESH)

        @pl.when(f < 3)
        def _():
            pl.semaphore_signal(sem, inc=1, device_id=(line.dp, f + 1), device_id_type=MESH)
        count = count + jnp.where(f > 0, 1, 0) + jnp.where(f < 3, 1, 0)
    pl.semaphore_wait(sem, count)


def each(act, n):
    def body(c, carry):
        act(c)
        return carry

    lax.fori_loop(0, n, body, 0)


def cube_shape(rows, dp_size, count):
    unit = 16 * dp_size
    padded = (rows + unit - 1) // unit * unit
    bits = tuple(2**n for n in range(dp_size.bit_length() - 1))
    return padded, split_rows(padded, unit, count), bits


class Weaver:
    def __init__(self, now, margin=0.5, cost=0.35):
        self.now, self.margin, self.cost = now, margin, cost
        self.streams = {}

    def add(self, name, floors, leads):
        self.streams[name] = [list(floors), list(leads), 0, self.now]

    def ready(self, name):
        floors, leads, n, last = self.streams[name]
        return max(floors[n], last + leads[n])

    def open(self):
        return [name for name, s in self.streams.items() if s[2] < len(s[0])]

    def take(self, name):
        stream = self.streams[name]
        self.now = max(self.now, self.ready(name)) + self.cost
        stream[2] += 1
        stream[3] = self.now
        return name, stream[2] - 1

    def unit(self, length):
        self.now += length
        out = []
        while self.open():
            name = min(self.open(), key=self.ready)
            if self.ready(name) > self.now - self.margin:
                break
            out.append(self.take(name))
        return out

    def until(self, names):
        out = []
        while any(name in names for name in self.open()):
            out.append(self.take(min(self.open(), key=self.ready)))
        return out


def line_floors(line, start):
    pace = line.rows * line.part.shape[1] * 2 / 40e3
    return [start + pace * (n + 1) + 3.0 for n in range(line.steps())]


def cube_floors(cube, start, lag=3.0):
    count = 2 * cube.nb
    ends, floors, times = [start] * len(cube.pieces), [[] for _ in cube.pieces], [[] for _ in cube.pieces]
    for t in range(count):
        near = t in (0, count - 1)
        share = 2 ** (min(t, count - 1 - t) + 1)
        busy = max(ends) if t not in (0, 1, count - 1) else start
        for p, (_, rows) in enumerate(cube.pieces):
            size = rows / share * 1024
            own = 2 * size / 430e3 if near else size / 30e3
            begin = ends[p] + (lag + 0.3 if t else 0.0)
            busy = max(busy, begin) + own
            ends[p] = busy
            floors[p].append(busy + lag)
            times[p].append(own + lag)
    return floors, times


def front_kernel(
    bits, starts_ref, tokens_in, gains_ref, pair_ref, value_ref, out_ref, gate_in, down_in,
    normed_out, pairs_out, values_out, wide_out, gate_out, down_out, attn_out, recip_out, mask_out,
    thin_ref, thick_ref, turned_ref, tokens_ref, gate_f32, down_f32,
    normed_ref, pairs_ref, values_ref, wide_ref, gate_ref, down_ref, attn_ref, recip_ref, mask_ref, acc_ref,
    send_sem, recv_sem, load_sem, store_sem,
):
    dp = lax.axis_index("dp")
    f = lax.axis_index("feat")
    slices = lax.axis_size("feat")
    last = 3
    pieces = 2 ** len(bits)
    j = lax.rem(dp, pieces)
    base = dp - j
    pair_cols, value_cols = pair_ref.shape[1], value_ref.shape[1]
    pairs_wide, values_wide = slices * pair_cols, slices * value_cols
    rows = pair_ref.shape[0] // pieces
    length = tokens_ref.shape[0]
    blocks = length // BT
    loads = [
        pltpu.make_async_copy(a, b, load_sem.at[n])
        for n, (a, b) in enumerate([(tokens_in, tokens_ref), (gate_in, gate_f32), (down_in, down_f32)])
    ]
    loads[0].start()

    def flip(k, bit):
        return k + bit - 2 * bit * lax.rem(k // bit, 2)

    colour_bits = [list(bits[1:]) + [bits[0]], list(bits[1:])[::-1] + [bits[0]]]

    def place(k, colour):
        return sum(k // bit % 2 * 2**n for n, bit in enumerate(colour_bits[colour]))

    def cast(k):
        at = pl.ds(pl.multiple_of(k * rows, rows), rows)
        pair = pair_ref[at, :].astype(BF16)
        thick = value_ref[at, :].astype(BF16)
        turned = out_ref[:, at].T.astype(BF16)
        for colour in range(2):
            part = slice(colour * rows // 2, (colour + 1) * rows // 2)
            thin_ref[colour, place(k, colour), 0] = pair[part]
            thick_ref[colour, place(k, colour), 0] = thick[part]
            turned_ref[colour, place(k, colour), 0] = turned[part]

    cast(j)
    order = [
        jnp.where(f == 0, 1, f - 1),
        jnp.where(f < 2, 2, jnp.where(f == 2, 3, 1)),
        jnp.where(f < 2, 3, 0),
    ]
    barrier = pltpu.get_barrier_semaphore()
    for bit in bits:
        pl.semaphore_signal(barrier, inc=1, device_id=(base + flip(j, bit), f), device_id_type=MESH)
    for z in order:
        pl.semaphore_signal(barrier, inc=1, device_id=(dp, z), device_id_type=MESH)
    pl.semaphore_wait(barrier, len(bits) + last)

    bufs = (thin_ref, thick_ref, turned_ref)
    here = (dp, f)

    def copy(wave, source, target, colour, kind, device, r=None):
        group = 0 if r is None or wave != 1 else r - 1
        return pltpu.make_async_remote_copy(
            src_ref=source, dst_ref=target, send_sem=send_sem.at[wave], recv_sem=recv_sem.at[wave, colour, kind, group],
            device_id=device, device_id_type=MESH,
        )

    for wave in range(3):
        for z in order:
            for colour in range(2):
                at = bufs[wave].at[colour, place(j, colour)]
                r = lax.rem(f - z + slices, slices)
                copy(wave, at.at[0], at.at[r], colour, 0, (dp, z), r).start()

    def held(wave, k, colour, n, r):
        first = place(k, colour) // 2**n * 2**n
        which = pl.ds(1, last) if r is None else pl.ds(r, 1)
        return bufs[wave].at[colour, pl.ds(first, 2**n), which]

    def start_step(wave, n, r):
        for colour in range(2):
            at = held(wave, j, colour, n, r)
            copy(wave, at, at, colour, 1 + n, (base + flip(j, colour_bits[colour][n]), f), r).start()

    def arrive(wave, a=None):
        r = None if a is None else relative[a]
        for colour in range(2):
            at = held(wave, j, colour, 0, r)
            copy(wave, at, at, colour, 0, here, r).wait_recv()
        start_step(wave, 0, r)

    def step(wave, n, a=None):
        r = None if a is None else relative[a]
        for colour in range(2):
            at = held(wave, flip(j, colour_bits[colour][n]), colour, n, r)
            copy(wave, at, at, colour, 1 + n, here, r).wait_recv()
        if n + 1 < len(bits):
            start_step(wave, n + 1, r)

    relative = [lax.rem(z - f + slices, slices) for z in order]

    def put(wave, r, lanes):
        for k in range(pieces):
            for colour in range(2):
                first = k * rows + colour * rows // 2
                wide_ref[first : first + rows // 2, lanes] = bufs[wave][colour, place(k, colour), r]

    def owner(r):
        return lax.rem(f + r, slices)

    def put_thin(r):
        put(0, r, pl.ds(pl.multiple_of(owner(r) * pair_cols, pair_cols), pair_cols))

    def lanes(first, z):
        return pl.ds(pl.multiple_of(first + z * value_cols, 128), value_cols)

    def store(n, source, target, at=None):
        if at is not None:
            source, target = source.at[:, at], target.at[:, at]
        return pltpu.make_async_copy(source, target, store_sem.at[n])

    def use(r):
        z = owner(r)
        put(1, r, lanes(pairs_wide, z))

        def some(n, carry):
            at = pl.ds(pl.multiple_of(n * BT, BT), BT)
            values_ref[at, lanes(0, z)] = nn(normed_ref[at, :], wide_ref[:, lanes(pairs_wide, z)]).astype(BF16)
            return carry

        lax.fori_loop(0, blocks, some, 0)
        store(5, wide_ref, wide_out, lanes(pairs_wide, z)).start()
        store(6, values_ref, values_out, lanes(0, z)).start()

    def put_turned(r):
        at = lanes(pairs_wide + values_wide, owner(r))
        put(2, r, at)
        store(5, wide_ref, wide_out, at).start()

    def cast_rest(n, carry):
        cast(lax.rem(j + n, pieces))
        return carry

    lax.fori_loop(1, pieces, cast_rest, 0)
    loads[0].wait()
    loads[1].start()
    loads[2].start()

    def norm(n, carry):
        at = pl.ds(pl.multiple_of(n * BT, BT), BT)
        x = tokens_ref[at, :].astype(F32)
        scale = lax.rsqrt(jnp.mean(x * x, axis=1, keepdims=True) + EPS)
        normed_ref[at, :] = (x * scale * gains_ref[0:1, :]).astype(BF16)
        return carry

    lax.fori_loop(0, blocks, norm, 0)
    store(0, normed_ref, normed_out).start()
    put_thin(0)
    arrive(0)
    use(0)
    step(0, 0)

    begin = jnp.zeros((length, 1), jnp.int32)
    position = lax.broadcasted_iota(jnp.int32, (length, 1), 0)
    for n in range(starts_ref.shape[1]):
        begin = jnp.where(starts_ref[0, n] <= position, jnp.maximum(begin, starts_ref[0, n]), begin)
    for n in range(blocks):
        rest = length - n * BT
        s = n * BT + lax.broadcasted_iota(jnp.int32, (rest, BT), 1)
        keep = jnp.logical_and(s <= position[n * BT :], s >= begin[n * BT :])
        mask_ref[n, :rest, :] = keep.astype(F32).astype(BF16)
        if n:
            mask_ref[n, rest:, :] = jnp.zeros((n * BT, BT), BF16)
    store(1, mask_ref, mask_out).start()
    def cast_all(source, target):
        def go(m, carry):
            at = pl.ds(pl.multiple_of(m * 16, 16), 16)
            target[at, :] = source[at, :].astype(BF16)
            return carry

        lax.fori_loop(0, source.shape[0] // 16, go, 0)

    step(0, 1)
    arrive(1, 0)
    arrive(1, 1)
    put_turned(0)
    loads[1].wait()
    loads[2].wait()
    cast_all(gate_f32.at[0], gate_ref.at[0])
    step(0, 2)
    step(1, 0, 0)
    arrive(1, 2)
    step(1, 0, 1)
    for r in range(1, slices):
        put_thin(r)

    half = pairs_wide // 2

    def project_pairs(n, carry):
        at = pl.ds(pl.multiple_of(n * BT, BT), BT)
        pairs = nn(normed_ref[at, :], wide_ref[:, :pairs_wide]).astype(BF16)
        pairs_ref[at, :half] = pairs[:, :half] * jnp.bfloat16(0.25)
        pairs_ref[at, half:] = pairs[:, half:]
        return carry

    lax.fori_loop(0, blocks, project_pairs, 0)
    store(4, pairs_ref, pairs_out).start()
    store(5, wide_ref, wide_out, pl.ds(0, pairs_wide)).start()

    lane = lax.broadcasted_iota(jnp.int32, (1, 128), 1)
    def cast_last():
        cast_all(down_f32, down_ref)
        store(2, gate_ref, gate_out).start()
        store(3, down_ref, down_out).start()

    def put_others():
        for r in range(1, slices):
            put_turned(r)

    def cast_up():
        cast_all(gate_f32.at[1], gate_ref.at[1])

    events = {
        1: [(step, 1, 1, 0), (step, 1, 0, 2), (arrive, 2)],
        2: [(cast_up,), (step, 1, 1, 1), (step, 1, 2, 0), (use, relative[0])],
        3: [(step, 1, 1, 2), (step, 2, 0)],
        4: [(step, 1, 2, 1), (use, relative[1])],
        5: [(cast_last,), (step, 2, 1)],
        6: [(step, 1, 2, 2), (use, relative[2])],
        7: [(step, 2, 2), (put_others,)],
    }

    def unit(n, carry):
        for at, acts in events.items():
            @pl.when(n == at)
            def _():
                for act in acts:
                    act[0](*act[1:])
        a = n // 2
        z = jnp.where(a == 0, f, jnp.where(a == 1, order[0], jnp.where(a == 2, order[1], order[2])))
        pair = 2 * z + lax.rem(n, 2)
        vl = pl.ds(pl.multiple_of(pair * 128, 128), 128)
        ql = pl.ds(pl.multiple_of(pair // 4 * 128, 128), 128)
        kl = pl.ds(pl.multiple_of(half + pair // 4 * 128, 128), 128)
        for block in range(blocks):
            first = block * BT
            below, there = pl.ds(first, length - first), pl.ds(first, BT)
            q, k, v = pairs_ref[below, ql], pairs_ref[there, kl], values_ref[there, vl]
            mask = mask_ref[block, : length - first, :]
            for m in range(2):
                own = lane // QK == lax.rem(2 * pair + m, 8)
                t1 = nt(q, jnp.where(own, k, jnp.zeros_like(k))) + 1.0
                p = (t1 * t1 + 1.0).astype(BF16) * mask
                out = nn(p, jnp.where(lane // HV == m, v, jnp.ones_like(v)))
                if block:
                    acc_ref[m, below, :] += out
                else:
                    acc_ref[m] = out
        one, two = acc_ref[0], acc_ref[1]
        numer = jnp.where(lane < HV, one, two)
        recip = 1.0 / pltpu.roll(jnp.where(lane < HV, two, one), HV, 1)
        attn_ref[:, vl] = (numer * recip).astype(BF16)
        recip_ref[:, vl] = recip
        store(7, attn_ref, attn_out, vl).start()
        store(8, recip_ref, recip_out, vl).start()
        return carry

    lax.fori_loop(0, 2 * slices, unit, 0)
    for wave in range(3):
        at = bufs[wave].at[:, :, pl.ds(0, last)]
        copy(wave, at, at, 0, 0, here).wait_send()
    for n, (source, target) in enumerate([
        (normed_ref, normed_out), (mask_ref, mask_out), (gate_ref, gate_out), (down_ref, down_out), (pairs_ref, pairs_out),
        (wide_ref, wide_out), (values_ref, values_out), (attn_ref, attn_out), (recip_ref, recip_out),
    ]):
        store(n, source, target).wait()


def front(starts, tokens, gains, pair_w, value_w, out_w, gate_turned, down):
    length = tokens.shape[0]
    ff = down.shape[0]
    slices = 4
    pair_cols, value_cols = pair_w.shape[1], value_w.shape[1]
    bits = (1, 2, 4)
    hbm = pl.BlockSpec(memory_space=pl.ANY)
    vmem = pl.BlockSpec(memory_space=pltpu.VMEM)
    shapes = [
        ((length, D), BF16),
        ((length, slices * pair_cols), BF16),
        ((length, slices * value_cols), BF16),
        ((D, slices * (pair_cols + 2 * value_cols)), BF16),
        ((2, ff, D), BF16),
        ((ff, D), BF16),
        ((length, slices * value_cols), BF16),
        ((length, slices * value_cols), F32),
        ((length // BT, length, BT), BF16),
    ]
    return pl.pallas_call(
        functools.partial(front_kernel, bits),
        out_shape=tuple(jax.ShapeDtypeStruct(*s) for s in shapes),
        in_specs=[pl.BlockSpec(memory_space=pltpu.SMEM), hbm] + [vmem] * 4 + [hbm] * 2,
        out_specs=(hbm,) * 9,
        scratch_shapes=[
            pltpu.VMEM((2, 8, slices, D // 16, pair_cols), BF16),
            pltpu.VMEM((2, 8, slices, D // 16, value_cols), BF16),
            pltpu.VMEM((2, 8, slices, D // 16, value_cols), BF16),
            pltpu.VMEM((length, D), BF16),
            pltpu.VMEM((2, ff, D), F32),
            pltpu.VMEM((ff, D), F32),
        ]
        + [pltpu.VMEM(*s) for s in shapes]
        + [
            pltpu.VMEM((2, length, 128), F32),
            pltpu.SemaphoreType.DMA((3,)),
            pltpu.SemaphoreType.DMA((3, 2, 4, 3)),
            pltpu.SemaphoreType.DMA((3,)),
            pltpu.SemaphoreType.DMA((9,)),
        ],
        compiler_params=pltpu.CompilerParams(collective_id=1, has_side_effects=True, vmem_limit_bytes=60 * 2**20),
        name="front",
    )(starts, tokens, gains, pair_w, value_w, out_w, gate_turned, down)


def feed_kernel(
    rows, tokens_in, cot_in, attn_in, recip_in, wide_in, gate_in, down_in, gains_ref,
    hidden_out, grad_hidden_out, gn_out, gnt_out, gd_out, ffn_out, grads_out,
    tokens_ref, cot_ref, attn_ref, out_w, gate_ref, down_ref, recip_ref,
    hidden_ref, scale_ref, normed_ref, product_t, gate_t, up_t, own_t, gain_ref, ga_ref, gn_ref, gnt_ref, gd_ref, ffn_ref, grads_ref,
    part, leaf, mid, total, send, recv, load_sem, store_sem,
):
    f = lax.axis_index("feat")
    line = LineSum(part, leaf, mid, total, send, recv, rows, (0, 3, 6))
    length = tokens_ref.shape[0]
    ff = down_ref.shape[0]
    value_cols = own_t.shape[0]
    blocks = length // BT
    first_out = wide_in.shape[1] - attn_ref.shape[1]
    top, others = pl.ds(0, BT), pl.ds(BT, length - BT)
    pairs = [
        (attn_in.at[top], attn_ref.at[top]), (wide_in.at[:, pl.ds(first_out, attn_ref.shape[1])], out_w),
        (tokens_in.at[top], tokens_ref.at[top]), (gate_in, gate_ref), (cot_in.at[top], cot_ref.at[top]), (down_in, down_ref),
        (attn_in.at[others], attn_ref.at[others]), (tokens_in.at[others], tokens_ref.at[others]),
        (cot_in.at[others], cot_ref.at[others]), (recip_in, recip_ref),
    ]
    loads = [pltpu.make_async_copy(a, b, load_sem.at[n]) for n, (a, b) in enumerate(pairs)]
    for load in loads[:6]:
        load.start()
    greet(line, None)
    for load in loads[:6]:
        load.wait()
    for load in loads[6:]:
        load.start()

    def store(source, target, n):
        at = pl.ds(pl.multiple_of(n * BT, BT), BT)
        return pltpu.make_async_copy(source.at[at], target.at[at], store_sem.at[n])

    def block(b, carry):
        at = pl.ds(pl.multiple_of(b * BT, BT), BT)
        turn = 4 * (b - 1)

        @pl.when(b == 1)
        def _():
            for load in loads[6:9]:
                load.wait()

        hidden = tokens_ref[at, :].astype(F32) + nt(attn_ref[at, :], out_w[...])
        hidden_ref[at, :] = hidden
        store(hidden_ref, hidden_out, b).start()
        scale = lax.rsqrt(jnp.mean(hidden * hidden, axis=1, keepdims=True) + EPS)
        scale_ref[at, :] = jnp.broadcast_to(scale, (BT, 128))
        normed = (hidden * scale * gains_ref[1:2, :]).astype(BF16)
        normed_ref[at, :] = normed
        line.serve(turn)
        gate = nt(normed, gate_ref[0])
        up = nt(normed, gate_ref[1])
        line.serve(turn + 1)
        back = nt(cot_ref[at, :], down_ref[...])
        sig = 1.0 / (1.0 + jnp.exp(-gate))
        active = gate * sig
        slope = sig * (1.0 + gate * (1.0 - sig))
        product = (active * up).astype(BF16)
        grad_gate = (back * up * slope).astype(BF16)
        grad_up = (back * active).astype(BF16)
        line.serve(turn + 2)
        part[at, :] = (nn(grad_gate, gate_ref[0]) + nn(grad_up, gate_ref[1])).astype(BF16)

        def out(c, carry):
            line.leaves(b * (BT // rows) + c)
            return carry

        lax.fori_loop(0, BT // rows, out, 0)
        ffn_ref[at, :] = nn(product, down_ref[...]).astype(BF16)
        product_t[:, at] = product.T
        gate_t[:, at] = grad_gate.T
        up_t[:, at] = grad_up.T
        line.serve(turn + 3)
        return carry

    lax.fori_loop(0, blocks, block, 0)
    served = 4 * (blocks - 1)
    gain_ref[...] = jnp.zeros_like(gain_ref)
    chunks = []
    at = 0
    while at < ff:
        chunks.append((at, min(176, ff - at)))
        at += chunks[-1][1]
    for n, (turned, right) in enumerate([(product_t, cot_ref), (gate_t, normed_ref), (up_t, normed_ref)]):
        for first, size in chunks:
            at = slice(n * ff + first, n * ff + first + size)
            grads_ref[at, :] = nn(turned[first : first + size, :], right[...]).astype(BF16)
            line.serve(jnp.int32(served))
            served += 1
    ffn_store = pltpu.make_async_copy(ffn_ref, ffn_out, store_sem.at[blocks])
    ffn_store.start()
    grads_store = pltpu.make_async_copy(
        grads_ref.at[pl.ds(0, 3 * ff)], grads_out.at[pl.ds(0, 3 * ff)], store_sem.at[blocks + 1]
    )
    grads_store.start()
    own_t[...] = own_column(attn_ref, f, value_cols).T
    loads[-1].wait()
    same = lax.broadcasted_iota(jnp.int32, (128, 128), 0) // HV == lax.broadcasted_iota(jnp.int32, (128, 128), 1) // HV
    negate = jnp.where(same, -1.0, 0.0).astype(BF16)
    size = 4 * rows
    units = length // size

    def out(n, source, target, at=None):
        if at is not None:
            source, target = source.at[at], target.at[at]
        return pltpu.make_async_copy(source, target, store_sem.at[blocks + 2 + n])

    def back_rows(u):
        at = pl.ds(u * size, size)
        for c in range(4):
            line.arrived(jnp.int32(4 * u + c))
        if u * size % BT == 0:
            store(hidden_ref, hidden_out, jnp.int32(u * size // BT)).wait()
        hidden, grad = hidden_ref[at, :], total[at, :].astype(F32)
        scale = scale_ref[at, 0:1]
        unit = hidden * scale
        u_two = grad * gains_ref[1:2, :]
        gh = cot_ref[at, :].astype(F32) + scale * (u_two - unit * jnp.mean(u_two * unit, axis=1, keepdims=True))
        hidden_ref[at, :] = gh
        out(0, hidden_ref, grad_hidden_out, at).start()
        ga_ref[at, :] = gh.astype(BF16)
        gain_ref[0:1, :] += jnp.sum(grad * unit, axis=0, keepdims=True)

    def prepare(u, half):
        at = pl.ds(u * size, size)
        ga = ga_ref[at, :]
        for m in range(2):
            wide = pl.ds((2 * half + m) * 256, 256)
            numer = nn(ga, out_w[:, wide]) * (2.0 * recip_ref[at, wide])
            low = numer.astype(BF16)
            both = (numer * attn_ref[at, wide].astype(F32)).astype(BF16)
            gn_ref[at, wide] = low
            gnt_ref[wide, at] = low.T
            gd_ref[at, wide] = jnp.concatenate([nn(both[:, :128], negate), nn(both[:, 128:], negate)], axis=1).astype(BF16)
        if half:
            out(1, gn_ref, gn_out, at).start()
            out(2, gd_ref, gd_out, at).start()
            out(3, gnt_ref, gnt_out, (slice(None), at)).start()

    tasks = [(u, q) for u in range(units) for q in range(3)]
    while tasks:
        if served < line.steps():
            line.serve(jnp.int32(served))
            served += 1
        for _ in range(2):
            if tasks and (served >= line.steps() or served > 4 * tasks[0][0] + 4 + line.lags[-1] + tasks[0][1]):
                u, q = tasks.pop(0)
                if q == 0:
                    back_rows(u)
                else:
                    prepare(u, q - 1)
    first = 3 * ff
    grads_ref[first : first + value_cols, :] = nn(own_t[...], ga_ref[...]).astype(BF16)
    first = first + value_cols
    rest = grads_ref.shape[0] - first
    grads_ref[first:, :] = jnp.zeros((rest, D), BF16)
    grads_ref[first : first + 16, :] = gain_ref[...].astype(BF16)
    last = pl.ds(3 * ff, grads_ref.shape[0] - 3 * ff)
    last_store = pltpu.make_async_copy(grads_ref.at[last], grads_out.at[last], store_sem.at[blocks + 6])
    last_store.start()
    line.drain()
    out(0, hidden_ref, grad_hidden_out).wait()
    out(1, gn_ref, gn_out).wait()
    out(2, gd_ref, gd_out).wait()
    out(3, gnt_ref, gnt_out).wait()
    ffn_store.wait()
    grads_store.wait()
    last_store.wait()


def feed(tokens, cotangent, attn, recip, wide, gate_turned, down, gains, padded):
    length = tokens.shape[0]
    ff = down.shape[0]
    nv, rows = attn.shape[1], 32
    count = length // rows
    hbm = pl.BlockSpec(memory_space=pl.ANY)
    vmem = pl.BlockSpec(memory_space=pltpu.VMEM)
    return pl.pallas_call(
        functools.partial(feed_kernel, rows),
        out_shape=(
            jax.ShapeDtypeStruct((length, D), F32),
            jax.ShapeDtypeStruct((length, D), F32),
            jax.ShapeDtypeStruct((length, nv), BF16),
            jax.ShapeDtypeStruct((nv, length), BF16),
            jax.ShapeDtypeStruct((length, nv), BF16),
            jax.ShapeDtypeStruct((length, D), BF16),
            jax.ShapeDtypeStruct((padded, D), BF16),
        ),
        in_specs=[hbm] * 7 + [vmem],
        out_specs=(hbm,) * 7,
        scratch_shapes=[
            pltpu.VMEM((length, D), BF16), pltpu.VMEM((length, D), BF16), pltpu.VMEM((length, nv), BF16),
            pltpu.VMEM((D, nv), BF16), pltpu.VMEM((2, ff, D), BF16), pltpu.VMEM((ff, D), BF16), pltpu.VMEM((length, nv), F32),
            pltpu.VMEM((length, D), F32), pltpu.VMEM((length, 128), F32), pltpu.VMEM((length, D), BF16),
            pltpu.VMEM((ff, length), BF16), pltpu.VMEM((ff, length), BF16), pltpu.VMEM((ff, length), BF16),
            pltpu.VMEM((nv // 4, length), BF16), pltpu.VMEM((16, D), F32), pltpu.VMEM((length, D), BF16),
            pltpu.VMEM((length, nv), BF16), pltpu.VMEM((nv, length), BF16), pltpu.VMEM((length, nv), BF16),
            pltpu.VMEM((length, D), BF16), pltpu.VMEM((padded, D), BF16),
            pltpu.VMEM((length, D), BF16), pltpu.VMEM((length, D), BF16), pltpu.VMEM((length, D), BF16),
            pltpu.VMEM((length, D), BF16),
            pltpu.SemaphoreType.DMA((2,)), pltpu.SemaphoreType.DMA((2, count)),
            pltpu.SemaphoreType.DMA((10,)), pltpu.SemaphoreType.DMA((length // BT + 7,)),
        ],
        compiler_params=pltpu.CompilerParams(collective_id=2, has_side_effects=True, vmem_limit_bytes=60 * 2**20),
        name="feed",
    )(tokens, cotangent, attn, recip, wide, gate_turned, down, gains)


def back_kernel(
    pieces, small_pieces, bits, rows,
    pairs_in, values_in, gn_in, gnt_in, gd_in, mask_in, ffn_in, grads_in, normed_in, wide_in, tokens_in,
    total_out, sums_out, grad_out, small_out,
    q_ref, k_ref, v_ref, gn_ref, gnt_ref, gd_ref, mask_ref, normed_ref, wide_ref, tokens_ref,
    part, leaf, mid, total, work, landing, sums, small_work, small_landing, small_sums,
    qt_ref, gq_ref, gkt_ref, gvt_ref, gp_ref, gv_ref, grad_ref, gain_ref,
    line_send, line_recv, cube_send, cube_recv, small_send, small_recv, load_sem, store_sem,
):
    f = lax.axis_index("feat")
    line = LineSum(part, leaf, mid, total, line_send, line_recv, rows, (0, 2, 4))
    cube = CubeSum(work, landing, sums, cube_send, cube_recv, pieces, bits)
    small = CubeSum(small_work, small_landing, small_sums, small_send, small_recv, small_pieces, bits)
    half = HEADS * QK
    first_loads = [
        pltpu.make_async_copy(grads_in.at[pl.ds(a, n)], work.at[pl.ds(a, n)], load_sem.at[m]) for m, (a, n) in enumerate(pieces)
    ] + [pltpu.make_async_copy(ffn_in, part, load_sem.at[len(pieces)])]
    sources = [
        (pairs_in.at[:, pl.ds(0, half)], q_ref), (pairs_in.at[:, pl.ds(half, half)], k_ref), (values_in, v_ref),
        (mask_in, mask_ref), (gn_in, gn_ref), (gd_in, gd_ref), (gnt_in, gnt_ref), (normed_in, normed_ref),
        (wide_in.at[:, pl.ds(0, wide_ref.shape[1])], wide_ref), (tokens_in, tokens_ref),
    ]
    loads = [pltpu.make_async_copy(a, b, load_sem.at[len(pieces) + 1 + n]) for n, (a, b) in enumerate(sources)]
    for load in first_loads:
        load.start()
    greet(line, cube)
    for p in range(len(pieces)):
        first_loads[p].wait()
        cube.launch(p)
    for load in loads[:7]:
        load.start()
    first_loads[-1].wait()
    each(line.leaves, line.count)
    gq_ref[...] = jnp.zeros_like(gq_ref)
    for load in loads[:7]:
        load.wait()
    for load in loads[7:]:
        load.start()
    qt_ref[...] = q_ref[...].T

    lane = lax.broadcasted_iota(jnp.int32, (1, 128), 1)
    length = q_ref.shape[0]
    blocks = length // BT
    hb = 2
    groups = HEADS // hb
    weaver = Weaver(2.0)
    weaver.add("line", line_floors(line, 0.5), [0.0] * line.steps())
    floors, times = cube_floors(cube, 0.0)
    for p in range(len(pieces)):
        weaver.add(("cube", p), floors[p], times[p])

    def take(items):
        for name, n in items:
            if name == "line":
                line.serve(jnp.int32(n))
            elif name[0] == "cube":
                cube.advance(name[1], n)
            else:
                small.advance(name[1], n)

    for block in range(blocks):
        lo = block * BT
        below, there = pl.ds(lo, length - lo), pl.ds(lo, BT)
        plans = [weaver.unit(0.43 * (blocks - block) + 0.1) for _ in range(groups)]

        def group(g, carry):
            h = g * hb
            ql = pl.ds(pl.multiple_of(h // 8 * 128, 128), 128)
            vl = pl.ds(pl.multiple_of(g * 128, 128), 128)
            q, k, v = q_ref[below, ql], k_ref[there, ql], v_ref[there, vl]
            both = jnp.concatenate([gn_ref[below, vl], gd_ref[below, vl]], axis=1)
            mask = mask_ref[block, : length - lo, :]
            gq, turned = None, []
            for a in range(hb):
                km = jnp.where(lane // QK == lax.rem(h + a, 8), k, jnp.zeros_like(k))
                vm = jnp.where(lane // HV == a, v, jnp.zeros_like(v))
                pick = jnp.where(lane == HV * a, jnp.ones_like(v), jnp.zeros_like(v))
                t1 = nt(q, km) + 1.0
                p = (t1 * t1 + 1.0).astype(BF16) * mask
                dp = nt(both, jnp.concatenate([vm, pick], axis=1)).astype(BF16) * mask
                gs = (dp.astype(F32) * t1).astype(BF16)
                out = nn(gs, km)
                gq = out if gq is None else gq + out
                qrows = pl.ds(pl.multiple_of((h + a) * QK, QK), QK)
                vrows = pl.ds(pl.multiple_of((h + a) * HV, HV), HV)
                gkt_ref[qrows, there] = nn(qt_ref[qrows, below], gs)
                turned.append(nn(gnt_ref[vrows, below], p) * 0.5)
            gq_ref[below, ql] += gq
            gvt = jnp.concatenate(turned, axis=0)
            gvt_ref[vl, there] = gvt.astype(BF16)
            gv_ref[there, vl] = gvt.T.astype(BF16)
            for n, plan in enumerate(plans):
                if plan:
                    @pl.when(g == n)
                    def _():
                        take(plan)
            return carry

        lax.fori_loop(0, groups, group, 0)
    gp_ref[:, :half] = (gq_ref[...] * 0.25).astype(BF16)
    gp_ref[:, half:] = gkt_ref[...].T.astype(BF16)
    for load in loads[7:]:
        load.wait()

    pair_cols, value_cols = 2 * half // 4, HEADS * HV // 4
    rest = value_cols + pair_cols

    def open_small(p):
        small.launch(p)
        floors, times = cube_floors(small, 0.0, 1.8)
        weaver.add(("small", p), [0.0] * len(floors[p]), times[p])

    small_work[0:value_cols, :] = nn(
        gvt_ref[pl.ds(pl.multiple_of(f * value_cols, value_cols), value_cols), :], normed_ref[...]
    ).astype(BF16)
    small_work[value_cols:rest, :] = nn(own_column(gp_ref, f, pair_cols).T, normed_ref[...]).astype(BF16)
    if len(small_pieces) > 1:
        open_small(0)
    take(weaver.unit(3.6))
    gain_ref[...] = jnp.zeros_like(gain_ref)
    for n in range(blocks):
        at = slice(n * BT, (n + 1) * BT)
        grad = nt(gp_ref[at, :], wide_ref[:, : 2 * half]) + nt(gv_ref[at, :], wide_ref[:, 2 * half :])
        grad_ref[at, :] = grad.astype(BF16)
        x = tokens_ref[at, :].astype(F32)
        scale = lax.rsqrt(jnp.mean(x * x, axis=1, keepdims=True) + EPS)
        gain_ref[0:1, :] += jnp.sum(grad * (x * scale), axis=0, keepdims=True)
        if n < blocks - 1:
            take(weaver.unit(1.4))
    grad_store = pltpu.make_async_copy(grad_ref, grad_out, store_sem.at[0])
    grad_store.start()
    small_work[rest:, :] = jnp.zeros((small_work.shape[0] - rest, D), BF16)
    small_work[rest : rest + 16, :] = gain_ref[...].astype(BF16)
    open_small(len(small_pieces) - 1)
    take(weaver.unit(1.6))
    take(weaver.until([("cube", p) for p in range(len(pieces))]))
    sums_store = pltpu.make_async_copy(sums, sums_out, store_sem.at[2])
    sums_store.start()
    take(weaver.until([("small", p) for p in range(len(small_pieces))]))
    small_store = pltpu.make_async_copy(small_sums, small_out, store_sem.at[1])
    small_store.start()
    take(weaver.until(["line"]))
    each(line.arrived, line.count)
    total_store = pltpu.make_async_copy(total, total_out, store_sem.at[3])
    total_store.start()
    line.drain()
    cube.drain()
    small.drain()
    for s in (sums_store, grad_store, small_store, total_store):
        s.wait()


def back(pairs, values, gn, gnt, gd, mask, ffn, grads, normed, wide, tokens, pieces, bits, dp_size):
    length = tokens.shape[0]
    nq, nv, rows = HEADS * QK, HEADS * HV, 64
    count = length // rows
    unit = 16 * dp_size
    first = (nv // 4 + nq // 2) // unit * unit
    small_pieces = [(0, first), (first, unit)] if first else []
    small_rows = first + unit
    need = nv // 4 + nq // 2 + 16
    if small_rows < need or not small_pieces:
        small_rows = (need + unit - 1) // unit * unit
        small_pieces = [(0, small_rows)]
    hbm = pl.BlockSpec(memory_space=pl.ANY)

    def buf(*shape, dtype=BF16):
        return pltpu.VMEM(shape, dtype)

    sems = []
    for p in (pieces, small_pieces):
        sems += [pltpu.SemaphoreType.DMA((2,)), pltpu.SemaphoreType.DMA((len(p), 2, 2 * len(bits)))]
    return pl.pallas_call(
        functools.partial(back_kernel, pieces, small_pieces, bits, rows),
        out_shape=(
            jax.ShapeDtypeStruct((length, D), BF16),
            jax.ShapeDtypeStruct(grads.shape, BF16),
            jax.ShapeDtypeStruct((length, D), BF16),
            jax.ShapeDtypeStruct((small_rows, D), BF16),
        ),
        in_specs=[hbm] * 11,
        out_specs=(hbm,) * 4,
        scratch_shapes=[
            buf(length, nq), buf(length, nq), buf(length, nv), buf(length, nv), buf(nv, length), buf(length, nv),
            buf(*mask.shape), buf(length, D), buf(D, 2 * nq + nv), buf(length, D),
            buf(length, D), buf(length, D), buf(length, D), buf(length, D),
            buf(*grads.shape), buf(*grads.shape), buf(*grads.shape),
            buf(small_rows, D), buf(small_rows, D), buf(small_rows, D),
            buf(nq, length), buf(length, nq, dtype=F32), buf(nq, length, dtype=F32), buf(nv, length), buf(length, 2 * nq), buf(length, nv),
            buf(length, D), buf(16, D, dtype=F32),
            pltpu.SemaphoreType.DMA((2,)), pltpu.SemaphoreType.DMA((2, count)), *sems,
            pltpu.SemaphoreType.DMA((len(pieces) + 11,)), pltpu.SemaphoreType.DMA((4,)),
        ],
        compiler_params=pltpu.CompilerParams(collective_id=4, has_side_effects=True, vmem_limit_bytes=62 * 2**20),
        name="back",
    )(pairs, values, gn, gnt, gd, mask, ffn, grads, normed, wide, tokens)


def update_kernel(
    rates,
    down_w, down_m, down_a, gate_w, gate_m, gate_a, out_w, out_m, out_a, value_w, value_m, value_a,
    pair_w, pair_m, pair_a, gain_w, gain_m, gain_a, big, small, hidden, total, grad_hidden, grad_normed, tokens, gains,
    mixed_o, input_o, pair_mo, pair_wo, pair_ao, value_mo, value_wo, value_ao, out_mo, out_wo, out_ao,
    gate_mo, gate_wo, gate_ao, down_mo, down_wo, down_ao, gain_mo, gain_wo, gain_ao,
):
    ff = down_w.shape[0]
    narrow = value_w.shape[1]
    pair_cols = pair_w.shape[1]

    def put(index, outs, grad, w, m, a, rate):
        moment_next, weight_next, average_next = update(w[index], grad, m[index], a[index], rate)
        outs[0][index], outs[1][index], outs[2][index] = moment_next, weight_next, average_next

    put(..., (down_mo, down_wo, down_ao), big[:ff, :].astype(F32), down_w, down_m, down_a, rates[4])
    for n in range(2):
        first = (n + 1) * ff
        put(n, (gate_mo, gate_wo, gate_ao), big[first : first + ff, :].astype(F32), gate_w, gate_m, gate_a, rates[3])
    first = 3 * ff
    put(..., (out_mo, out_wo, out_ao), big[first : first + out_w.shape[0], :].astype(F32), out_w, out_m, out_a, rates[2])
    first = first + out_w.shape[0]
    put(..., (value_mo, value_wo, value_ao), small[:narrow, :].astype(F32).T, value_w, value_m, value_a, rates[1])
    put(..., (pair_mo, pair_wo, pair_ao), small[narrow : narrow + pair_cols, :].astype(F32).T, pair_w, pair_m, pair_a, rates[0])
    gain_one = small[narrow + pair_cols : narrow + pair_cols + 16, :].astype(F32)[0:1, :]
    gain_two = big[first : first + 16, :].astype(F32)[0:1, :]
    put(slice(0, 1), (gain_mo, gain_wo, gain_ao), gain_one, gain_w, gain_m, gain_a, rates[5])
    put(slice(1, 2), (gain_mo, gain_wo, gain_ao), gain_two, gain_w, gain_m, gain_a, rates[5])

    mixed_o[...] = (hidden[...] + total[...].astype(F32)).astype(BF16)
    x = tokens[...].astype(F32)
    scale = lax.rsqrt(jnp.mean(x * x, axis=1, keepdims=True) + EPS)
    unit = x * scale
    u = grad_normed[...].astype(F32) * gains[0:1, :]
    input_o[...] = grad_hidden[...] + scale * (u - unit * jnp.mean(u * unit, axis=1, keepdims=True))


def finish(rates, weights, big, small, hidden, total, grad_hidden, grad_normed, tokens, gains):
    length = tokens.shape[0]
    steps = D // 128
    rows = length // steps
    ff = weights[0][0].shape[0]
    narrow, pair_cols = weights[3][0].shape[1], weights[4][0].shape[1]

    def cols(n):
        return pl.BlockSpec((n, 128), lambda i: (0, i))

    def tall(n):
        return pl.BlockSpec((128, n), lambda i: (i, 0))

    token = pl.BlockSpec((rows, D), lambda i: (i, 0))
    specs = [cols(ff), pl.BlockSpec((2, ff, 128), lambda i: (0, 0, i)), cols(weights[2][0].shape[0]), tall(narrow), tall(pair_cols), cols(2)]
    order = [4, 3, 2, 1, 0, 5]
    flat = [a for group in weights for a in group]
    out_shape = [jax.ShapeDtypeStruct((length, D), BF16), jax.ShapeDtypeStruct((length, D), F32)]
    out_specs = [token, token]
    for n in order:
        out_shape += [jax.ShapeDtypeStruct(weights[n][0].shape, F32)] * 3
        out_specs += [specs[n]] * 3
    in_specs = [specs[n] for n in range(6) for _ in range(3)]
    in_specs += [cols(big.shape[0]), cols(small.shape[0])] + [token] * 5 + [pl.BlockSpec((2, D), lambda i: (0, 0))]
    return pl.pallas_call(
        functools.partial(update_kernel, rates),
        grid=(steps,),
        out_shape=out_shape,
        in_specs=in_specs,
        out_specs=out_specs,
        compiler_params=pltpu.CompilerParams(vmem_limit_bytes=62 * 2**20),
        name="finish",
    )(*flat, big, small, hidden, total, grad_hidden, grad_normed, tokens, gains)


def update(weight, grad_total, moment, average, rate):
    moment_next = MOMENTUM * moment + grad_total
    weight_next = weight - rate * (grad_total + MOMENTUM * moment_next)
    average_next = average + (weight_next - average) / STEP
    return (moment_next, weight_next, average_next)


def on_device(
    tokens,
    cotangent,
    doc_starts,
    queries_keys,
    value_weight,
    out_weight,
    gate_up,
    down_weight,
    norm_gains,
    queries_moment,
    value_moment,
    out_moment,
    gate_moment,
    down_moment,
    gains_moment,
    queries_average,
    value_average,
    out_average,
    gate_average,
    down_average,
    gains_average,
):
    total_tokens = float(tokens.shape[0] * lax.axis_size("dp"))
    dp_size = lax.axis_size("dp")
    ff = down_weight.shape[0]
    gate_turned = gate_up.transpose(0, 2, 1)
    normed_one, pairs, values, wide, gate_low, down_low, attn_low, recip, mask = front(
        doc_starts, tokens, norm_gains, queries_keys, value_weight, out_weight, gate_turned, down_weight
    )
    padded, pieces, bits = cube_shape(3 * ff + out_weight.shape[0] + 16, dp_size, 4)
    hidden_one, grad_hidden, grad_numer, grad_numer_turned, grad_denom, ffn_part, big = feed(
        tokens, cotangent, attn_low, recip, wide, gate_low, down_low, norm_gains, padded
    )
    total, big, grad_normed_one, small = back(
        pairs, values, grad_numer, grad_numer_turned, grad_denom, mask, ffn_part, big, normed_one, wide, tokens,
        pieces, bits, dp_size,
    )
    rates = (
        (D * total_tokens) ** (-0.5),
        (D * total_tokens) ** (-0.5),
        (HEADS * HV * total_tokens) ** (-0.5),
        (D * total_tokens) ** (-0.5),
        (FF * total_tokens) ** (-0.5),
        0.2 * total_tokens ** (-0.5),
    )
    weights = (
        (down_weight, down_moment, down_average),
        (gate_turned, gate_moment.transpose(0, 2, 1), gate_average.transpose(0, 2, 1)),
        (out_weight, out_moment, out_average),
        (value_weight, value_moment, value_average),
        (queries_keys, queries_moment, queries_average),
        (norm_gains, gains_moment, gains_average),
    )
    outs = list(finish(rates, weights, big, small, hidden_one, total, grad_hidden, grad_normed_one, tokens, norm_gains))
    outs[11:14] = [o.transpose(0, 2, 1) for o in outs[11:14]]
    return tuple(outs)


def solution(mesh):
    in_specs = (
        P("dp", None),
        P("dp", None),
        P("dp", None),
        P(None, "feat"),
        P(None, "feat"),
        P("feat", None),
        P(None, None, "feat"),
        P("feat", None),
        P(),
        P(None, "feat"),
        P(None, "feat"),
        P("feat", None),
        P(None, None, "feat"),
        P("feat", None),
        P(),
        P(None, "feat"),
        P(None, "feat"),
        P("feat", None),
        P(None, None, "feat"),
        P("feat", None),
        P(),
    )
    out_specs = (
        P("dp", None),
        P("dp", None),
        P(None, "feat"),
        P(None, "feat"),
        P(None, "feat"),
        P(None, "feat"),
        P(None, "feat"),
        P(None, "feat"),
        P("feat", None),
        P("feat", None),
        P("feat", None),
        P(None, None, "feat"),
        P(None, None, "feat"),
        P(None, None, "feat"),
        P("feat", None),
        P("feat", None),
        P("feat", None),
        P(),
        P(),
        P(),
    )
    return jax.shard_map(
        on_device, mesh=mesh, in_specs=in_specs, out_specs=out_specs, check_vma=False
    )
```

```python
import functools
import jax
import jax.numpy as jnp
from jax import lax
from jax.experimental import pallas as pl
from jax.experimental.pallas import tpu as pltpu
from jax.sharding import PartitionSpec as P

D = 1024
HEADS = 16
QK = 16
HV = 64
FF = 2752
STEP = 4
BT = 256
F32 = jnp.float32
BF16 = jnp.bfloat16

MESH = pl.DeviceIdType.MESH
EPS = 1e-06
MOMENTUM = 0.9


def nt(a, b):
    return lax.dot_general(a, b, (((1,), (1,)), ((), ())), preferred_element_type=F32)


def nn(a, b):
    return lax.dot_general(a, b, (((1,), (0,)), ((), ())), preferred_element_type=F32)


class LineSum:
    def __init__(self, part, leaf, mid, total, send, recv, rows, lags=(0, 2, 4)):
        self.part, self.leaf, self.mid, self.total, self.send, self.recv = part, leaf, mid, total, send, recv
        self.rows, self.lags = rows, lags
        self.count = part.shape[0] // rows
        self.dp, self.f = lax.axis_index("dp"), lax.axis_index("feat")

    def place(self, c):
        odd = lax.rem(c, 2)
        return self.f + odd * (3 - 2 * self.f), 1 - 2 * odd

    def copy(self, c, src, dst, kind, slot, to):
        at = pl.ds(pl.multiple_of(c * self.rows, self.rows), self.rows)
        return pltpu.make_async_remote_copy(
            src_ref=src.at[at], dst_ref=dst.at[at], send_sem=self.send.at[slot], recv_sem=self.recv.at[min(kind, 1), c],
            device_id=(self.dp, to), device_id_type=MESH)

    def leaves(self, c):
        p, up = self.place(c)

        @pl.when(p == 3)
        def _():
            self.copy(c, self.part, self.leaf, 0, 0, self.f - up).start()

        @pl.when(p == 0)
        def _():
            self.copy(c, self.part, self.leaf, 0, 0, self.f + up).start()

    def middle(self, c):
        p, up = self.place(c)
        at = pl.ds(pl.multiple_of(c * self.rows, self.rows), self.rows)

        @pl.when(p == 2)
        def _():
            self.copy(c, self.part, self.leaf, 0, 0, self.f).wait_recv()
            self.part[at, :] = self.part[at, :] + self.leaf[at, :]
            self.copy(c, self.part, self.mid, 1, 0, self.f - up).start()

    def root(self, c):
        p, up = self.place(c)
        at = pl.ds(pl.multiple_of(c * self.rows, self.rows), self.rows)

        @pl.when(p == 1)
        def _():
            self.copy(c, self.part, self.leaf, 0, 0, self.f).wait_recv()
            self.copy(c, self.part, self.mid, 1, 0, self.f).wait_recv()
            self.total[at, :] = self.part[at, :] + self.leaf[at, :] + self.mid[at, :]
            self.copy(c, self.total, self.total, 2, 1, self.f + up).start()
            self.copy(c, self.total, self.total, 2, 0, self.f - up).start()

    def onward(self, c):
        p, up = self.place(c)

        @pl.when(p == 2)
        def _():
            self.copy(c, self.total, self.total, 2, 0, self.f).wait_recv()
            self.copy(c, self.total, self.total, 2, 1, self.f + up).start()

    def serve(self, i):
        for lag, act in zip(self.lags, (self.middle, self.root, self.onward)):
            c = i - lag

            @pl.when(jnp.logical_and(c >= 0, c < self.count))
            def _():
                act(c)

    def steps(self):
        return self.count + self.lags[-1]

    def arrived(self, c):
        p, up = self.place(c)

        @pl.when(jnp.logical_or(p == 0, p == 3))
        def _():
            self.copy(c, self.total, self.total, 2, 0, self.f).wait_recv()

    def drain(self):
        def all_sent(slot):
            pltpu.make_async_remote_copy(
                src_ref=self.part, dst_ref=self.part, send_sem=self.send.at[slot], recv_sem=self.recv.at[0, 0],
                device_id=(self.dp, self.f), device_id_type=MESH,
            ).wait_send()

        all_sent(0)

        @pl.when(jnp.logical_or(self.f == 1, self.f == 2))
        def _():
            all_sent(1)


class CubeSum:
    def __init__(self, work, recv, out, send_sem, recv_sem, pieces, bits):
        self.work, self.recv, self.out, self.send_sem, self.recv_sem = work, recv, out, send_sem, recv_sem
        self.pieces, self.nb = pieces, len(bits)
        self.dp, self.f = lax.axis_index("dp"), lax.axis_index("feat")
        self.orders = [list(bits), [bits[0]] + list(bits[1:])[::-1]]
        self.bits = bits

    def partner(self, bit):
        return self.dp + bit - 2 * bit * lax.rem(self.dp // bit, 2)

    def lanes(self, colour):
        half = self.work.shape[1] // 2
        return pl.ds(colour * half, half)

    def segment(self, piece, colour, k):
        first, rows = self.pieces[piece]
        start = first
        for bit in self.orders[colour][:k]:
            rows = rows // 2
            start = start + rows * lax.rem(self.dp // bit, 2)
        return start, rows

    def at(self, start, rows):
        return pl.ds(pl.multiple_of(start, 16), rows)

    def halve(self, piece, colour, k):
        start, rows = self.segment(piece, colour, k)
        rows = rows // 2
        bit = self.orders[colour][k]
        own = lax.rem(self.dp // bit, 2)
        first, whole = self.pieces[piece]
        landing = first + whole - 2 * rows
        return pltpu.make_async_remote_copy(
            src_ref=self.work.at[self.at(start + rows * (1 - own), rows), self.lanes(colour)],
            dst_ref=self.recv.at[self.at(landing, rows), self.lanes(colour)],
            send_sem=self.send_sem.at[0], recv_sem=self.recv_sem.at[piece, colour, k],
            device_id=(self.partner(bit), self.f), device_id_type=MESH)

    def add(self, piece, colour, k):
        start, rows = self.segment(piece, colour, k + 1)
        first, whole = self.pieces[piece]
        landing = first + whole - 2 * rows
        target = self.out if k + 1 == self.nb else self.work
        mine = self.work[self.at(start, rows), self.lanes(colour)]
        target[self.at(start, rows), self.lanes(colour)] = mine + self.recv[self.at(landing, rows), self.lanes(colour)]

    def double(self, piece, colour, k):
        start, rows = self.segment(piece, colour, k + 1)
        bit = self.orders[colour][k]
        at = self.at(start, rows)
        slot = 2 * self.nb - 1 - k
        return pltpu.make_async_remote_copy(
            src_ref=self.out.at[at, self.lanes(colour)], dst_ref=self.out.at[at, self.lanes(colour)],
            send_sem=self.send_sem.at[1], recv_sem=self.recv_sem.at[piece, colour, slot],
            device_id=(self.partner(bit), self.f), device_id_type=MESH)

    def launch(self, piece):
        for colour in range(2):
            self.halve(piece, colour, 0).start()

    def advance(self, piece, t):
        for colour in range(2):
            if t < self.nb:
                self.halve(piece, colour, t).wait_recv()
                self.add(piece, colour, t)
                if t + 1 < self.nb:
                    self.halve(piece, colour, t + 1).start()
                else:
                    self.double(piece, colour, self.nb - 1).start()
            else:
                k = 2 * self.nb - 1 - t
                self.double(piece, colour, k).wait_recv()
                if k > 0:
                    self.double(piece, colour, k - 1).start()

    def drain(self):
        rows = self.work.shape[0]
        sent = pl.ds(0, rows - rows // 2**self.nb)
        for n, ref in enumerate((self.work, self.out)):
            pltpu.make_async_remote_copy(
                src_ref=ref.at[sent], dst_ref=ref.at[sent], send_sem=self.send_sem.at[n], recv_sem=self.recv_sem.at[0, 0, 0],
                device_id=(self.dp, self.f), device_id_type=MESH,
            ).wait_send()


def split_rows(rows, unit, count):
    units = rows // unit
    out, first = [], 0
    for n in range(count):
        take = (units * (n + 1) // count - units * n // count) * unit
        out.append((first, take))
        first += take
    return [p for p in out if p[1]]


def own_column(ref, f, width):
    return ref[:, pl.ds(pl.multiple_of(f * width, width), width)]


def greet(line, cube):
    sem = pltpu.get_barrier_semaphore()
    f = lax.axis_index("feat")
    count = jnp.int32(0)
    if cube is not None:
        for bit in cube.bits:
            pl.semaphore_signal(sem, inc=1, device_id=(cube.partner(bit), f), device_id_type=MESH)
        count = count + len(cube.bits)
    if line is not None:
        @pl.when(f > 0)
        def _():
            pl.semaphore_signal(sem, inc=1, device_id=(line.dp, f - 1), device_id_type=MESH)

        @pl.when(f < 3)
        def _():
            pl.semaphore_signal(sem, inc=1, device_id=(line.dp, f + 1), device_id_type=MESH)
        count = count + jnp.where(f > 0, 1, 0) + jnp.where(f < 3, 1, 0)
    pl.semaphore_wait(sem, count)


def each(act, n):
    def body(c, carry):
        act(c)
        return carry

    lax.fori_loop(0, n, body, 0)


def cube_shape(rows, dp_size, count):
    unit = 16 * dp_size
    padded = (rows + unit - 1) // unit * unit
    bits = tuple(2**n for n in range(dp_size.bit_length() - 1))
    return padded, split_rows(padded, unit, count), bits


class Weaver:
    def __init__(self, now, margin=0.5, cost=0.25):
        self.now, self.margin, self.cost = now, margin, cost
        self.streams = {}

    def add(self, name, floors, leads):
        self.streams[name] = [list(floors), list(leads), 0, self.now]

    def ready(self, name):
        floors, leads, n, last = self.streams[name]
        return max(floors[n], last + leads[n])

    def open(self):
        return [name for name, s in self.streams.items() if s[2] < len(s[0])]

    def take(self, name):
        stream = self.streams[name]
        self.now = max(self.now, self.ready(name)) + self.cost
        stream[2] += 1
        stream[3] = self.now
        return name, stream[2] - 1

    def unit(self, length):
        self.now += length
        out = []
        while self.open():
            name = min(self.open(), key=self.ready)
            if self.ready(name) > self.now - self.margin:
                break
            out.append(self.take(name))
        return out

    def until(self, names):
        out = []
        while any(name in names for name in self.open()):
            out.append(self.take(min(self.open(), key=self.ready)))
        return out


def line_floors(line, start):
    pace = line.rows * line.part.shape[1] * 2 / 40e3
    return [start + pace * (n + 1) + 3.0 for n in range(line.steps())]


def cube_floors(cube, start, lag=3.0):
    count = 2 * cube.nb
    ends, floors, times = [start] * len(cube.pieces), [[] for _ in cube.pieces], [[] for _ in cube.pieces]
    for t in range(count):
        near = t in (0, count - 1)
        share = 2 ** (min(t, count - 1 - t) + 1)
        busy = max(ends) if t not in (0, 1, count - 1) else start
        for p, (_, rows) in enumerate(cube.pieces):
            size = rows / share * 1024
            own = 2 * size / 430e3 if near else size / 30e3
            begin = ends[p] + (lag + 0.3 if t else 0.0)
            busy = max(busy, begin) + own
            ends[p] = busy
            floors[p].append(busy + lag)
            times[p].append(own + lag)
    return floors, times


def front_kernel(
    bits, starts_ref, tokens_in, gains_ref, pair_ref, value_ref, out_ref, gate_in, down_in,
    normed_out, pairs_out, values_out, wide_out, gate_out, down_out, attn_out, recip_out, mask_out,
    thin_ref, thick_ref, turned_ref, tokens_ref, gate_f32, down_f32,
    normed_ref, pairs_ref, values_ref, wide_ref, gate_ref, down_ref, attn_ref, recip_ref, mask_ref, acc_ref,
    send_sem, recv_sem, load_sem, store_sem,
):
    dp = lax.axis_index("dp")
    f = lax.axis_index("feat")
    slices = lax.axis_size("feat")
    last = 3
    pieces = 2 ** len(bits)
    j = lax.rem(dp, pieces)
    base = dp - j
    pair_cols, value_cols = pair_ref.shape[1], value_ref.shape[1]
    pairs_wide, values_wide = slices * pair_cols, slices * value_cols
    rows = pair_ref.shape[0] // pieces
    length = tokens_ref.shape[0]
    blocks = length // BT
    loads = [
        pltpu.make_async_copy(a, b, load_sem.at[n])
        for n, (a, b) in enumerate([(tokens_in, tokens_ref), (gate_in, gate_f32), (down_in, down_f32)])
    ]
    loads[0].start()

    def flip(k, bit):
        return k + bit - 2 * bit * lax.rem(k // bit, 2)

    colour_bits = [list(bits[1:]) + [bits[0]], list(bits[1:])[::-1] + [bits[0]]]

    def place(k, colour):
        return sum(k // bit % 2 * 2**n for n, bit in enumerate(colour_bits[colour]))

    def cast(k):
        at = pl.ds(pl.multiple_of(k * rows, rows), rows)
        pair = pair_ref[at, :].astype(BF16)
        thick = value_ref[at, :].astype(BF16)
        turned = out_ref[:, at].T.astype(BF16)
        for colour in range(2):
            part = slice(colour * rows // 2, (colour + 1) * rows // 2)
            thin_ref[colour, place(k, colour), 0] = pair[part]
            thick_ref[colour, place(k, colour), 0] = thick[part]
            turned_ref[colour, place(k, colour), 0] = turned[part]

    cast(j)
    order = [
        jnp.where(f == 0, 1, f - 1),
        jnp.where(f < 2, 2, jnp.where(f == 2, 3, 1)),
        jnp.where(f < 2, 3, 0),
    ]
    barrier = pltpu.get_barrier_semaphore()
    for bit in bits:
        pl.semaphore_signal(barrier, inc=1, device_id=(base + flip(j, bit), f), device_id_type=MESH)
    for z in order:
        pl.semaphore_signal(barrier, inc=1, device_id=(dp, z), device_id_type=MESH)
    pl.semaphore_wait(barrier, len(bits) + last)

    bufs = (thin_ref, thick_ref, turned_ref)
    here = (dp, f)

    def copy(wave, source, target, colour, kind, device, r=None):
        group = 0 if r is None or wave != 1 else r - 1
        return pltpu.make_async_remote_copy(
            src_ref=source, dst_ref=target, send_sem=send_sem.at[wave], recv_sem=recv_sem.at[wave, colour, kind, group],
            device_id=device, device_id_type=MESH,
        )

    for wave in range(3):
        for z in order:
            for colour in range(2):
                at = bufs[wave].at[colour, place(j, colour)]
                r = lax.rem(f - z + slices, slices)
                copy(wave, at.at[0], at.at[r], colour, 0, (dp, z), r).start()

    def held(wave, k, colour, n, r):
        first = place(k, colour) // 2**n * 2**n
        which = pl.ds(1, last) if r is None else pl.ds(r, 1)
        return bufs[wave].at[colour, pl.ds(first, 2**n), which]

    def start_step(wave, n, r):
        for colour in range(2):
            at = held(wave, j, colour, n, r)
            copy(wave, at, at, colour, 1 + n, (base + flip(j, colour_bits[colour][n]), f), r).start()

    def arrive(wave, a=None):
        r = None if a is None else relative[a]
        for colour in range(2):
            at = held(wave, j, colour, 0, r)
            copy(wave, at, at, colour, 0, here, r).wait_recv()
        start_step(wave, 0, r)

    def step(wave, n, a=None):
        r = None if a is None else relative[a]
        for colour in range(2):
            at = held(wave, flip(j, colour_bits[colour][n]), colour, n, r)
            copy(wave, at, at, colour, 1 + n, here, r).wait_recv()
        if n + 1 < len(bits):
            start_step(wave, n + 1, r)

    relative = [lax.rem(z - f + slices, slices) for z in order]

    def put(wave, r, lanes):
        for k in range(pieces):
            for colour in range(2):
                first = k * rows + colour * rows // 2
                wide_ref[first : first + rows // 2, lanes] = bufs[wave][colour, place(k, colour), r]

    def owner(r):
        return lax.rem(f + r, slices)

    def put_thin(r):
        put(0, r, pl.ds(pl.multiple_of(owner(r) * pair_cols, pair_cols), pair_cols))

    def lanes(first, z):
        return pl.ds(pl.multiple_of(first + z * value_cols, 128), value_cols)

    def store(n, source, target, at=None):
        if at is not None:
            source, target = source.at[:, at], target.at[:, at]
        return pltpu.make_async_copy(source, target, store_sem.at[n])

    def use(r):
        z = owner(r)
        put(1, r, lanes(pairs_wide, z))

        def some(n, carry):
            at = pl.ds(pl.multiple_of(n * BT, BT), BT)
            values_ref[at, lanes(0, z)] = nn(normed_ref[at, :], wide_ref[:, lanes(pairs_wide, z)]).astype(BF16)
            return carry

        lax.fori_loop(0, blocks, some, 0)
        store(5, wide_ref, wide_out, lanes(pairs_wide, z)).start()
        store(6, values_ref, values_out, lanes(0, z)).start()

    def put_turned(r):
        at = lanes(pairs_wide + values_wide, owner(r))
        put(2, r, at)
        store(5, wide_ref, wide_out, at).start()

    def cast_rest(n, carry):
        cast(lax.rem(j + n, pieces))
        return carry

    lax.fori_loop(1, pieces, cast_rest, 0)
    loads[0].wait()
    loads[1].start()
    loads[2].start()

    def norm(n, carry):
        at = pl.ds(pl.multiple_of(n * BT, BT), BT)
        x = tokens_ref[at, :].astype(F32)
        scale = lax.rsqrt(jnp.mean(x * x, axis=1, keepdims=True) + EPS)
        normed_ref[at, :] = (x * scale * gains_ref[0:1, :]).astype(BF16)
        return carry

    lax.fori_loop(0, blocks, norm, 0)
    store(0, normed_ref, normed_out).start()
    put_thin(0)
    arrive(0)
    use(0)
    step(0, 0)

    begin = jnp.zeros((length, 1), jnp.int32)
    position = lax.broadcasted_iota(jnp.int32, (length, 1), 0)
    for n in range(starts_ref.shape[1]):
        begin = jnp.where(starts_ref[0, n] <= position, jnp.maximum(begin, starts_ref[0, n]), begin)
    for n in range(blocks):
        rest = length - n * BT
        s = n * BT + lax.broadcasted_iota(jnp.int32, (rest, BT), 1)
        keep = jnp.logical_and(s <= position[n * BT :], s >= begin[n * BT :])
        mask_ref[n, :rest, :] = keep.astype(F32).astype(BF16)
        if n:
            mask_ref[n, rest:, :] = jnp.zeros((n * BT, BT), BF16)
    store(1, mask_ref, mask_out).start()
    def cast_all(source, target):
        def go(m, carry):
            at = pl.ds(pl.multiple_of(m * 16, 16), 16)
            target[at, :] = source[at, :].astype(BF16)
            return carry

        lax.fori_loop(0, source.shape[0] // 16, go, 0)

    step(0, 1)
    arrive(1, 0)
    arrive(1, 1)
    put_turned(0)
    loads[1].wait()
    loads[2].wait()
    cast_all(gate_f32.at[0], gate_ref.at[0])
    step(0, 2)
    step(1, 0, 0)
    arrive(1, 2)
    step(1, 0, 1)
    for r in range(1, slices):
        put_thin(r)

    half = pairs_wide // 2

    def project_pairs(n, carry):
        at = pl.ds(pl.multiple_of(n * BT, BT), BT)
        pairs = nn(normed_ref[at, :], wide_ref[:, :pairs_wide]).astype(BF16)
        pairs_ref[at, :half] = pairs[:, :half] * jnp.bfloat16(0.25)
        pairs_ref[at, half:] = pairs[:, half:]
        return carry

    lax.fori_loop(0, blocks, project_pairs, 0)
    store(4, pairs_ref, pairs_out).start()
    store(5, wide_ref, wide_out, pl.ds(0, pairs_wide)).start()

    lane = lax.broadcasted_iota(jnp.int32, (1, 128), 1)
    def cast_last():
        cast_all(down_f32, down_ref)
        store(2, gate_ref, gate_out).start()
        store(3, down_ref, down_out).start()

    def put_others():
        for r in range(1, slices):
            put_turned(r)

    def cast_up():
        cast_all(gate_f32.at[1], gate_ref.at[1])

    events = {
        1: [(step, 1, 1, 0), (step, 1, 0, 2), (arrive, 2)],
        2: [(cast_up,), (step, 1, 1, 1), (step, 1, 2, 0), (use, relative[0])],
        3: [(step, 1, 1, 2), (step, 2, 0)],
        4: [(step, 1, 2, 1), (use, relative[1])],
        5: [(cast_last,), (step, 2, 1)],
        6: [(step, 1, 2, 2), (use, relative[2])],
        7: [(step, 2, 2), (put_others,)],
    }

    def unit(n, carry):
        for at, acts in events.items():
            @pl.when(n == at)
            def _():
                for act in acts:
                    act[0](*act[1:])
        a = n // 2
        z = jnp.where(a == 0, f, jnp.where(a == 1, order[0], jnp.where(a == 2, order[1], order[2])))
        pair = 2 * z + lax.rem(n, 2)
        vl = pl.ds(pl.multiple_of(pair * 128, 128), 128)
        ql = pl.ds(pl.multiple_of(pair // 4 * 128, 128), 128)
        kl = pl.ds(pl.multiple_of(half + pair // 4 * 128, 128), 128)
        for block in range(blocks):
            first = block * BT
            below, there = pl.ds(first, length - first), pl.ds(first, BT)
            q, k, v = pairs_ref[below, ql], pairs_ref[there, kl], values_ref[there, vl]
            mask = mask_ref[block, : length - first, :]
            for m in range(2):
                own = lane // QK == lax.rem(2 * pair + m, 8)
                t1 = nt(q, jnp.where(own, k, jnp.zeros_like(k))) + 1.0
                p = (t1 * t1 + 1.0).astype(BF16) * mask
                out = nn(p, jnp.where(lane // HV == m, v, jnp.ones_like(v)))
                if block:
                    acc_ref[m, below, :] += out
                else:
                    acc_ref[m] = out
        one, two = acc_ref[0], acc_ref[1]
        numer = jnp.where(lane < HV, one, two)
        recip = 1.0 / pltpu.roll(jnp.where(lane < HV, two, one), HV, 1)
        attn_ref[:, vl] = (numer * recip).astype(BF16)
        recip_ref[:, vl] = recip
        store(7, attn_ref, attn_out, vl).start()
        store(8, recip_ref, recip_out, vl).start()
        return carry

    lax.fori_loop(0, 2 * slices, unit, 0)
    for wave in range(3):
        at = bufs[wave].at[:, :, pl.ds(0, last)]
        copy(wave, at, at, 0, 0, here).wait_send()
    for n, (source, target) in enumerate([
        (normed_ref, normed_out), (mask_ref, mask_out), (gate_ref, gate_out), (down_ref, down_out), (pairs_ref, pairs_out),
        (wide_ref, wide_out), (values_ref, values_out), (attn_ref, attn_out), (recip_ref, recip_out),
    ]):
        store(n, source, target).wait()


def front(starts, tokens, gains, pair_w, value_w, out_w, gate_turned, down):
    length = tokens.shape[0]
    ff = down.shape[0]
    slices = 4
    pair_cols, value_cols = pair_w.shape[1], value_w.shape[1]
    bits = (1, 2, 4)
    hbm = pl.BlockSpec(memory_space=pl.ANY)
    vmem = pl.BlockSpec(memory_space=pltpu.VMEM)
    shapes = [
        ((length, D), BF16),
        ((length, slices * pair_cols), BF16),
        ((length, slices * value_cols), BF16),
        ((D, slices * (pair_cols + 2 * value_cols)), BF16),
        ((2, ff, D), BF16),
        ((ff, D), BF16),
        ((length, slices * value_cols), BF16),
        ((length, slices * value_cols), F32),
        ((length // BT, length, BT), BF16),
    ]
    return pl.pallas_call(
        functools.partial(front_kernel, bits),
        out_shape=tuple(jax.ShapeDtypeStruct(*s) for s in shapes),
        in_specs=[pl.BlockSpec(memory_space=pltpu.SMEM), hbm] + [vmem] * 4 + [hbm] * 2,
        out_specs=(hbm,) * 9,
        scratch_shapes=[
            pltpu.VMEM((2, 8, slices, D // 16, pair_cols), BF16),
            pltpu.VMEM((2, 8, slices, D // 16, value_cols), BF16),
            pltpu.VMEM((2, 8, slices, D // 16, value_cols), BF16),
            pltpu.VMEM((length, D), BF16),
            pltpu.VMEM((2, ff, D), F32),
            pltpu.VMEM((ff, D), F32),
        ]
        + [pltpu.VMEM(*s) for s in shapes]
        + [
            pltpu.VMEM((2, length, 128), F32),
            pltpu.SemaphoreType.DMA((3,)),
            pltpu.SemaphoreType.DMA((3, 2, 4, 3)),
            pltpu.SemaphoreType.DMA((3,)),
            pltpu.SemaphoreType.DMA((9,)),
        ],
        compiler_params=pltpu.CompilerParams(collective_id=1, has_side_effects=True, vmem_limit_bytes=60 * 2**20),
        name="front",
    )(starts, tokens, gains, pair_w, value_w, out_w, gate_turned, down)


def feed_kernel(
    rows, tokens_in, cot_in, attn_in, recip_in, wide_in, gate_in, down_in, gains_ref,
    hidden_out, grad_hidden_out, gn_out, gnt_out, gd_out, ffn_out, grads_out,
    tokens_ref, cot_ref, attn_ref, out_w, gate_ref, down_ref, recip_ref,
    hidden_ref, scale_ref, normed_ref, product_t, gate_t, up_t, own_t, gain_ref, ga_ref, gn_ref, gnt_ref, gd_ref, ffn_ref, grads_ref,
    part, leaf, mid, total, send, recv, load_sem, store_sem,
):
    f = lax.axis_index("feat")
    line = LineSum(part, leaf, mid, total, send, recv, rows, (0, 3, 6))
    length = tokens_ref.shape[0]
    ff = down_ref.shape[0]
    value_cols = own_t.shape[0]
    blocks = length // BT
    first_out = wide_in.shape[1] - attn_ref.shape[1]
    top, others = pl.ds(0, BT), pl.ds(BT, length - BT)
    pairs = [
        (attn_in.at[top], attn_ref.at[top]), (wide_in.at[:, pl.ds(first_out, attn_ref.shape[1])], out_w),
        (tokens_in.at[top], tokens_ref.at[top]), (gate_in, gate_ref), (cot_in.at[top], cot_ref.at[top]), (down_in, down_ref),
        (attn_in.at[others], attn_ref.at[others]), (tokens_in.at[others], tokens_ref.at[others]),
        (cot_in.at[others], cot_ref.at[others]), (recip_in, recip_ref),
    ]
    loads = [pltpu.make_async_copy(a, b, load_sem.at[n]) for n, (a, b) in enumerate(pairs)]
    for load in loads[:6]:
        load.start()
    greet(line, None)
    for load in loads[:6]:
        load.wait()
    for load in loads[6:]:
        load.start()

    def store(source, target, n):
        at = pl.ds(pl.multiple_of(n * BT, BT), BT)
        return pltpu.make_async_copy(source.at[at], target.at[at], store_sem.at[n])

    def block(b, carry):
        at = pl.ds(pl.multiple_of(b * BT, BT), BT)
        turn = 4 * (b - 1)

        @pl.when(b == 1)
        def _():
            for load in loads[6:9]:
                load.wait()

        hidden = tokens_ref[at, :].astype(F32) + nt(attn_ref[at, :], out_w[...])
        hidden_ref[at, :] = hidden
        store(hidden_ref, hidden_out, b).start()
        scale = lax.rsqrt(jnp.mean(hidden * hidden, axis=1, keepdims=True) + EPS)
        scale_ref[at, :] = jnp.broadcast_to(scale, (BT, 128))
        normed = (hidden * scale * gains_ref[1:2, :]).astype(BF16)
        normed_ref[at, :] = normed
        line.serve(turn)
        gate = nt(normed, gate_ref[0])
        up = nt(normed, gate_ref[1])
        line.serve(turn + 1)
        back = nt(cot_ref[at, :], down_ref[...])
        sig = 1.0 / (1.0 + jnp.exp(-gate))
        active = gate * sig
        slope = sig * (1.0 + gate * (1.0 - sig))
        product = (active * up).astype(BF16)
        grad_gate = (back * up * slope).astype(BF16)
        grad_up = (back * active).astype(BF16)
        line.serve(turn + 2)
        part[at, :] = (nn(grad_gate, gate_ref[0]) + nn(grad_up, gate_ref[1])).astype(BF16)

        def out(c, carry):
            line.leaves(b * (BT // rows) + c)
            return carry

        lax.fori_loop(0, BT // rows, out, 0)
        ffn_ref[at, :] = nn(product, down_ref[...]).astype(BF16)
        product_t[:, at] = product.T
        gate_t[:, at] = grad_gate.T
        up_t[:, at] = grad_up.T
        line.serve(turn + 3)
        return carry

    lax.fori_loop(0, blocks, block, 0)
    served = 4 * (blocks - 1)
    gain_ref[...] = jnp.zeros_like(gain_ref)
    chunks = []
    at = 0
    while at < ff:
        chunks.append((at, min(176, ff - at)))
        at += chunks[-1][1]
    for n, (turned, right) in enumerate([(product_t, cot_ref), (gate_t, normed_ref), (up_t, normed_ref)]):
        for first, size in chunks:
            at = slice(n * ff + first, n * ff + first + size)
            grads_ref[at, :] = nn(turned[first : first + size, :], right[...]).astype(BF16)
            line.serve(jnp.int32(served))
            served += 1
    ffn_store = pltpu.make_async_copy(ffn_ref, ffn_out, store_sem.at[blocks])
    ffn_store.start()
    grads_store = pltpu.make_async_copy(
        grads_ref.at[pl.ds(0, 3 * ff)], grads_out.at[pl.ds(0, 3 * ff)], store_sem.at[blocks + 1]
    )
    grads_store.start()
    own_t[...] = own_column(attn_ref, f, value_cols).T
    loads[-1].wait()
    same = lax.broadcasted_iota(jnp.int32, (128, 128), 0) // HV == lax.broadcasted_iota(jnp.int32, (128, 128), 1) // HV
    negate = jnp.where(same, -1.0, 0.0).astype(BF16)
    size = 4 * rows
    units = length // size

    def out(n, source, target, at=None):
        if at is not None:
            source, target = source.at[at], target.at[at]
        return pltpu.make_async_copy(source, target, store_sem.at[blocks + 2 + n])

    def back_rows(u):
        at = pl.ds(u * size, size)
        for c in range(4):
            line.arrived(jnp.int32(4 * u + c))
        if u * size % BT == 0:
            store(hidden_ref, hidden_out, jnp.int32(u * size // BT)).wait()
        hidden, grad = hidden_ref[at, :], total[at, :].astype(F32)
        scale = scale_ref[at, 0:1]
        unit = hidden * scale
        u_two = grad * gains_ref[1:2, :]
        gh = cot_ref[at, :].astype(F32) + scale * (u_two - unit * jnp.mean(u_two * unit, axis=1, keepdims=True))
        hidden_ref[at, :] = gh
        out(0, hidden_ref, grad_hidden_out, at).start()
        ga_ref[at, :] = gh.astype(BF16)
        gain_ref[0:1, :] += jnp.sum(grad * unit, axis=0, keepdims=True)

    def prepare(u, half):
        at = pl.ds(u * size, size)
        ga = ga_ref[at, :]
        for m in range(2):
            wide = pl.ds((2 * half + m) * 256, 256)
            numer = nn(ga, out_w[:, wide]) * (2.0 * recip_ref[at, wide])
            low = numer.astype(BF16)
            both = (numer * attn_ref[at, wide].astype(F32)).astype(BF16)
            gn_ref[at, wide] = low
            gnt_ref[wide, at] = low.T
            gd_ref[at, wide] = jnp.concatenate([nn(both[:, :128], negate), nn(both[:, 128:], negate)], axis=1).astype(BF16)
        if half:
            out(1, gn_ref, gn_out, at).start()
            out(2, gd_ref, gd_out, at).start()
            out(3, gnt_ref, gnt_out, (slice(None), at)).start()

    tasks = [(u, q) for u in range(units) for q in range(3)]
    while tasks:
        if served < line.steps():
            line.serve(jnp.int32(served))
            served += 1
        for _ in range(2):
            if tasks and (served >= line.steps() or served > 4 * tasks[0][0] + 4 + line.lags[-1] + tasks[0][1]):
                u, q = tasks.pop(0)
                if q == 0:
                    back_rows(u)
                else:
                    prepare(u, q - 1)
    first = 3 * ff
    grads_ref[first : first + value_cols, :] = nn(own_t[...], ga_ref[...]).astype(BF16)
    first = first + value_cols
    rest = grads_ref.shape[0] - first
    grads_ref[first:, :] = jnp.zeros((rest, D), BF16)
    grads_ref[first : first + 16, :] = gain_ref[...].astype(BF16)
    last = pl.ds(3 * ff, grads_ref.shape[0] - 3 * ff)
    last_store = pltpu.make_async_copy(grads_ref.at[last], grads_out.at[last], store_sem.at[blocks + 6])
    last_store.start()
    line.drain()
    out(0, hidden_ref, grad_hidden_out).wait()
    out(1, gn_ref, gn_out).wait()
    out(2, gd_ref, gd_out).wait()
    out(3, gnt_ref, gnt_out).wait()
    ffn_store.wait()
    grads_store.wait()
    last_store.wait()


def feed(tokens, cotangent, attn, recip, wide, gate_turned, down, gains, padded):
    length = tokens.shape[0]
    ff = down.shape[0]
    nv, rows = attn.shape[1], 32
    count = length // rows
    hbm = pl.BlockSpec(memory_space=pl.ANY)
    vmem = pl.BlockSpec(memory_space=pltpu.VMEM)
    return pl.pallas_call(
        functools.partial(feed_kernel, rows),
        out_shape=(
            jax.ShapeDtypeStruct((length, D), F32),
            jax.ShapeDtypeStruct((length, D), F32),
            jax.ShapeDtypeStruct((length, nv), BF16),
            jax.ShapeDtypeStruct((nv, length), BF16),
            jax.ShapeDtypeStruct((length, nv), BF16),
            jax.ShapeDtypeStruct((length, D), BF16),
            jax.ShapeDtypeStruct((padded, D), BF16),
        ),
        in_specs=[hbm] * 7 + [vmem],
        out_specs=(hbm,) * 7,
        scratch_shapes=[
            pltpu.VMEM((length, D), BF16), pltpu.VMEM((length, D), BF16), pltpu.VMEM((length, nv), BF16),
            pltpu.VMEM((D, nv), BF16), pltpu.VMEM((2, ff, D), BF16), pltpu.VMEM((ff, D), BF16), pltpu.VMEM((length, nv), F32),
            pltpu.VMEM((length, D), F32), pltpu.VMEM((length, 128), F32), pltpu.VMEM((length, D), BF16),
            pltpu.VMEM((ff, length), BF16), pltpu.VMEM((ff, length), BF16), pltpu.VMEM((ff, length), BF16),
            pltpu.VMEM((nv // 4, length), BF16), pltpu.VMEM((16, D), F32), pltpu.VMEM((length, D), BF16),
            pltpu.VMEM((length, nv), BF16), pltpu.VMEM((nv, length), BF16), pltpu.VMEM((length, nv), BF16),
            pltpu.VMEM((length, D), BF16), pltpu.VMEM((padded, D), BF16),
            pltpu.VMEM((length, D), BF16), pltpu.VMEM((length, D), BF16), pltpu.VMEM((length, D), BF16),
            pltpu.VMEM((length, D), BF16),
            pltpu.SemaphoreType.DMA((2,)), pltpu.SemaphoreType.DMA((2, count)),
            pltpu.SemaphoreType.DMA((10,)), pltpu.SemaphoreType.DMA((length // BT + 7,)),
        ],
        compiler_params=pltpu.CompilerParams(collective_id=2, has_side_effects=True, vmem_limit_bytes=60 * 2**20),
        name="feed",
    )(tokens, cotangent, attn, recip, wide, gate_turned, down, gains)


def back_kernel(
    pieces, small_pieces, bits, rows,
    pairs_in, values_in, gn_in, gnt_in, gd_in, mask_in, ffn_in, grads_in, normed_in, wide_in, tokens_in,
    total_out, sums_out, grad_out, small_out,
    q_ref, k_ref, v_ref, gn_ref, gnt_ref, gd_ref, mask_ref, normed_ref, wide_ref, tokens_ref,
    part, leaf, mid, total, work, landing, sums, small_work, small_landing, small_sums,
    qt_ref, gq_ref, gkt_ref, gvt_ref, gp_ref, gv_ref, grad_ref, gain_ref,
    line_send, line_recv, cube_send, cube_recv, small_send, small_recv, load_sem, store_sem,
):
    f = lax.axis_index("feat")
    line = LineSum(part, leaf, mid, total, line_send, line_recv, rows, (0, 2, 4))
    cube = CubeSum(work, landing, sums, cube_send, cube_recv, pieces, bits)
    small = CubeSum(small_work, small_landing, small_sums, small_send, small_recv, small_pieces, bits)
    half = HEADS * QK
    first_loads = [
        pltpu.make_async_copy(grads_in.at[pl.ds(a, n)], work.at[pl.ds(a, n)], load_sem.at[m]) for m, (a, n) in enumerate(pieces)
    ] + [pltpu.make_async_copy(ffn_in, part, load_sem.at[len(pieces)])]
    sources = [
        (pairs_in.at[:, pl.ds(0, half)], q_ref), (pairs_in.at[:, pl.ds(half, half)], k_ref), (values_in, v_ref),
        (mask_in, mask_ref), (gn_in, gn_ref), (gd_in, gd_ref), (gnt_in, gnt_ref), (normed_in, normed_ref),
        (wide_in.at[:, pl.ds(0, wide_ref.shape[1])], wide_ref), (tokens_in, tokens_ref),
    ]
    loads = [pltpu.make_async_copy(a, b, load_sem.at[len(pieces) + 1 + n]) for n, (a, b) in enumerate(sources)]
    for load in first_loads:
        load.start()
    greet(line, cube)
    for p in range(len(pieces)):
        first_loads[p].wait()
        cube.launch(p)
    for load in loads[:7]:
        load.start()
    first_loads[-1].wait()
    each(line.leaves, line.count)
    gq_ref[...] = jnp.zeros_like(gq_ref)
    for load in loads[:7]:
        load.wait()
    for load in loads[7:]:
        load.start()
    qt_ref[...] = q_ref[...].T

    lane = lax.broadcasted_iota(jnp.int32, (1, 128), 1)
    length = q_ref.shape[0]
    blocks = length // BT
    hb = 2
    groups = HEADS // hb
    weaver = Weaver(2.0)
    weaver.add("line", line_floors(line, 0.5), [0.0] * line.steps())
    floors, times = cube_floors(cube, 0.0)
    for p in range(len(pieces)):
        weaver.add(("cube", p), floors[p], times[p])

    def take(items):
        for name, n in items:
            if name == "line":
                line.serve(jnp.int32(n))
            elif name[0] == "cube":
                cube.advance(name[1], n)
            else:
                small.advance(name[1], n)

    for block in range(blocks):
        lo = block * BT
        below, there = pl.ds(lo, length - lo), pl.ds(lo, BT)
        plans = [weaver.unit(0.43 * (blocks - block) + 0.1) for _ in range(groups)]

        def group(g, carry):
            h = g * hb
            ql = pl.ds(pl.multiple_of(h // 8 * 128, 128), 128)
            vl = pl.ds(pl.multiple_of(g * 128, 128), 128)
            q, k, v = q_ref[below, ql], k_ref[there, ql], v_ref[there, vl]
            both = jnp.concatenate([gn_ref[below, vl], gd_ref[below, vl]], axis=1)
            mask = mask_ref[block, : length - lo, :]
            gq, turned = None, []
            for a in range(hb):
                km = jnp.where(lane // QK == lax.rem(h + a, 8), k, jnp.zeros_like(k))
                vm = jnp.where(lane // HV == a, v, jnp.zeros_like(v))
                pick = jnp.where(lane == HV * a, jnp.ones_like(v), jnp.zeros_like(v))
                t1 = nt(q, km) + 1.0
                p = (t1 * t1 + 1.0).astype(BF16) * mask
                dp = nt(both, jnp.concatenate([vm, pick], axis=1)).astype(BF16) * mask
                gs = (dp.astype(F32) * t1).astype(BF16)
                out = nn(gs, km)
                gq = out if gq is None else gq + out
                qrows = pl.ds(pl.multiple_of((h + a) * QK, QK), QK)
                vrows = pl.ds(pl.multiple_of((h + a) * HV, HV), HV)
                gkt_ref[qrows, there] = nn(qt_ref[qrows, below], gs)
                turned.append(nn(gnt_ref[vrows, below], p) * 0.5)
            gq_ref[below, ql] += gq
            gvt = jnp.concatenate(turned, axis=0)
            gvt_ref[vl, there] = gvt.astype(BF16)
            gv_ref[there, vl] = gvt.T.astype(BF16)
            for n, plan in enumerate(plans):
                if plan:
                    @pl.when(g == n)
                    def _():
                        take(plan)
            return carry

        lax.fori_loop(0, groups, group, 0)
    gp_ref[:, :half] = (gq_ref[...] * 0.25).astype(BF16)
    gp_ref[:, half:] = gkt_ref[...].T.astype(BF16)
    for load in loads[7:]:
        load.wait()

    pair_cols, value_cols = 2 * half // 4, HEADS * HV // 4
    rest = value_cols + pair_cols

    def open_small(p):
        small.launch(p)
        floors, times = cube_floors(small, 0.0, 1.8)
        weaver.add(("small", p), [0.0] * len(floors[p]), times[p])

    small_work[0:value_cols, :] = nn(
        gvt_ref[pl.ds(pl.multiple_of(f * value_cols, value_cols), value_cols), :], normed_ref[...]
    ).astype(BF16)
    small_work[value_cols:rest, :] = nn(own_column(gp_ref, f, pair_cols).T, normed_ref[...]).astype(BF16)
    if len(small_pieces) > 1:
        open_small(0)
    take(weaver.unit(3.6))
    gain_ref[...] = jnp.zeros_like(gain_ref)
    for n in range(blocks):
        at = slice(n * BT, (n + 1) * BT)
        grad = nt(gp_ref[at, :], wide_ref[:, : 2 * half]) + nt(gv_ref[at, :], wide_ref[:, 2 * half :])
        grad_ref[at, :] = grad.astype(BF16)
        x = tokens_ref[at, :].astype(F32)
        scale = lax.rsqrt(jnp.mean(x * x, axis=1, keepdims=True) + EPS)
        gain_ref[0:1, :] += jnp.sum(grad * (x * scale), axis=0, keepdims=True)
        if n < blocks - 1:
            take(weaver.unit(1.4))
    grad_store = pltpu.make_async_copy(grad_ref, grad_out, store_sem.at[0])
    grad_store.start()
    small_work[rest:, :] = jnp.zeros((small_work.shape[0] - rest, D), BF16)
    small_work[rest : rest + 16, :] = gain_ref[...].astype(BF16)
    open_small(len(small_pieces) - 1)
    take(weaver.unit(1.6))
    take(weaver.until([("cube", p) for p in range(len(pieces))]))
    sums_store = pltpu.make_async_copy(sums, sums_out, store_sem.at[2])
    sums_store.start()
    take(weaver.until([("small", p) for p in range(len(small_pieces))]))
    small_store = pltpu.make_async_copy(small_sums, small_out, store_sem.at[1])
    small_store.start()
    take(weaver.until(["line"]))
    each(line.arrived, line.count)
    total_store = pltpu.make_async_copy(total, total_out, store_sem.at[3])
    total_store.start()
    line.drain()
    cube.drain()
    small.drain()
    for s in (sums_store, grad_store, small_store, total_store):
        s.wait()


def back(pairs, values, gn, gnt, gd, mask, ffn, grads, normed, wide, tokens, pieces, bits, dp_size):
    length = tokens.shape[0]
    nq, nv, rows = HEADS * QK, HEADS * HV, 64
    count = length // rows
    unit = 16 * dp_size
    first = (nv // 4 + nq // 2) // unit * unit
    small_pieces = [(0, first), (first, unit)] if first else []
    small_rows = first + unit
    need = nv // 4 + nq // 2 + 16
    if small_rows < need or not small_pieces:
        small_rows = (need + unit - 1) // unit * unit
        small_pieces = [(0, small_rows)]
    hbm = pl.BlockSpec(memory_space=pl.ANY)

    def buf(*shape, dtype=BF16):
        return pltpu.VMEM(shape, dtype)

    sems = []
    for p in (pieces, small_pieces):
        sems += [pltpu.SemaphoreType.DMA((2,)), pltpu.SemaphoreType.DMA((len(p), 2, 2 * len(bits)))]
    return pl.pallas_call(
        functools.partial(back_kernel, pieces, small_pieces, bits, rows),
        out_shape=(
            jax.ShapeDtypeStruct((length, D), BF16),
            jax.ShapeDtypeStruct(grads.shape, BF16),
            jax.ShapeDtypeStruct((length, D), BF16),
            jax.ShapeDtypeStruct((small_rows, D), BF16),
        ),
        in_specs=[hbm] * 11,
        out_specs=(hbm,) * 4,
        scratch_shapes=[
            buf(length, nq), buf(length, nq), buf(length, nv), buf(length, nv), buf(nv, length), buf(length, nv),
            buf(*mask.shape), buf(length, D), buf(D, 2 * nq + nv), buf(length, D),
            buf(length, D), buf(length, D), buf(length, D), buf(length, D),
            buf(*grads.shape), buf(*grads.shape), buf(*grads.shape),
            buf(small_rows, D), buf(small_rows, D), buf(small_rows, D),
            buf(nq, length), buf(length, nq, dtype=F32), buf(nq, length, dtype=F32), buf(nv, length), buf(length, 2 * nq), buf(length, nv),
            buf(length, D), buf(16, D, dtype=F32),
            pltpu.SemaphoreType.DMA((2,)), pltpu.SemaphoreType.DMA((2, count)), *sems,
            pltpu.SemaphoreType.DMA((len(pieces) + 11,)), pltpu.SemaphoreType.DMA((4,)),
        ],
        compiler_params=pltpu.CompilerParams(collective_id=4, has_side_effects=True, vmem_limit_bytes=62 * 2**20),
        name="back",
    )(pairs, values, gn, gnt, gd, mask, ffn, grads, normed, wide, tokens)


def update_kernel(
    rates,
    down_w, down_m, down_a, gate_w, gate_m, gate_a, out_w, out_m, out_a, value_w, value_m, value_a,
    pair_w, pair_m, pair_a, gain_w, gain_m, gain_a, big, small, hidden, total, grad_hidden, grad_normed, tokens, gains,
    mixed_o, input_o, pair_mo, pair_wo, pair_ao, value_mo, value_wo, value_ao, out_mo, out_wo, out_ao,
    gate_mo, gate_wo, gate_ao, down_mo, down_wo, down_ao, gain_mo, gain_wo, gain_ao,
):
    ff = down_w.shape[0]
    narrow = value_w.shape[1]
    pair_cols = pair_w.shape[1]

    def put(index, outs, grad, w, m, a, rate):
        moment_next, weight_next, average_next = update(w[index], grad, m[index], a[index], rate)
        outs[0][index], outs[1][index], outs[2][index] = moment_next, weight_next, average_next

    put(..., (down_mo, down_wo, down_ao), big[:ff, :].astype(F32), down_w, down_m, down_a, rates[4])
    for n in range(2):
        first = (n + 1) * ff
        put(n, (gate_mo, gate_wo, gate_ao), big[first : first + ff, :].astype(F32), gate_w, gate_m, gate_a, rates[3])
    first = 3 * ff
    put(..., (out_mo, out_wo, out_ao), big[first : first + out_w.shape[0], :].astype(F32), out_w, out_m, out_a, rates[2])
    first = first + out_w.shape[0]
    put(..., (value_mo, value_wo, value_ao), small[:narrow, :].astype(F32).T, value_w, value_m, value_a, rates[1])
    put(..., (pair_mo, pair_wo, pair_ao), small[narrow : narrow + pair_cols, :].astype(F32).T, pair_w, pair_m, pair_a, rates[0])
    gain_one = small[narrow + pair_cols : narrow + pair_cols + 16, :].astype(F32)[0:1, :]
    gain_two = big[first : first + 16, :].astype(F32)[0:1, :]
    put(slice(0, 1), (gain_mo, gain_wo, gain_ao), gain_one, gain_w, gain_m, gain_a, rates[5])
    put(slice(1, 2), (gain_mo, gain_wo, gain_ao), gain_two, gain_w, gain_m, gain_a, rates[5])

    mixed_o[...] = (hidden[...] + total[...].astype(F32)).astype(BF16)
    x = tokens[...].astype(F32)
    scale = lax.rsqrt(jnp.mean(x * x, axis=1, keepdims=True) + EPS)
    unit = x * scale
    u = grad_normed[...].astype(F32) * gains[0:1, :]
    input_o[...] = grad_hidden[...] + scale * (u - unit * jnp.mean(u * unit, axis=1, keepdims=True))


def finish(rates, weights, big, small, hidden, total, grad_hidden, grad_normed, tokens, gains):
    length = tokens.shape[0]
    steps = D // 128
    rows = length // steps
    ff = weights[0][0].shape[0]
    narrow, pair_cols = weights[3][0].shape[1], weights[4][0].shape[1]

    def cols(n):
        return pl.BlockSpec((n, 128), lambda i: (0, i))

    def tall(n):
        return pl.BlockSpec((128, n), lambda i: (i, 0))

    token = pl.BlockSpec((rows, D), lambda i: (i, 0))
    specs = [cols(ff), pl.BlockSpec((2, ff, 128), lambda i: (0, 0, i)), cols(weights[2][0].shape[0]), tall(narrow), tall(pair_cols), cols(2)]
    order = [4, 3, 2, 1, 0, 5]
    flat = [a for group in weights for a in group]
    out_shape = [jax.ShapeDtypeStruct((length, D), BF16), jax.ShapeDtypeStruct((length, D), F32)]
    out_specs = [token, token]
    for n in order:
        out_shape += [jax.ShapeDtypeStruct(weights[n][0].shape, F32)] * 3
        out_specs += [specs[n]] * 3
    in_specs = [specs[n] for n in range(6) for _ in range(3)]
    in_specs += [cols(big.shape[0]), cols(small.shape[0])] + [token] * 5 + [pl.BlockSpec((2, D), lambda i: (0, 0))]
    return pl.pallas_call(
        functools.partial(update_kernel, rates),
        grid=(steps,),
        out_shape=out_shape,
        in_specs=in_specs,
        out_specs=out_specs,
        compiler_params=pltpu.CompilerParams(vmem_limit_bytes=62 * 2**20),
        name="finish",
    )(*flat, big, small, hidden, total, grad_hidden, grad_normed, tokens, gains)


def update(weight, grad_total, moment, average, rate):
    moment_next = MOMENTUM * moment + grad_total
    weight_next = weight - rate * (grad_total + MOMENTUM * moment_next)
    average_next = average + (weight_next - average) / STEP
    return (moment_next, weight_next, average_next)


def on_device(
    tokens,
    cotangent,
    doc_starts,
    queries_keys,
    value_weight,
    out_weight,
    gate_up,
    down_weight,
    norm_gains,
    queries_moment,
    value_moment,
    out_moment,
    gate_moment,
    down_moment,
    gains_moment,
    queries_average,
    value_average,
    out_average,
    gate_average,
    down_average,
    gains_average,
):
    total_tokens = float(tokens.shape[0] * lax.axis_size("dp"))
    dp_size = lax.axis_size("dp")
    ff = down_weight.shape[0]
    gate_turned = gate_up.transpose(0, 2, 1)
    normed_one, pairs, values, wide, gate_low, down_low, attn_low, recip, mask = front(
        doc_starts, tokens, norm_gains, queries_keys, value_weight, out_weight, gate_turned, down_weight
    )
    padded, pieces, bits = cube_shape(3 * ff + out_weight.shape[0] + 16, dp_size, 4)
    hidden_one, grad_hidden, grad_numer, grad_numer_turned, grad_denom, ffn_part, big = feed(
        tokens, cotangent, attn_low, recip, wide, gate_low, down_low, norm_gains, padded
    )
    total, big, grad_normed_one, small = back(
        pairs, values, grad_numer, grad_numer_turned, grad_denom, mask, ffn_part, big, normed_one, wide, tokens,
        pieces, bits, dp_size,
    )
    rates = (
        (D * total_tokens) ** (-0.5),
        (D * total_tokens) ** (-0.5),
        (HEADS * HV * total_tokens) ** (-0.5),
        (D * total_tokens) ** (-0.5),
        (FF * total_tokens) ** (-0.5),
        0.2 * total_tokens ** (-0.5),
    )
    weights = (
        (down_weight, down_moment, down_average),
        (gate_turned, gate_moment.transpose(0, 2, 1), gate_average.transpose(0, 2, 1)),
        (out_weight, out_moment, out_average),
        (value_weight, value_moment, value_average),
        (queries_keys, queries_moment, queries_average),
        (norm_gains, gains_moment, gains_average),
    )
    outs = list(finish(rates, weights, big, small, hidden_one, total, grad_hidden, grad_normed_one, tokens, norm_gains))
    outs[11:14] = [o.transpose(0, 2, 1) for o in outs[11:14]]
    return tuple(outs)


def solution(mesh):
    in_specs = (
        P("dp", None),
        P("dp", None),
        P("dp", None),
        P(None, "feat"),
        P(None, "feat"),
        P("feat", None),
        P(None, None, "feat"),
        P("feat", None),
        P(),
        P(None, "feat"),
        P(None, "feat"),
        P("feat", None),
        P(None, None, "feat"),
        P("feat", None),
        P(),
        P(None, "feat"),
        P(None, "feat"),
        P("feat", None),
        P(None, None, "feat"),
        P("feat", None),
        P(),
    )
    out_specs = (
        P("dp", None),
        P("dp", None),
        P(None, "feat"),
        P(None, "feat"),
        P(None, "feat"),
        P(None, "feat"),
        P(None, "feat"),
        P(None, "feat"),
        P("feat", None),
        P("feat", None),
        P("feat", None),
        P(None, None, "feat"),
        P(None, None, "feat"),
        P(None, None, "feat"),
        P("feat", None),
        P("feat", None),
        P("feat", None),
        P(),
        P(),
        P(),
    )
    return jax.shard_map(
        on_device, mesh=mesh, in_specs=in_specs, out_specs=out_specs, check_vma=False
    )
```
